32 devices in a mesh: ctx: 8 (over z, y), fsdp: 4 (over x, core).
Axes of the slice: x: 2, y: 2, z: 4, core: 2. Of those that a mesh axis runs over, the one named last changes fastest.
Arguments:
- inputs: float32 [12288, 768], P(('ctx', 'fsdp')), may hold values from -6 to 6
- out_grad: float32 [12288, 768], P(('ctx', 'fsdp')), may hold values from -6 to 6
- vectors: float32 [4, 768], replicated
- block_order: int32 [4, 32], P('fsdp'), may hold values from 0 to 31, as said below
- seq_lengths: int32 [4, 4], P('fsdp'), may hold values from 1 to 1536, 3072 in all within a row
- expert_ids: int32 [12288, 2], P(('ctx', 'fsdp')), may hold values from 0 to 11, all different within a row; in each aligned block of 384 rows (0 to 383, 384 to 767, ...) at most 96 rows name the same one
- attn_weights: bfloat16 [144, 128, 128], P('fsdp')
- attn_left: float32 [144, 128, 128], P('fsdp'), as said below
- attn_right: float32 [144, 128, 128], P('fsdp'), as said below
- attn_left_root: float32 [144, 128, 128], P('fsdp'), as said below
- attn_right_root: float32 [144, 128, 128], P('fsdp'), as said below
- expert_weights: bfloat16 [8, 288, 128, 128], P('fsdp', 'ctx')
- expert_left: float32 [8, 288, 128, 128], P('fsdp', 'ctx'), as said below
- expert_right: float32 [8, 288, 128, 128], P('fsdp', 'ctx'), as said below
- expert_left_root: float32 [8, 288, 128, 128], P('fsdp', 'ctx'), as said below
- expert_right_root: float32 [8, 288, 128, 128], P('fsdp', 'ctx'), as said below
- router_weights: bfloat16 [768, 12], replicated, may hold values from -0.15625 to 0.15625
- router_left: float32 [6, 128, 128], replicated, as said below
- router_right: float32 [6, 12, 12], replicated, as said below
- router_left_root: float32 [6, 128, 128], replicated, as said below
- router_right_root: float32 [6, 12, 12], replicated, as said below
Outputs:
- output: float32 [12288, 768], P(('ctx', 'fsdp'))
- input_grad: float32 [12288, 768], P(('ctx', 'fsdp'))
- vector_grads: float32 [4, 768], replicated
- vector_new: float32 [4, 768], replicated
- attn_grads: float32 [144, 128, 128], P('fsdp')
- attn_left_new: float32 [144, 128, 128], P('fsdp')
- attn_right_new: float32 [144, 128, 128], P('fsdp')
- attn_new: float32 [144, 128, 128], P('fsdp')
- expert_grads: float32 [8, 288, 128, 128], P('fsdp', 'ctx')
- expert_left_new: float32 [8, 288, 128, 128], P('fsdp', 'ctx')
- expert_right_new: float32 [8, 288, 128, 128], P('fsdp', 'ctx')
- expert_new: float32 [8, 288, 128, 128], P('fsdp', 'ctx')
- router_grads: float32 [768, 12], replicated
- router_left_new: float32 [6, 128, 128], replicated
- router_right_new: float32 [6, 12, 12], replicated
- router_new: float32 [768, 12], replicated
The draws below stay inside these ranges and needn't reach their ends.
Inputs may be any that keep to these rules, and one draw needn't show every extreme that they name: On device c of ctx in group g, rows k * 96 to (k + 1) * 96 - 1 hold the places from block_order[g, c * 4 + k] * 96 on, in order; each row of block_order is a permutation of 0 to 31 whose entry c * 4 + k lies between k * 8 and (k + 1) * 8 - 1. `seq_lengths`: row g sums to 3072; its largest entry is 1536. `expert_ids`: A token's two ids differ. Ids below 8 are feed-forward experts, 8 the zero expert, 9 the copy expert, higher ones constant experts. Among the rows of one device no id appears more than 96 times, and some id reaches 96. `attn_left`: symmetric. `attn_right`: symmetric. `attn_left_root`: symmetric. `attn_right_root`: symmetric. `expert_left`: symmetric. `expert_right`: symmetric. `expert_left_root`: symmetric. `expert_right_root`: symmetric. `router_left`: symmetric. `router_right`: symmetric. `router_left_root`: symmetric. `router_right_root`: symmetric.
All inputs are finite; a program needn't handle non-finite values.
Results may differ from the reference program's by a relative error of at most 0.01.
The reference program's roundings to bfloat16 on the way count: a program that leaves them out, or rounds other values in their place, can miss the bound.
Values may be sent and summed in bfloat16 or wider, within the bound.
No kernel may reach another device: no remote copies, remote signals or barrier semaphores. Data moves between devices by JAX's collectives and lax.ppermute only.
A program may use at most 256 MiB of HBM per device.

```python
import math
import jax
import jax.numpy as jnp
import numpy as np
from jax import lax

D = 768
HEADS = 12
HDIM = 64
FF = 2048
EXPERTS = 8
ZEROS = 4
BS = 128
SLOTS = 4
NSEQ = 4
TOK_DEV = 384
GROUPS = 4
GROUP = 3072
TOKENS = 12288
NBLK = 32
PBLK = 96
LONGEST = 1536
MOST = 96
SPLIT = 1
SLICE = 2048
NSLICE = 8
NROUTE = 12
ATT_BLOCKS = 144
SLICE_BLOCKS = 288
ROUTER_BLOCKS = 6
N_CTX = 8
N_FSDP = 4


def scaled_normal(key, number, scales):
    values = jnp.clip(jax.random.normal(key, (number, BS, BS), jnp.float32), -4.0, 4.0)
    return values * scales[:, None, None]


def level_split(number, boundary, before, after):
    return jnp.where(jnp.arange(number) < boundary, before, after).astype(jnp.float32)


def diagonal_stats(key, levels, breadth, size_now):
    number = levels.shape[0]
    base_level = breadth * levels * levels
    spread = jnp.exp(jax.random.uniform(key, (number, size_now), jnp.float32, 0.0, math.log(4.0)))
    return (base_level[:, None] * spread)[:, :, None] * jnp.eye(size_now, dtype=jnp.float32)[None]


def root_matrices(key, levels, breadth, size_now):
    number = levels.shape[0]
    scale_now = (breadth * levels * levels) ** (-0.25)
    first_key, second_key = jax.random.split(key)
    diagonal = jnp.exp(jax.random.uniform(first_key, (number, size_now), jnp.float32, 0.0, math.log(2.0)))
    spread = jax.random.uniform(second_key, (number, size_now, size_now), jnp.float32, -1.0, 1.0) * (0.9 / math.sqrt(size_now))
    spread = 0.5 * (spread + jnp.swapaxes(spread, 1, 2))
    identity = jnp.eye(size_now, dtype=jnp.float32)[None]
    return scale_now[:, None, None] * (spread * (1.0 - identity) + diagonal[:, :, None] * identity)


def attn_levels():
    per_side = D // BS
    return level_split(ATT_BLOCKS, 3 * per_side * per_side, 0.5 * math.sqrt(TOKENS), 0.1 * math.sqrt(TOKENS))


def expert_levels():
    within = jnp.arange(NSLICE * SLICE_BLOCKS) % SLICE_BLOCKS
    routed = math.sqrt(TOKENS / 6.0)
    return jnp.where(within < 2 * (SLICE_BLOCKS // 3), 0.15 * routed, 0.25 * routed).astype(jnp.float32)


def router_levels():
    return jnp.full((ROUTER_BLOCKS,), 3.0 * math.sqrt(TOKENS), jnp.float32)


def expert_shape(values):
    return values.reshape(NSLICE, SLICE_BLOCKS, BS, BS)


def draw_vectors(key, part):
    key = jax.random.fold_in(key, 1)
    first_key, second_key = jax.random.split(key)
    norm_gains = 1.0 + 0.1 * jax.random.uniform(first_key, (2, D), jnp.float32, -3.0, 3.0)
    constants = jnp.clip(jax.random.normal(second_key, (2, D), jnp.float32), -4.0, 4.0)
    return jnp.concatenate([norm_gains, constants], axis=0)


def draw_block_order(key, part):
    key = jax.random.fold_in(key, 2)
    quarter = NBLK // SLOTS
    keys_all = jax.random.split(key, GROUPS * SLOTS)
    orders = jax.vmap(lambda single: jax.random.permutation(single, quarter))(keys_all).reshape(GROUPS, SLOTS, quarter)
    orders = orders + (jnp.arange(SLOTS, dtype=jnp.int32) * quarter)[None, :, None]
    return jnp.swapaxes(orders, 1, 2).reshape(GROUPS, NBLK).astype(jnp.int32)


def draw_attn_weights(key, part):
    key = jax.random.fold_in(key, 3)
    per_side = D // BS
    scales = level_split(ATT_BLOCKS, 3 * per_side * per_side, D ** (-0.5), 8.0 * D ** (-0.5))
    return scaled_normal(key, ATT_BLOCKS, scales).astype(jnp.bfloat16)


def draw_attn_left(key, part):
    key = jax.random.fold_in(key, 4)
    return diagonal_stats(key, attn_levels(), BS, BS)


def draw_attn_right(key, part):
    key = jax.random.fold_in(key, 5)
    return diagonal_stats(key, attn_levels(), BS, BS)


def draw_attn_left_root(key, part):
    key = jax.random.fold_in(key, 6)
    return root_matrices(key, attn_levels(), BS, BS)


def draw_attn_right_root(key, part):
    key = jax.random.fold_in(key, 7)
    return root_matrices(key, attn_levels(), BS, BS)


def draw_expert_weights(key, part):
    key = jax.random.fold_in(key, 8)
    within = jnp.arange(NSLICE * SLICE_BLOCKS) % SLICE_BLOCKS
    scales = jnp.where(within < 2 * (SLICE_BLOCKS // 3), D ** (-0.5), FF ** (-0.5)).astype(jnp.float32)
    return expert_shape(scaled_normal(key, NSLICE * SLICE_BLOCKS, scales)).astype(jnp.bfloat16)


def draw_expert_left(key, part):
    key = jax.random.fold_in(key, 9)
    return expert_shape(diagonal_stats(key, expert_levels(), BS, BS))


def draw_expert_right(key, part):
    key = jax.random.fold_in(key, 10)
    return expert_shape(diagonal_stats(key, expert_levels(), BS, BS))


def draw_expert_left_root(key, part):
    key = jax.random.fold_in(key, 11)
    return expert_shape(root_matrices(key, expert_levels(), BS, BS))


def draw_expert_right_root(key, part):
    key = jax.random.fold_in(key, 12)
    return expert_shape(root_matrices(key, expert_levels(), BS, BS))


def draw_router_left(key, part):
    key = jax.random.fold_in(key, 13)
    return diagonal_stats(key, router_levels(), NROUTE, BS)


def draw_router_right(key, part):
    key = jax.random.fold_in(key, 14)
    return diagonal_stats(key, router_levels(), BS, NROUTE)


def draw_router_left_root(key, part):
    key = jax.random.fold_in(key, 15)
    return root_matrices(key, router_levels(), NROUTE, BS)


def draw_router_right_root(key, part):
    key = jax.random.fold_in(key, 16)
    return root_matrices(key, router_levels(), BS, NROUTE)


def steps_of(own_key, extent, pieces, low, high):
    level = 1.0
    for axis_at, shards_of in pieces:
        heights = jax.random.uniform(jax.random.fold_in(jax.random.fold_in(own_key, 6), axis_at), (shards_of,), jnp.float32, low / len(pieces), high / len(pieces))
        level = level * jnp.repeat(jnp.exp(heights), extent[axis_at] // shards_of).reshape((-1,) + (1,) * (len(extent) - 1 - axis_at))
    return level


def length_profile(count, total, bound, skew):
    portions = [(1 << 20) // math.isqrt(grade ** skew) + 1 for grade in range(2, count + 1)]
    spare, counts = total - bound - (count - 1), [1] * (count - 1)
    while spare > 0:
        movable = [i for i in range(count - 1) if counts[i] < bound]
        whole, budget = sum([portions[i] for i in movable]), spare
        for i in movable:
            extra = min(bound - counts[i], max(1, budget * portions[i] // whole), spare)
            counts[i] = counts[i] + extra
            spare = spare - extra
    return np.array([bound] + counts)


def uneven_parts(stream_key, count, total, limit, lean):
    if count == 2:
        one = jax.random.randint(stream_key, (), max(1, total - limit), min(limit, total - 1) + 1)
        return jnp.stack([one, total - one])
    lengths = jnp.asarray(length_profile(count, total, limit, lean), jnp.int32)
    couples = (count - 1) // 2
    giver, receiver = lengths[1:1 + 2 * couples:2], lengths[2:2 + 2 * couples:2]
    margin = jnp.minimum(giver - 1, limit - receiver)
    moved = jax.random.randint(jax.random.fold_in(stream_key, 1), (couples,), 0, 1 << 20) % (margin + 1)
    lengths = lengths.at[1:1 + 2 * couples:2].set(giver - moved).at[2:2 + 2 * couples:2].set(receiver + moved)
    return lengths[jax.random.permutation(jax.random.fold_in(stream_key, 2), count)]


def deal_out(own_key, own, number, rows, count, top, reach, skew):
    ranking = jax.random.permutation(own_key, count)
    crowded, common = portions_of(count, rows * top, reach, skew, True), portions_of(count, rows * top, reach, skew, False)
    places = jnp.arange(count)

    def named(lengths, turn):
        used = int((lengths > 0).sum())
        fixed = max(1, used // 4)
        passed = fixed + (places - fixed + turn * (used - fixed)) % max(1, count - fixed)
        return jnp.zeros((count,), jnp.int32).at[ranking[jnp.where(places < fixed, places, passed)]].set(jnp.asarray(lengths, jnp.int32))

    lengths = jnp.where(number % 4 == 0, named(crowded, number // 4), named(common, number - number // 4 - 1))
    mixed = jax.random.permutation(jax.random.fold_in(own, 3), count)
    source_of, sink = mixed[0:count // 2 * 2:2], mixed[1:count // 2 * 2:2]
    slack = jnp.minimum(lengths[source_of] - 1, reach - lengths[sink]) // 2
    slack = jnp.where((source_of == ranking[0]) | (sink == ranking[0]) | (lengths[sink] == 0), 0, jnp.maximum(slack, 0))
    passed = jax.random.randint(jax.random.fold_in(own, 4), (count // 2,), 0, 1 << 20) % (slack + 1)
    lengths = lengths.at[source_of].add(-passed).at[sink].add(passed)
    items = jnp.searchsorted(jnp.cumsum(lengths), jnp.arange(rows * top), side="right").astype(jnp.int32)
    listing = items.reshape(top, rows).T
    listing = listing[jax.random.permutation(jax.random.fold_in(own, 1), rows)]
    turn = jax.random.randint(jax.random.fold_in(own, 2), (rows, 1), 0, top)
    return jnp.take_along_axis(listing, (jnp.arange(top)[None, :] + turn) % top, axis=1)


def portions_of(count, total, bound, lean, full):
    weights = [(1 << 20) // math.isqrt(standing ** lean) + 1 for standing in range(1, count + 1)]
    largest = bound if full else min(bound, max(-(-total // count), total * weights[0] // sum(weights)))
    least = 1 if total - largest >= count - 1 else 0
    counts, surplus = [largest] + [least] * (count - 1), total - largest - least * (count - 1)
    while surplus > 0:
        movable = [i for i in range(1, count) if counts[i] < largest] or [i for i in range(1, count) if counts[i] < bound]
        mass, budget = sum([weights[i] for i in movable]), surplus
        for i in movable:
            extra = min(bound - counts[i], max(1, budget * weights[i] // mass), surplus)
            counts[i] = counts[i] + extra
            surplus = surplus - extra
    return np.array(counts)


def noise(stream_key, extent, scale, reach, cuts=(), held_as=jnp.bfloat16):
    values = scale * jax.random.normal(stream_key, extent, jnp.float32)
    if cuts:
        values = values * steps_of(stream_key, extent, cuts, -0.22, 0.18)
    return jnp.clip(values, -reach, reach).astype(held_as)


def setup_inputs(seed: int = 0) -> dict:
    seeds = jax.random.split(jax.random.key(seed), 22)
    inputs = noise(seeds[0], (TOKENS, D), 1.0, 6.0, ((0, 32),), jnp.float32)
    out_grad = noise(seeds[1], (TOKENS, D), 1.0, 6.0, ((0, 32),), jnp.float32)
    vectors = draw_vectors(jax.random.fold_in(seeds[21], 71), 0)
    block_order = draw_block_order(jax.random.fold_in(seeds[21], 71), 0)
    seq_lengths = jax.vmap(lambda own: uneven_parts(own, NSEQ, GROUP, LONGEST, 2))(jax.random.split(seeds[4], GROUPS)).reshape((GROUPS, NSEQ)).astype(jnp.int32)
    expert_ids_keys = jax.random.split(jax.random.fold_in(seeds[5], 1), TOKENS // TOK_DEV)
    expert_ids_turns = jax.random.permutation(jax.random.fold_in(seeds[5], 3), TOKENS // TOK_DEV)
    expert_ids = jax.vmap(lambda own, number: deal_out(jax.random.fold_in(seeds[5], 2), own, number, TOK_DEV, NROUTE, 2, MOST, 1))(expert_ids_keys, expert_ids_turns).reshape((TOKENS, 2))
    attn_weights = draw_attn_weights(jax.random.fold_in(seeds[21], 71), 0)
    attn_left = draw_attn_left(jax.random.fold_in(seeds[21], 71), 0)
    attn_right = draw_attn_right(jax.random.fold_in(seeds[21], 71), 0)
    attn_left_root = draw_attn_left_root(jax.random.fold_in(seeds[21], 71), 0)
    attn_right_root = draw_attn_right_root(jax.random.fold_in(seeds[21], 71), 0)
    expert_weights = draw_expert_weights(jax.random.fold_in(seeds[21], 71), 0)
    expert_left = draw_expert_left(jax.random.fold_in(seeds[21], 71), 0)
    expert_right = draw_expert_right(jax.random.fold_in(seeds[21], 71), 0)
    expert_left_root = draw_expert_left_root(jax.random.fold_in(seeds[21], 71), 0)
    expert_right_root = draw_expert_right_root(jax.random.fold_in(seeds[21], 71), 0)
    router_weights = noise(seeds[16], (D, NROUTE), (D * 16 // 9) ** -0.5, 0.15625)
    router_left = draw_router_left(jax.random.fold_in(seeds[21], 71), 0)
    router_right = draw_router_right(jax.random.fold_in(seeds[21], 71), 0)
    router_left_root = draw_router_left_root(jax.random.fold_in(seeds[21], 71), 0)
    router_right_root = draw_router_right_root(jax.random.fold_in(seeds[21], 71), 0)
    return {"inputs": inputs, "out_grad": out_grad, "vectors": vectors, "block_order": block_order, "seq_lengths": seq_lengths, "expert_ids": expert_ids, "attn_weights": attn_weights, "attn_left": attn_left, "attn_right": attn_right, "attn_left_root": attn_left_root, "attn_right_root": attn_right_root, "expert_weights": expert_weights, "expert_left": expert_left, "expert_right": expert_right, "expert_left_root": expert_left_root, "expert_right_root": expert_right_root, "router_weights": router_weights, "router_left": router_left, "router_right": router_right, "router_left_root": router_left_root, "router_right_root": router_right_root}


EPSILON = 1e-06
SCORE_SCALE = 0.125
STAT_DECAY = 0.5
RATE_PROJECT = 0.4
RATE_OUTPUT = 3.0
RATE_EXPERT = 0.4
RATE_ROUTER = 0.2
RATE_VECTOR = 0.1
MASKED_SCORE = -1e+30
PRECISE = lax.Precision.HIGHEST

@jax.custom_vjp
def low(v):
    return lax.optimization_barrier(v.astype(jnp.bfloat16)).astype(jnp.float32)

@jax.custom_vjp
def low_back(v):
    return v

def low_keep(v):
    return (low(v), None)

def low_pass(kept, grad):
    return (grad,)

def back_keep(v):
    return (v, None)

def back_low(kept, grad):
    return (low(grad),)
low.defvjp(low_keep, low_pass)
low_back.defvjp(back_keep, back_low)

def to_matrix(blocks, height, breadth):
    block_height = blocks.shape[1]
    block_breadth = blocks.shape[2]
    shaped = blocks.reshape(height // block_height, breadth // block_breadth, block_height, block_breadth)
    return shaped.transpose(0, 2, 1, 3).reshape(height, breadth)

def to_blocks(matrix, block_height, block_breadth):
    height = matrix.shape[0]
    breadth = matrix.shape[1]
    shaped = matrix.reshape(height // block_height, block_height, breadth // block_breadth, block_breadth)
    return shaped.transpose(0, 2, 1, 3).reshape(-1, block_height, block_breadth)

def normalize(values, scaling):
    return values * lax.rsqrt(lax.optimization_barrier(jnp.mean(values * values, axis=-1, keepdims=True)) + EPSILON) * scaling

def positions_of(block_order, seq_lengths):
    offsets = jnp.arange(PBLK, dtype=jnp.int32)
    places = (block_order[:, :, None] * PBLK + offsets[None, None, :]).reshape(GROUPS, GROUP)
    sequence_ends = jnp.cumsum(seq_lengths, axis=1).astype(jnp.int32)
    documents = lax.optimization_barrier(jnp.sum((places[:, :, None] >= sequence_ends[:, None, :]).astype(jnp.int32), axis=2))
    return (places, documents)

def attend(queries, key_rows, value_rows, places, documents):

    def one_group(members):
        group_query, group_key, group_value, group_place, group_document = members

        def one_block(block):
            block_query, block_place, block_document = block
            scores = jnp.einsum('qhd,khd->hqk', block_query, group_key, precision=PRECISE) * SCORE_SCALE
            scores = low_back(scores)
            allowed = (block_document[:, None] == group_document[None, :]) & (group_place[None, :] <= block_place[:, None])
            scores = jnp.where(allowed[None], scores, MASKED_SCORE)
            row_peak = lax.optimization_barrier(jnp.max(scores, axis=-1, keepdims=True))
            weights = jnp.exp(scores - row_peak)
            weights = low(weights / lax.optimization_barrier(jnp.sum(weights, axis=-1, keepdims=True)))
            return jnp.einsum('hqk,khd->qhd', weights, group_value, precision=PRECISE)
        blocks = (group_query.reshape(-1, TOK_DEV, HEADS, HDIM), group_place.reshape(-1, TOK_DEV), group_document.reshape(-1, TOK_DEV))
        return lax.map(jax.checkpoint(one_block), blocks).reshape(GROUP, HEADS, HDIM)
    return lax.map(one_group, (queries, key_rows, value_rows, places, documents))

def experts_apply(second_low, route_gates, expert_ids, expert_weights):
    capacity = MOST * N_CTX * N_FSDP
    numbers = jnp.arange(EXPERTS, dtype=jnp.int32)
    member = expert_ids[:, :, None] == numbers[None, None, :]
    chosen = jnp.any(member, axis=1)
    scaled = lax.optimization_barrier(jnp.sum(jnp.where(member, route_gates[:, :, None], 0.0), axis=1))
    row_ranks = jnp.cumsum(chosen.astype(jnp.int32), axis=0) - 1
    token_numbers = jnp.broadcast_to(jnp.arange(TOKENS, dtype=jnp.int32)[:, None], (TOKENS, EXPERTS))
    expert_numbers = jnp.broadcast_to(numbers[None, :], (TOKENS, EXPERTS))
    slot_index = jnp.where(chosen, row_ranks, capacity)
    picked = jnp.zeros((EXPERTS, capacity), jnp.int32).at[expert_numbers, slot_index].set(token_numbers, mode='drop')
    filled = jnp.arange(capacity, dtype=jnp.int32)[None, :] < lax.optimization_barrier(jnp.sum(chosen.astype(jnp.int32), axis=0))[:, None]
    factors = jnp.where(filled, jnp.take_along_axis(scaled.T, picked, axis=1), 0.0)
    slice_rows = jnp.repeat(picked, SPLIT, axis=0)
    slice_factors = jnp.repeat(factors, SPLIT, axis=0)
    third_part = SLICE_BLOCKS // 3

    def one_slice(members):
        blocks, rows_here, factors_here = members
        w_gate = to_matrix(blocks[:third_part], D, SLICE)
        w_up = to_matrix(blocks[third_part:2 * third_part], D, SLICE)
        w_down = to_matrix(blocks[2 * third_part:], SLICE, D)
        entering = low_back(second_low[rows_here])
        gate_proj = low_back(jnp.dot(entering, w_gate, precision=PRECISE))
        up_proj = low_back(jnp.dot(entering, w_up, precision=PRECISE))
        activated = low(jax.nn.silu(gate_proj) * up_proj)
        result = low_back(low(jnp.dot(activated, w_down, precision=PRECISE)))
        return result * factors_here[:, None]
    contrib = lax.map(jax.checkpoint(one_slice), (expert_weights, slice_rows, slice_factors))
    gathered_sum = jnp.zeros((TOKENS, D), jnp.float32)
    return gathered_sum.at[slice_rows.reshape(-1)].add(contrib.reshape(-1, D))

def fixed_routes(second, route_gates, expert_ids, constants):
    copy_share = lax.optimization_barrier(jnp.sum(jnp.where(expert_ids == EXPERTS + 1, route_gates, 0.0), axis=1))
    numbers = EXPERTS + 2 + jnp.arange(ZEROS - 2, dtype=jnp.int32)
    const_share = lax.optimization_barrier(jnp.sum(jnp.where(expert_ids[:, :, None] == numbers[None, None, :], route_gates[:, :, None], 0.0), axis=1))
    return copy_share[:, None] * second + jnp.dot(const_share, constants, precision=PRECISE)

def forward_pass(inputs, vectors, attn_weights, expert_weights, router_weights, expert_ids, places, documents):
    per_side = D // BS
    w_project = to_matrix(attn_weights[:3 * per_side * per_side], D, 3 * D)
    w_output = to_matrix(attn_weights[3 * per_side * per_side:], D, D)
    first_norm = low(normalize(inputs, vectors[0]))
    projected = low_back(low(jnp.dot(first_norm, w_project, precision=PRECISE)))
    grouped = projected.reshape(N_CTX, GROUPS, TOK_DEV, 3, HEADS, HDIM).transpose(1, 0, 2, 3, 4, 5).reshape(GROUPS, GROUP, 3, HEADS, HDIM)
    attended = attend(grouped[:, :, 0], grouped[:, :, 1], grouped[:, :, 2], places, documents)
    attended = attended.reshape(GROUPS, N_CTX, TOK_DEV, D).transpose(1, 0, 2, 3).reshape(TOKENS, D)
    attended = low_back(low(attended))
    middle = inputs + low_back(jnp.dot(attended, w_output, precision=PRECISE))
    second = normalize(middle, vectors[1])
    second_low = low(second)
    logits = jnp.dot(second_low, router_weights, precision=PRECISE)
    route_gates = jax.nn.softmax(jnp.take_along_axis(logits, expert_ids, axis=1), axis=-1)
    routed = experts_apply(second_low, route_gates, expert_ids, expert_weights)
    return middle + routed + fixed_routes(second, route_gates, expert_ids, vectors[2:])

def shampoo_step(weights, gradient, left_stat, right_stat, left_root, right_root, step_rates):
    left_new = STAT_DECAY * left_stat + (1.0 - STAT_DECAY) * jnp.einsum('nij,nkj->nik', gradient, gradient, precision=PRECISE)
    right_new = STAT_DECAY * right_stat + (1.0 - STAT_DECAY) * jnp.einsum('nji,njk->nik', gradient, gradient, precision=PRECISE)
    turned = jnp.einsum('nij,njk->nik', gradient, right_root, precision=PRECISE)
    direction = jnp.einsum('nij,njk->nik', left_root, turned, precision=PRECISE)
    return (left_new, right_new, weights - step_rates * direction)

def reference(inputs, out_grad, vectors, block_order, seq_lengths, expert_ids, attn_weights, attn_left, attn_right, attn_left_root, attn_right_root, expert_weights, expert_left, expert_right, expert_left_root, expert_right_root, router_weights, router_left, router_right, router_left_root, router_right_root):
    places, documents = positions_of(block_order, seq_lengths)

    def closed(inputs_now, vectors_now, attn_now, expert_now, router_now):
        return forward_pass(inputs_now, vectors_now, attn_now, expert_now, router_now, expert_ids, places, documents)
    attn_float = attn_weights.astype(jnp.float32)
    expert_float = expert_weights.astype(jnp.float32)
    router_float = router_weights.astype(jnp.float32)
    output, pullback = jax.vjp(closed, inputs, vectors, attn_float, expert_float, router_float)
    input_grad, vector_grads, attn_grads, expert_grads, router_grads = pullback(out_grad)
    per_side = D // BS
    attn_rates = jnp.where(jnp.arange(ATT_BLOCKS) < 3 * per_side * per_side, RATE_PROJECT, RATE_OUTPUT)[:, None, None]
    attn_left_new, attn_right_new, attn_new = shampoo_step(attn_float, attn_grads, attn_left, attn_right, attn_left_root, attn_right_root, attn_rates)
    flat_shape = (-1, BS, BS)
    expert_left_flat, expert_right_flat, expert_flat = shampoo_step(expert_float.reshape(flat_shape), expert_grads.reshape(flat_shape), expert_left.reshape(flat_shape), expert_right.reshape(flat_shape), expert_left_root.reshape(flat_shape), expert_right_root.reshape(flat_shape), RATE_EXPERT)
    expert_left_new = expert_left_flat.reshape(expert_left.shape)
    expert_right_new = expert_right_flat.reshape(expert_right.shape)
    expert_new = expert_flat.reshape(expert_weights.shape)
    router_left_new, router_right_new, router_moved = shampoo_step(to_blocks(router_float, BS, NROUTE), to_blocks(router_grads, BS, NROUTE), router_left, router_right, router_left_root, router_right_root, RATE_ROUTER)
    router_new = to_matrix(router_moved, D, NROUTE)
    vector_new = vectors - RATE_VECTOR * TOKENS ** (-0.5) * vector_grads
    return (output, input_grad, vector_grads, vector_new, attn_grads, attn_left_new, attn_right_new, attn_new, expert_grads, expert_left_new, expert_right_new, expert_new, router_grads, router_left_new, router_right_new, router_new)
```

```python
import functools

import jax
import jax.numpy as jnp
from jax import lax
from jax.experimental import pallas as pl
from jax.experimental.pallas import tpu as pltpu
from jax.sharding import PartitionSpec as P

D = 768
HEADS = 12
HDIM = 64
EXPERTS = 8
ZEROS = 4
BS = 128
SLOTS = 4
HEAD_GROUPS = 4
GROUP_WIDTH = HEADS // HEAD_GROUPS * HDIM
GROUP_HEADS = HEADS // HEAD_GROUPS
CHUNK = 256
TILE = 256
SUB = 32

EPSILON = 1e-06
SCORE_SCALE = 0.125
STAT_DECAY = 0.5
RATE_PROJECT = 0.4
RATE_OUTPUT = 3.0
RATE_EXPERT = 0.4
RATE_ROUTER = 0.2
RATE_VECTOR = 0.1
MASKED_SCORE = -1e30
PRECISE = lax.Precision.HIGHEST
F32 = jnp.float32
LOW = jnp.bfloat16
VMEM_LIMIT = 56 * 1024 * 1024


def to_matrix(blocks, height, breadth):
    block_height = blocks.shape[1]
    block_breadth = blocks.shape[2]
    shaped = blocks.reshape(
        height // block_height, breadth // block_breadth, block_height, block_breadth
    )
    return shaped.transpose(0, 2, 1, 3).reshape(height, breadth)


def to_blocks(matrix, block_height, block_breadth):
    height = matrix.shape[0]
    breadth = matrix.shape[1]
    shaped = matrix.reshape(
        height // block_height, block_height, breadth // block_breadth, block_breadth
    )
    return shaped.transpose(0, 2, 1, 3).reshape(-1, block_height, block_breadth)


def normalize_parts(values, scaling):
    factor = lax.rsqrt(jnp.mean(values * values, axis=-1, keepdims=True) + EPSILON)
    return (values * factor * scaling, factor)


def normalize_back(values, factor, scaling, gradient):
    unit_rows = values * factor
    scaled = gradient * scaling
    value_grad = factor * (
        scaled - unit_rows * jnp.mean(scaled * unit_rows, axis=-1, keepdims=True)
    )
    return (value_grad, jnp.sum(gradient * unit_rows, axis=0))


def dot(left, right, left_dim=1, right_dim=0):
    return lax.dot_general(
        left, right, (((left_dim,), (right_dim,)), ((), ())), preferred_element_type=F32
    )


def vmem_spec():
    return pl.BlockSpec(memory_space=pltpu.VMEM)


def smem_spec():
    return pl.BlockSpec(memory_space=pltpu.SMEM)


def params():
    return pltpu.CompilerParams(vmem_limit_bytes=VMEM_LIMIT)


def project_kernel(rows_in, gain, places, shards):
    rows = rows_in.shape[0]
    owners = len(shards) - 1
    depth = D // owners
    breadth = 3 * D
    block_rows = depth // BS
    block_columns = breadth // BS
    pair = 2 * GROUP_WIDTH

    def kernel(places_ref, rows_ref, gain_ref, *refs):
        shard_refs = refs[: owners + 1]
        first_out, factor_out, query_out, pair_out, matrix, first_s = refs[owners + 1 :]
        for number, shard in enumerate(shard_refs):
            owner = places_ref[number]

            @pl.when(owner < owners)
            def _(owner=owner, shard=shard):
                for row in range(block_rows):
                    for column in range(block_columns):
                        matrix[
                            owner, row * BS : (row + 1) * BS, column * BS : (column + 1) * BS
                        ] = shard[row * block_columns + column]

        def norm(tile, carry):
            at = pl.ds(pl.multiple_of(tile * SUB, SUB), SUB)
            values = rows_ref[at, :]
            factor = lax.rsqrt(jnp.mean(values * values, axis=1, keepdims=True) + EPSILON)
            first = (values * factor * gain_ref[...]).astype(LOW)
            factor_out[at, :] = factor
            first_out[at, :] = first
            for owner in range(owners):
                first_s[owner, at, :] = first[:, owner * depth : (owner + 1) * depth]
            return carry

        lax.fori_loop(0, rows // SUB, norm, 0)
        for tile in range(breadth // pair):
            at = slice(tile * pair, (tile + 1) * pair)
            total = dot(first_s[0], matrix[0, :, at])
            for owner in range(1, owners):
                total = total + dot(first_s[owner], matrix[owner, :, at])
            total = total.astype(LOW)
            part = tile * pair // D
            group = tile * pair % D // GROUP_WIDTH
            for side in range(2):
                piece = total[:, side * GROUP_WIDTH : (side + 1) * GROUP_WIDTH]
                if part == 0:
                    query_out[group + side] = jnp.concatenate(
                        [piece[: rows // 2], piece[rows // 2 :]], axis=1
                    )
                else:
                    pair_out[
                        group + side, :, (part - 1) * GROUP_WIDTH : part * GROUP_WIDTH
                    ] = piece

    return pl.pallas_call(
        kernel,
        in_specs=[smem_spec()] + [vmem_spec()] * (owners + 3),
        out_specs=[vmem_spec()] * 5,
        out_shape=[
            jax.ShapeDtypeStruct((rows, D), LOW),
            jax.ShapeDtypeStruct((rows, 1), F32),
            jax.ShapeDtypeStruct((HEAD_GROUPS, rows // 2, pair), LOW),
            jax.ShapeDtypeStruct((HEAD_GROUPS, rows, pair), LOW),
            jax.ShapeDtypeStruct((owners, depth, breadth), LOW),
        ],
        scratch_shapes=[pltpu.VMEM((owners, rows, depth), LOW)],
        compiler_params=params(),
        cost_estimate=pl.CostEstimate(
            flops=2 * rows * D, bytes_accessed=1_000_000, transcendentals=0
        ),
        name="project",
    )(places, rows_in, gain, *shards)


def head_masks(value):
    lane = lax.broadcasted_iota(jnp.int32, (1, GROUP_WIDTH), 1)
    return [
        jnp.where(lane // HDIM == head, value, 0.0).astype(F32) for head in range(GROUP_HEADS)
    ]


def stack_heads(rows, masks):
    return jnp.concatenate([rows * mask.astype(rows.dtype) for mask in masks], axis=0)


def packed_at(slot, block_rows):
    first_row = slot % 2 * block_rows
    first_lane = slot // 2 * GROUP_WIDTH
    return slice(first_row, first_row + block_rows), slice(first_lane, first_lane + GROUP_WIDTH)


def pack_rows(values):
    groups, rows, width = values.shape
    return values.reshape(groups, 2, rows // 2, width).transpose(0, 2, 1, 3).reshape(
        groups, rows // 2, 2 * width
    )


def unpack_rows(values):
    groups, rows, width = values.shape
    return values.reshape(groups, rows, 2, width // 2).transpose(0, 2, 1, 3).reshape(
        groups, 2 * rows, width // 2
    )


def fill_sorted(kpb, sources, key_sorted, value_sorted, block_rows, block_count):
    key_sorted[0:CHUNK, :] = jnp.zeros((CHUNK, GROUP_WIDTH), LOW)
    value_sorted[0:CHUNK, :] = jnp.zeros((CHUNK, GROUP_WIDTH), LOW)
    for number, source in enumerate(sources):

        def fill(item, carry, source=source, number=number):
            from_row = pl.multiple_of(item % SLOTS * block_rows, block_rows)
            to_row = pl.multiple_of(CHUNK + kpb[number, item] * block_rows, 32)
            rows = source[item // SLOTS, pl.ds(from_row, block_rows), :]
            key_sorted[pl.ds(to_row, block_rows), :] = rows[:, 0:GROUP_WIDTH]
            value_sorted[pl.ds(to_row, block_rows), :] = rows[:, GROUP_WIDTH:]
            return carry

        lax.fori_loop(0, block_count, fill, 0)


def list_steps(kpb, ends, sequences, block_rows, block_count, block_of, place_of):
    def one_block(item, first_step):
        first = kpb[0, item] * block_rows
        lowest = jnp.int32(0)
        for sequence in range(sequences):
            ending = ends[sequence]
            lowest = jnp.where(first >= ending, ending, lowest)
        top = first + block_rows
        count = (top - lowest + CHUNK - 1) // CHUNK

        def one_step(step, carry):
            block_of[first_step + step] = item
            place_of[first_step + step] = top - (step + 1) * CHUNK
            return carry

        lax.fori_loop(0, count, one_step, 0)
        return first_step + count

    return lax.fori_loop(0, block_count, one_block, jnp.int32(0))


def fill_limits(kpb, ends, sequences, block_rows, item, start_s, place_s):
    for tile in range(GROUP_HEADS * block_rows // SUB):
        within = tile * SUB % block_rows
        places = (
            kpb[0, item] * block_rows
            + within
            + lax.broadcasted_iota(jnp.int32, (SUB, BS), 0)
        )
        starts = jnp.zeros_like(places)
        for sequence in range(sequences):
            ending = ends[sequence]
            starts = jnp.where(places >= ending, ending, starts)
        at_rows = slice(tile * SUB, (tile + 1) * SUB)
        start_s[item, at_rows, :] = starts
        place_s[item, at_rows, :] = places


def pipeline(total, scores, middle, products):
    scores(jnp.int32(0), 0)

    def pair(number, carry):
        step = 2 * number
        scores(step + 1, 1)
        middle(step, 0)
        products(step - 1, 1)
        scores(step + 2, 0)
        middle(step + 1, 1)
        products(step, 0)
        return carry

    lax.fori_loop(0, (total + 2) // 2, pair, 0)


def tile_slices(count):
    return [slice(tile * SUB, (tile + 1) * SUB) for tile in range(count)]


def attend_kernel(sources_count, block_rows, sequences, *refs):
    kpb, ends, queries = refs[:3]
    sources = refs[3 : 3 + sources_count]
    raw_out, low_out, lse_out, key_sorted, value_sorted, query_s, start_s, place_s = refs[
        3 + sources_count : 11 + sources_count
    ]
    best_s, total_s, gathered_s, score_0, score_1, weight_0, weight_1, fade_0, fade_1 = refs[
        11 + sources_count : 20 + sources_count
    ]
    block_of, place_of = refs[20 + sources_count :]
    score_s, weight_s, fade_s = (score_0, score_1), (weight_0, weight_1), (fade_0, fade_1)
    block_count = queries.shape[0] * SLOTS
    stacked = GROUP_HEADS * block_rows
    tiles = tile_slices(stacked // SUB)
    fill_sorted(kpb, sources, key_sorted, value_sorted, block_rows, block_count)
    total = list_steps(kpb, ends, sequences, block_rows, block_count, block_of, place_of)
    masks = head_masks(SCORE_SCALE)
    plain = head_masks(1.0)

    def load(group, carry):
        for slot in range(SLOTS):
            rows, lanes = packed_at(slot, block_rows)
            query_s[group * SLOTS + slot] = stack_heads(queries[group, rows, lanes], masks)
        return carry

    lax.fori_loop(0, block_count // SLOTS, load, 0)

    def prepare(item, carry):
        fill_limits(kpb, ends, sequences, block_rows, item, start_s, place_s)
        best_s[item] = jnp.full((stacked, BS), MASKED_SCORE, F32)
        total_s[item] = jnp.zeros((stacked, BS), F32)
        gathered_s[item] = jnp.zeros((stacked, GROUP_WIDTH), F32)
        return carry

    lax.fori_loop(0, block_count, prepare, 0)
    weight_1[...] = jnp.zeros_like(weight_1)
    fade_1[...] = jnp.ones_like(fade_1)

    def find(step):
        inside = jnp.clip(step, 0, total - 1)
        return block_of[inside], place_of[inside]

    def scores(step, side):
        item, low_place = find(step)
        at = pl.multiple_of(low_place + CHUNK, 32)
        score_s[side][...] = dot(query_s[item], key_sorted[pl.ds(at, CHUNK), :], 1, 1)

    def middle(step, side):
        item, low_place = find(step)
        low_place = jnp.where(step < total, low_place, -(1 << 24))
        lanes = low_place + lax.broadcasted_iota(jnp.int32, (1, BS), 1)
        for rows in tiles:
            starts, places = start_s[item, rows, :], place_s[item, rows, :]
            parts = []
            for part in range(CHUNK // BS):
                key_places = lanes + part * BS
                allowed = (key_places >= starts) & (key_places <= places)
                found = score_s[side][rows, part * BS : (part + 1) * BS]
                parts.append(jnp.where(allowed, found, MASKED_SCORE))
            best = best_s[item, rows, :]
            top = jnp.max(functools.reduce(jnp.maximum, parts), axis=1, keepdims=True)
            peak = jnp.maximum(best, top)
            fade = jnp.exp(best - peak)
            so_far = total_s[item, rows, :] * fade
            for part, found in enumerate(parts):
                weights = jnp.exp(found - peak)
                so_far = so_far + weights
                weight_s[side][rows, part * BS : (part + 1) * BS] = weights.astype(LOW)
            best_s[item, rows, :] = peak
            total_s[item, rows, :] = so_far
            fade_s[side][rows, :] = fade

    def products(step, side):
        item, low_place = find(step)
        at = pl.multiple_of(low_place + CHUNK, 32)
        fade = fade_s[side][...]
        fade = jnp.concatenate([fade, fade[:, : GROUP_WIDTH - BS]], axis=1)
        gathered_s[item] = gathered_s[item] * fade + dot(
            weight_s[side][...], value_sorted[pl.ds(at, CHUNK), :]
        )

    pipeline(total, scores, middle, products)

    def finish(group, carry):
        for slot in range(SLOTS):
            item = group * SLOTS + slot
            rows, lanes = packed_at(slot, block_rows)
            sums = jnp.sum(total_s[item], axis=1, keepdims=True)
            gathered = gathered_s[item] / sums
            result = jnp.zeros((block_rows, GROUP_WIDTH), F32)
            for head in range(GROUP_HEADS):
                result = result + (
                    plain[head] * gathered[head * block_rows : (head + 1) * block_rows]
                )
            raw_out[group, slot * block_rows : (slot + 1) * block_rows, :] = result
            low_out[group, rows, lanes] = result.astype(LOW)
            lse_out[item] = best_s[item][:, 0:1] + jnp.log(sums)
        return carry

    lax.fori_loop(0, block_count // SLOTS, finish, 0)


def attend_sizes(queries, pairs):
    groups, rows, _ = pairs[0].shape
    block_rows = rows // SLOTS
    all_rows = groups * rows * len(pairs)
    blocks = groups * SLOTS
    stacked = GROUP_HEADS * block_rows
    return groups, rows, block_rows, all_rows, blocks, stacked


def attend(kpb, ends, queries, pairs):
    groups, rows, block_rows, all_rows, blocks, stacked = attend_sizes(queries, pairs)
    steps = blocks * (all_rows // CHUNK + 1)
    return pl.pallas_call(
        functools.partial(attend_kernel, len(pairs), block_rows, ends.shape[0]),
        in_specs=[smem_spec()] * 2 + [vmem_spec()] * (1 + len(pairs)),
        out_specs=[vmem_spec()] * 3,
        out_shape=[
            jax.ShapeDtypeStruct((groups, rows, GROUP_WIDTH), F32),
            jax.ShapeDtypeStruct((groups, rows // 2, 2 * GROUP_WIDTH), LOW),
            jax.ShapeDtypeStruct((blocks, stacked, 1), F32),
        ],
        scratch_shapes=[
            pltpu.VMEM((CHUNK + all_rows, GROUP_WIDTH), LOW),
            pltpu.VMEM((CHUNK + all_rows, GROUP_WIDTH), LOW),
            pltpu.VMEM((blocks, stacked, GROUP_WIDTH), LOW),
            pltpu.VMEM((blocks, stacked, BS), jnp.int32),
            pltpu.VMEM((blocks, stacked, BS), jnp.int32),
            pltpu.VMEM((blocks, stacked, BS), F32),
            pltpu.VMEM((blocks, stacked, BS), F32),
            pltpu.VMEM((blocks, stacked, GROUP_WIDTH), F32),
            pltpu.VMEM((stacked, CHUNK), F32),
            pltpu.VMEM((stacked, CHUNK), F32),
            pltpu.VMEM((stacked, CHUNK), LOW),
            pltpu.VMEM((stacked, CHUNK), LOW),
            pltpu.VMEM((stacked, BS), F32),
            pltpu.VMEM((stacked, BS), F32),
            pltpu.SMEM((steps,), jnp.int32),
            pltpu.SMEM((steps,), jnp.int32),
        ],
        compiler_params=params(),
        cost_estimate=pl.CostEstimate(
            flops=groups * rows * HDIM,
            bytes_accessed=1_000_000,
            transcendentals=0,
        ),
        name="attend_forward",
    )(kpb, ends, queries, *pairs)


def attend_back_kernel(sources_count, block_rows, sequences, *refs):
    kpb, ends, queries = refs[:3]
    sources = refs[3 : 3 + sources_count]
    out_grad, raw, lse = refs[3 + sources_count : 6 + sources_count]
    query_out = refs[6 + sources_count]
    pair_outs = refs[7 + sources_count : 7 + 2 * sources_count]
    rest = refs[7 + 2 * sources_count :]
    key_sorted, value_sorted, key_grad, value_grad, query_s, grad_s, query_grad = rest[:7]
    start_s, place_s, shift_s, delta_s = rest[7:11]
    score_s, back_s, weight_s, change_s = rest[11:13], rest[13:15], rest[15:17], rest[17:19]
    block_of, place_of = rest[19:]
    block_count = queries.shape[0] * SLOTS
    stacked = GROUP_HEADS * block_rows
    tiles = tile_slices(stacked // SUB)
    fill_sorted(kpb, sources, key_sorted, value_sorted, block_rows, block_count)
    total = list_steps(kpb, ends, sequences, block_rows, block_count, block_of, place_of)
    key_grad[...] = jnp.zeros_like(key_grad)
    value_grad[...] = jnp.zeros_like(value_grad)
    weight_s[1][...] = jnp.zeros_like(weight_s[1])
    change_s[1][...] = jnp.zeros_like(change_s[1])
    masks = head_masks(SCORE_SCALE)
    plain = head_masks(1.0)

    def load(group, carry):
        for slot in range(SLOTS):
            item = group * SLOTS + slot
            rows, lanes = packed_at(slot, block_rows)
            query_s[item] = stack_heads(queries[group, rows, lanes], masks)
            grad = stack_heads(out_grad[group, rows, lanes], plain)
            grad_s[item] = grad
            values = raw[group, slot * block_rows : (slot + 1) * block_rows, :]
            delta = jnp.sum(
                grad.astype(F32) * jnp.concatenate([values] * GROUP_HEADS, axis=0),
                axis=1,
                keepdims=True,
            )
            delta_s[item] = jnp.broadcast_to(delta, (stacked, BS))
        return carry

    lax.fori_loop(0, block_count // SLOTS, load, 0)

    def prepare(item, carry):
        shift_s[item] = jnp.broadcast_to(lse[item], (stacked, BS))
        query_grad[item] = jnp.zeros((stacked, GROUP_WIDTH), F32)
        fill_limits(kpb, ends, sequences, block_rows, item, start_s, place_s)
        return carry

    lax.fori_loop(0, block_count, prepare, 0)

    def find(step):
        inside = jnp.clip(step, 0, total - 1)
        return block_of[inside], place_of[inside]

    def scores(step, side):
        item, low_place = find(step)
        at = pl.ds(pl.multiple_of(low_place + CHUNK, 32), CHUNK)
        score_s[side][...] = dot(query_s[item], key_sorted[at, :], 1, 1)
        back_s[side][...] = dot(grad_s[item], value_sorted[at, :], 1, 1)

    def middle(step, side):
        item, low_place = find(step)
        low_place = jnp.where(step < total, low_place, -(1 << 24))
        lanes = low_place + lax.broadcasted_iota(jnp.int32, (1, BS), 1)
        for rows in tiles:
            starts, places = start_s[item, rows, :], place_s[item, rows, :]
            shift, delta = shift_s[item, rows, :], delta_s[item, rows, :]
            for part in range(CHUNK // BS):
                at_lanes = slice(part * BS, (part + 1) * BS)
                key_places = lanes + part * BS
                allowed = (key_places >= starts) & (key_places <= places)
                found = score_s[side][rows, at_lanes] - shift
                weights = jnp.exp(jnp.where(allowed, found, MASKED_SCORE))
                weight_s[side][rows, at_lanes] = weights.astype(LOW)
                change = weights * (back_s[side][rows, at_lanes] - delta)
                change_s[side][rows, at_lanes] = change.astype(LOW)

    def products(step, side):
        item, low_place = find(step)
        at = pl.ds(pl.multiple_of(low_place + CHUNK, 32), CHUNK)
        value_grad[at, :] += dot(weight_s[side][...], grad_s[item], 0, 0)
        key_grad[at, :] += dot(change_s[side][...], query_s[item], 0, 0)
        query_grad[item] += dot(change_s[side][...], key_sorted[at, :])

    pipeline(total, scores, middle, products)

    def finish(item, carry):
        at = pl.ds(pl.multiple_of(item % SLOTS * block_rows, block_rows), block_rows)
        result = jnp.zeros((block_rows, GROUP_WIDTH), F32)
        for head in range(GROUP_HEADS):
            result = result + masks[head] * (
                query_grad[item, head * block_rows : (head + 1) * block_rows, :]
            )
        query_out[item // SLOTS, at, :] = result.astype(LOW)
        return carry

    lax.fori_loop(0, block_count, finish, 0)
    for number, target in enumerate(pair_outs):

        def drain(item, carry, number=number, target=target):
            to_row = pl.multiple_of(item % SLOTS * block_rows, block_rows)
            from_row = pl.multiple_of(CHUNK + kpb[number, item] * block_rows, 32)
            pair = jnp.concatenate(
                [
                    key_grad[pl.ds(from_row, block_rows), :],
                    value_grad[pl.ds(from_row, block_rows), :],
                ],
                axis=1,
            )
            target[item // SLOTS, pl.ds(to_row, block_rows), :] = pair.astype(target.dtype)
            return carry

        lax.fori_loop(0, block_count, drain, 0)


def attend_back(kpb, ends, queries, pairs, out_grad, raw, lse):
    groups, rows, block_rows, all_rows, blocks, stacked = attend_sizes(queries, pairs)
    steps = blocks * (all_rows // CHUNK + 1)
    limit = pltpu.VMEM((blocks, stacked, BS), jnp.int32)
    row_values = pltpu.VMEM((blocks, stacked, BS), F32)
    sorted_low = pltpu.VMEM((CHUNK + all_rows, GROUP_WIDTH), LOW)
    sorted_sum = pltpu.VMEM((CHUNK + all_rows, GROUP_WIDTH), F32)
    stacked_low = pltpu.VMEM((blocks, stacked, GROUP_WIDTH), LOW)
    square = pltpu.VMEM((stacked, CHUNK), F32)
    square_low = pltpu.VMEM((stacked, CHUNK), LOW)
    return pl.pallas_call(
        functools.partial(attend_back_kernel, len(pairs), block_rows, ends.shape[0]),
        in_specs=[smem_spec()] * 2 + [vmem_spec()] * (4 + len(pairs)),
        out_specs=[vmem_spec()] * (1 + len(pairs)),
        out_shape=[
            jax.ShapeDtypeStruct((groups, rows, GROUP_WIDTH), LOW),
            jax.ShapeDtypeStruct((groups, rows, 2 * GROUP_WIDTH), F32),
        ]
        + [jax.ShapeDtypeStruct((groups, rows, 2 * GROUP_WIDTH), LOW) for _ in pairs[1:]],
        scratch_shapes=[sorted_low] * 2
        + [sorted_sum] * 2
        + [stacked_low] * 2
        + [pltpu.VMEM((blocks, stacked, GROUP_WIDTH), F32)]
        + [limit] * 2
        + [row_values] * 2
        + [square] * 4
        + [square_low] * 4
        + [pltpu.SMEM((steps,), jnp.int32)] * 2,
        compiler_params=params(),
        cost_estimate=pl.CostEstimate(
            flops=groups * rows * HDIM,
            bytes_accessed=1_000_000,
            transcendentals=0,
        ),
        name="attend_backward",
    )(kpb, ends, queries, *pairs, out_grad, raw, lse)


def side_blocks():
    return D // BS


def bring(places, sources, held, done):
    copies = []
    for number, source in enumerate(sources):
        size = source.shape[0]
        target = held.at[pl.ds(places[number] * size, size)]
        copies.append(pltpu.make_async_copy(source, target, done.at[number]))
    for copy in copies:
        copy.start()
    for copy in copies:
        copy.wait()


def wide_tile(held, first, hidden_blocks, step):
    rows = []
    for row in range(side_blocks()):
        at = first + row * hidden_blocks + 2 * step
        rows.append(jnp.concatenate([held[at], held[at + 1]], axis=1))
    return jnp.concatenate(rows, axis=0)


def tall_tile(held, first, step):
    side = side_blocks()
    rows = []
    for half in range(2):
        at = first + (2 * step + half) * side
        rows.append(jnp.concatenate([held[at + column] for column in range(side)], axis=1))
    return jnp.concatenate(rows, axis=0)


def expert_sizes(weights):
    total = sum(array.shape[0] for array in weights[1])
    return total, total // (3 * side_blocks())


def expert_forward(rows_in, weights):
    rows = rows_in.shape[0]
    places, sources = weights
    count = len(sources)
    total_blocks, hidden_blocks = expert_sizes(weights)
    up_first = side_blocks() * hidden_blocks

    def kernel(places_ref, rows_ref, *refs):
        source_refs = refs[:count]
        result, gate_o, up_o, inner_o, total, held, done = refs[count:]
        step = pl.program_id(0)

        @pl.when(step == 0)
        def _():
            bring(places_ref, source_refs, held, done)
            total[...] = jnp.zeros_like(total)

        gate_tile = wide_tile(held, 0, hidden_blocks, step)
        up_tile = wide_tile(held, up_first, hidden_blocks, step)
        down_tile = tall_tile(held, 2 * up_first, step)

        for number in range(rows // TILE):
            first = number * TILE
            at = pl.ds(first, TILE)
            entering = rows_ref[at, :]
            gate_o[at, :] = dot(entering, gate_tile)
            up_o[at, :] = dot(entering, up_tile)
            for sub in range(TILE // SUB):
                now = pl.ds(first + sub * SUB, SUB)
                gate = gate_o[now, :]
                inner_o[now, :] = (gate * jax.nn.sigmoid(gate) * up_o[now, :]).astype(LOW)
            total[at, :] += dot(inner_o[at, :], down_tile)

        @pl.when(step == pl.num_programs(0) - 1)
        def _():
            result[...] = total[...].astype(LOW)

    fixed = pl.BlockSpec((rows, D), lambda step: (0, 0))
    hidden = pl.BlockSpec((rows, TILE), lambda step: (0, step))
    hidden_size = (rows, hidden_blocks * BS)
    return pl.pallas_call(
        kernel,
        grid=(hidden_blocks // 2,),
        in_specs=[smem_spec(), fixed] + [pl.BlockSpec(memory_space=pl.ANY)] * count,
        out_specs=[fixed] + [hidden] * 3,
        out_shape=[
            jax.ShapeDtypeStruct((rows, D), LOW),
            jax.ShapeDtypeStruct(hidden_size, F32),
            jax.ShapeDtypeStruct(hidden_size, F32),
            jax.ShapeDtypeStruct(hidden_size, LOW),
        ],
        scratch_shapes=[
            pltpu.VMEM((rows, D), F32),
            pltpu.VMEM((total_blocks, BS, BS), LOW),
            pltpu.SemaphoreType.DMA((count,)),
        ],
        compiler_params=params(),
        cost_estimate=pl.CostEstimate(
            flops=6 * rows * D * hidden_blocks * BS,
            bytes_accessed=6 * D * hidden_blocks * BS + 4 * rows * D,
            transcendentals=0,
        ),
        name="expert_forward",
    )(places, rows_in, *sources)


def expert_row_grads(grads_in, gate_in, up_in, weights):
    rows = grads_in.shape[0]
    places, sources = weights
    count = len(sources)
    total_blocks, hidden_blocks = expert_sizes(weights)
    up_first = side_blocks() * hidden_blocks

    def kernel(places_ref, grads_ref, gate_i, up_i, *refs):
        source_refs = refs[:count]
        back, gate_s, up_s, total, inner_grad_s, held, done = refs[count:]
        step = pl.program_id(0)

        @pl.when(step == 0)
        def _():
            bring(places_ref, source_refs, held, done)
            total[...] = jnp.zeros_like(total)

        gate_tile = wide_tile(held, 0, hidden_blocks, step)
        up_tile = wide_tile(held, up_first, hidden_blocks, step)
        down_tile = tall_tile(held, 2 * up_first, step)

        for number in range(rows // TILE):
            first = number * TILE
            at = pl.ds(first, TILE)
            inner_grad_s[at, :] = dot(grads_ref[at, :], down_tile, 1, 1)
            for sub in range(TILE // SUB):
                now = pl.ds(first + sub * SUB, SUB)
                gate = gate_i[now, :]
                inner_grad = inner_grad_s[now, :]
                sigmoid = jax.nn.sigmoid(gate)
                up_s[now, :] = (inner_grad * (gate * sigmoid)).astype(LOW)
                gate_s[now, :] = (
                    inner_grad * up_i[now, :] * (sigmoid * (1.0 + gate * (1.0 - sigmoid)))
                ).astype(LOW)
            total[at, :] += dot(gate_s[at, :], gate_tile, 1, 1) + dot(
                up_s[at, :], up_tile, 1, 1
            )

        @pl.when(step == pl.num_programs(0) - 1)
        def _():
            back[...] = total[...].astype(LOW)

    fixed = pl.BlockSpec((rows, D), lambda step: (0, 0))
    hidden = pl.BlockSpec((rows, TILE), lambda step: (0, step))
    hidden_shape = jax.ShapeDtypeStruct((rows, hidden_blocks * BS), LOW)
    return pl.pallas_call(
        kernel,
        grid=(hidden_blocks // 2,),
        in_specs=[smem_spec(), fixed, hidden, hidden]
        + [pl.BlockSpec(memory_space=pl.ANY)] * count,
        out_specs=[fixed] + [hidden] * 2,
        out_shape=[jax.ShapeDtypeStruct((rows, D), LOW)] + [hidden_shape] * 2,
        scratch_shapes=[
            pltpu.VMEM((rows, D), F32),
            pltpu.VMEM((rows, TILE), F32),
            pltpu.VMEM((total_blocks, BS, BS), LOW),
            pltpu.SemaphoreType.DMA((count,)),
        ],
        compiler_params=params(),
        cost_estimate=pl.CostEstimate(
            flops=6 * rows * D * hidden_blocks * BS,
            bytes_accessed=12 * D * hidden_blocks * BS + 6 * rows * D,
            transcendentals=0,
        ),
        name="expert_row_grads",
    )(places, grads_in, gate_in, up_in, *sources)


def expert_weight_grads(places, rows_in, grads_in, gate_grads, up_grads, inner, sizes):
    rows = rows_in.shape[0]
    hidden_blocks = gate_grads.shape[1] // BS
    side = side_blocks()
    total_blocks = 3 * side * hidden_blocks
    count = len(sizes)
    pieces = sum(len(group) for group in sizes)

    def kernel(places_ref, rows_ref, grads_ref, gate_s, up_s, inner_s, *refs):
        outs = refs[:count]
        turned, held, done = refs[count:]
        step = pl.program_id(0)

        @pl.when(step == 0)
        def _():
            turned[...] = rows_ref[...].T

        def wide_out(source, first):
            product = dot(turned[...], source[...]).astype(LOW)
            for row in range(side):
                for column in range(2):
                    held[first + row * hidden_blocks + 2 * step + column] = product[
                        row * BS : (row + 1) * BS, column * BS : (column + 1) * BS
                    ]

        wide_out(gate_s, 0)
        wide_out(up_s, side * hidden_blocks)
        product = dot(inner_s[...], grads_ref[...], 0, 0).astype(LOW)
        for half in range(2):
            for column in range(side):
                held[2 * side * hidden_blocks + (2 * step + half) * side + column] = product[
                    half * BS : (half + 1) * BS, column * BS : (column + 1) * BS
                ]

        @pl.when(step == pl.num_programs(0) - 1)
        def _():
            copies = []
            for target, group in zip(outs, sizes):
                first = 0
                for size in group:
                    number = len(copies)
                    source = held.at[pl.ds(places_ref[number] * size, size)]
                    into = target.at[pl.ds(first, size)]
                    copies.append(pltpu.make_async_copy(source, into, done.at[number]))
                    first += size
            for copy in copies:
                copy.start()
            for copy in copies:
                copy.wait()

    fixed = pl.BlockSpec((rows, D), lambda step: (0, 0))
    hidden = pl.BlockSpec((rows, TILE), lambda step: (0, step))
    return pl.pallas_call(
        kernel,
        grid=(hidden_blocks // 2,),
        in_specs=[smem_spec(), fixed, fixed] + [hidden] * 3,
        out_specs=[pl.BlockSpec(memory_space=pl.ANY)] * count,
        out_shape=[jax.ShapeDtypeStruct((sum(group), BS, BS), LOW) for group in sizes],
        scratch_shapes=[
            pltpu.VMEM((D, rows), LOW),
            pltpu.VMEM((total_blocks, BS, BS), LOW),
            pltpu.SemaphoreType.DMA((pieces,)),
        ],
        compiler_params=params(),
        cost_estimate=pl.CostEstimate(
            flops=6 * rows * D * hidden_blocks * BS,
            bytes_accessed=12 * D * hidden_blocks * BS + 6 * rows * D,
            transcendentals=0,
        ),
        name="expert_weight_grads",
    )(places, rows_in, grads_in, gate_grads, up_grads, inner)


def expert_half_grads(which, places, rows_in, grads_in, gate_grads, up_grads, inner, sizes):
    rows = rows_in.shape[0]
    hidden_blocks = gate_grads.shape[1] // BS
    side = side_blocks()
    middle_row = side // 2
    total_blocks = 3 * side * hidden_blocks // 2
    count = len(sizes)
    pieces = sum(len(group) for group in sizes)

    def kernel(which_ref, places_ref, rows_ref, grads_ref, gate_s, up_s, inner_s, *refs):
        outs = refs[:count]
        turned, held, done = refs[count:]
        step = pl.program_id(0)

        @pl.when(step == 0)
        def _():
            turned[...] = rows_ref[...].T

        def wide_out(source, first_row, last_row, first):
            product = dot(turned[first_row * BS : last_row * BS, :], source[...]).astype(LOW)
            for row in range(last_row - first_row):
                for column in range(2):
                    held[first + row * hidden_blocks + 2 * step + column] = product[
                        row * BS : (row + 1) * BS, column * BS : (column + 1) * BS
                    ]

        @pl.when(which_ref[0] == 0)
        def _():
            wide_out(gate_s, 0, side, 0)
            wide_out(up_s, 0, middle_row, side * hidden_blocks)

        @pl.when(which_ref[0] == 1)
        def _():
            wide_out(up_s, middle_row, side, 0)
            product = dot(inner_s[...], grads_ref[...], 0, 0).astype(LOW)
            for half in range(2):
                for column in range(side):
                    held[middle_row * hidden_blocks + (2 * step + half) * side + column] = product[
                        half * BS : (half + 1) * BS, column * BS : (column + 1) * BS
                    ]

        @pl.when(step == pl.num_programs(0) - 1)
        def _():
            copies = []
            for target, group in zip(outs, sizes):
                first = 0
                for size in group:
                    number = len(copies)
                    source = held.at[pl.ds(places_ref[number] * size, size)]
                    into = target.at[pl.ds(first, size)]
                    copies.append(pltpu.make_async_copy(source, into, done.at[number]))
                    first += size
            for copy in copies:
                copy.start()
            for copy in copies:
                copy.wait()

    fixed = pl.BlockSpec((rows, D), lambda step: (0, 0))
    hidden = pl.BlockSpec((rows, TILE), lambda step: (0, step))
    return pl.pallas_call(
        kernel,
        grid=(hidden_blocks // 2,),
        in_specs=[smem_spec(), smem_spec(), fixed, fixed] + [hidden] * 3,
        out_specs=[pl.BlockSpec(memory_space=pl.ANY)] * count,
        out_shape=[jax.ShapeDtypeStruct((sum(group), BS, BS), LOW) for group in sizes],
        scratch_shapes=[
            pltpu.VMEM((D, rows), LOW),
            pltpu.VMEM((total_blocks, BS, BS), LOW),
            pltpu.SemaphoreType.DMA((pieces,)),
        ],
        compiler_params=params(),
        cost_estimate=pl.CostEstimate(
            flops=3 * rows * D * hidden_blocks * BS,
            bytes_accessed=6 * D * hidden_blocks * BS + 6 * rows * D,
            transcendentals=0,
        ),
        name="expert_half_grads",
    )(which, places, rows_in, grads_in, gate_grads, up_grads, inner)


def split_low(values):
    high = values.astype(LOW)
    return high, (values - high.astype(F32)).astype(LOW)


def renew(gradient, weights, left, right, left_root, right_root, rate):
    short = gradient.astype(LOW)
    left_new = STAT_DECAY * left + (1.0 - STAT_DECAY) * dot(short, short, 1, 1)
    right_new = STAT_DECAY * right + (1.0 - STAT_DECAY) * dot(short, short, 0, 0)
    high, rest = split_low(right_root)
    turned = (dot(short, high) + dot(short, rest)).astype(LOW)
    high, rest = split_low(left_root)
    direction = dot(high, turned) + dot(rest, turned)
    return (gradient, left_new, right_new, weights.astype(F32) - rate * direction)


def block_width(count):
    return 4 if count % 4 == 0 else 3 if count % 3 == 0 else 1


def shampoo_half(half, gradients, stats, filled):
    parts = len(gradients)
    count = gradients[0].shape[0]
    width = block_width(count)
    steps = count // width
    spec = pl.BlockSpec((width, BS, BS), lambda step, half: (half[0] * steps + step, 0, 0))
    grad_spec = pl.BlockSpec((width, BS, BS), lambda step, half: (step, 0, 0))

    def kernel(half_ref, *refs):
        for number in range(width):
            total = refs[0][number].astype(F32)
            for ref in refs[1:parts]:
                total = total + ref[number].astype(F32)
            now = [ref[number] for ref in refs[parts : parts + 5]]
            results = renew(total, *now, RATE_EXPERT)
            for target, result in zip(refs[-4:], results):
                target[number] = result

    shape = jax.ShapeDtypeStruct(stats[0].shape, F32)
    extra = list(filled or ())
    return pl.pallas_call(
        kernel,
        grid_spec=pltpu.PrefetchScalarGridSpec(
            num_scalar_prefetch=1,
            grid=(steps,),
            in_specs=[grad_spec] * parts
            + [spec] * 5
            + [pl.BlockSpec(memory_space=pl.ANY)] * len(extra),
            out_specs=[spec] * 4,
        ),
        out_shape=[shape] * 4,
        input_output_aliases={6 + parts + number: number for number in range(len(extra))},
        compiler_params=params(),
        cost_estimate=pl.CostEstimate(
            flops=count * 24 * BS * BS * BS,
            bytes_accessed=count * BS * BS * (34 + 2 * parts),
            transcendentals=0,
        ),
        name="shampoo_half",
    )(half, *gradients, *stats, *extra)


def shampoo(rates, gradient, stats):
    count = gradient.shape[0]
    width = block_width(count)
    spec = pl.BlockSpec((width, BS, BS), lambda step: (step, 0, 0))
    shape = jax.ShapeDtypeStruct((count, BS, BS), F32)

    def kernel(rates_ref, *refs):
        step = pl.program_id(0)
        for number in range(width):
            gradient_now, *stats_now = [ref[number] for ref in refs[:6]]
            results = renew(
                gradient_now.astype(F32), *stats_now, rates_ref[step * width + number]
            )
            for target, result in zip(refs[6:], results):
                target[number] = result

    return pl.pallas_call(
        kernel,
        grid=(count // width,),
        in_specs=[smem_spec()] + [spec] * 6,
        out_specs=[spec] * 4,
        out_shape=[shape] * 4,
        compiler_params=params(),
        cost_estimate=pl.CostEstimate(
            flops=count * 24 * BS * BS * BS,
            bytes_accessed=count * BS * BS * 38,
            transcendentals=0,
        ),
        name="shampoo_blocks",
    )(rates, gradient, *stats)


def shampoo_panel(turn, places, panels, stats):
    groups = len(panels)
    panel_rows = panels[0].shape[0]
    parts = 3
    breadth = groups * GROUP_WIDTH
    count = stats[0].shape[0]
    width = block_width(count)
    spec = pl.BlockSpec((width, BS, BS), lambda step, turn, places: (step, 0, 0))
    fixed = pl.BlockSpec(panels[0].shape, lambda step, turn, places: (0, 0))
    shape = jax.ShapeDtypeStruct((count, BS, BS), F32)
    per_part = breadth // BS
    per_row = parts * per_part
    side = D // BS

    def kernel(turn_ref, places_ref, *refs):
        step = pl.program_id(0)
        panel_refs = refs[:groups]
        stat_refs = refs[groups : groups + 5]
        outs = refs[groups + 5 : groups + 9]
        ordered, matrix = refs[groups + 9 :]

        @pl.when(step == 0)
        def _():
            for number, panel in enumerate(panel_refs):
                ordered[places_ref[number]] = panel[...]
            for part in range(parts):
                matrix[:, part * breadth : (part + 1) * breadth] = jnp.concatenate(
                    [
                        ordered[group, :, part * GROUP_WIDTH : (part + 1) * GROUP_WIDTH].astype(F32)
                        for group in range(groups)
                    ],
                    axis=1,
                )

        turned = turn_ref[0] == 1
        rate = jnp.where(turned, RATE_OUTPUT, RATE_PROJECT).astype(F32)
        for number in range(width):
            block = step * width + number
            row_now = jnp.where(turned, block % side % 2, block // per_row)
            column_now = jnp.where(
                turned, block % side // 2 * per_part + block // side, block % per_row
            )
            found = matrix[
                pl.ds(pl.multiple_of(row_now * BS, BS), BS),
                pl.ds(pl.multiple_of(column_now * BS, BS), BS),
            ]
            found = jnp.where(turned, found.T, found)
            results = renew(found, *[ref[number] for ref in stat_refs], rate)
            for target, result in zip(outs, results):
                target[number] = result

    return pl.pallas_call(
        kernel,
        grid_spec=pltpu.PrefetchScalarGridSpec(
            num_scalar_prefetch=2,
            grid=(count // width,),
            in_specs=[fixed] * groups + [spec] * 5,
            out_specs=[spec] * 4,
            scratch_shapes=[
                pltpu.VMEM((groups, *panels[0].shape), LOW),
                pltpu.VMEM((panel_rows, parts * breadth), F32),
            ],
        ),
        out_shape=[shape] * 4,
        compiler_params=params(),
        cost_estimate=pl.CostEstimate(
            flops=count * 24 * BS * BS * BS,
            bytes_accessed=count * BS * BS * 38,
            transcendentals=0,
        ),
        name="shampoo_panel",
    )(turn, places, *panels, *stats)


def shampoo_small(weights, gradient, left_stat, right_stat, left_root, right_root, step_rates):
    left_new = STAT_DECAY * left_stat + (1.0 - STAT_DECAY) * jnp.einsum(
        "nij,nkj->nik", gradient, gradient, precision=PRECISE
    )
    right_new = STAT_DECAY * right_stat + (1.0 - STAT_DECAY) * jnp.einsum(
        "nji,njk->nik", gradient, gradient, precision=PRECISE
    )
    turned = jnp.einsum("nij,njk->nik", gradient, right_root, precision=PRECISE)
    direction = jnp.einsum("nij,njk->nik", left_root, turned, precision=PRECISE)
    return (left_new, right_new, weights - step_rates * direction)


def shifted(values, axis, size, distance):
    return lax.ppermute(values, axis, [(i, (i + distance) % size) for i in range(size)])


def crossed(values, axes, size, distance):
    return lax.ppermute(values, axes, [(i, i ^ distance) for i in range(size)])


def direct_sum(values, axes, size):
    terms = [values] + [crossed(values, axes, size, step) for step in range(1, size)]
    while len(terms) > 1:
        terms = [terms[at] + terms[at + 1] for at in range(0, len(terms), 2)]
    return terms[0]


def everywhere_sum(values, sizes):
    a_size, b_size, c_size, f_size = sizes
    values = direct_sum(values, "f", f_size)
    values = direct_sum(values, "c", c_size)
    return direct_sum(values, ("a", "b"), a_size * b_size)


def body(
    sizes,
    inputs,
    out_grad,
    vectors,
    block_order,
    seq_lengths,
    expert_ids,
    attn_weights,
    attn_left,
    attn_right,
    attn_left_root,
    attn_right_root,
    expert_weights,
    expert_left,
    expert_right,
    expert_left_root,
    expert_right_root,
    router_weights,
    router_left,
    router_right,
    router_left_root,
    router_right_root,
):
    a_size, b_size, c_size, f_size = sizes
    rows = inputs.shape[0]
    capacity = rows // 4
    tokens_all = rows * a_size * b_size * c_size * f_size
    per_side = D // BS
    project_blocks = 3 * per_side * per_side
    a_place = lax.axis_index("a")
    c_place = lax.axis_index("c")
    f_place = lax.axis_index("f")
    per_device = attn_weights.shape[0]
    per = expert_weights.shape[1]
    shares = b_size * c_size
    local_slices = expert_weights.shape[0]

    by_panels = f_size == 4 and c_size == 2 and a_size == 2
    ends = jnp.cumsum(seq_lengths[0]).astype(jnp.int32)
    order = block_order[0].reshape(a_size * b_size, c_size, SLOTS)
    kpb = jnp.stack(
        [
            lax.dynamic_index_in_dim(order, (c_place - step) % c_size, 1, False).reshape(-1)
            for step in range(c_size)
        ]
    )

    split_count = expert_weights.shape[0] * f_size // EXPERTS
    numbers = jnp.arange(EXPERTS, dtype=jnp.int32)
    spots = (numbers % a_size) * f_size + numbers // a_size if split_count == 1 else numbers
    route_count = EXPERTS + ZEROS
    named = expert_ids[:, :, None] == jnp.arange(route_count, dtype=jnp.int32)[None, None, :]
    route_member = named.astype(F32)
    chosen = jnp.any(named[:, :, :EXPERTS], axis=1).astype(LOW)
    row_numbers = jnp.arange(rows, dtype=jnp.int32)
    before = (row_numbers[None, :] < row_numbers[:, None]).astype(LOW)
    ranks = jnp.dot(before, chosen, preferred_element_type=F32).astype(jnp.int32)
    slots = jnp.sum(
        jnp.where(named[:, :, :EXPERTS], (spots * capacity)[None, None, :] + ranks[:, None, :], 0),
        axis=2,
    )
    slots = jnp.where(expert_ids < EXPERTS, slots, -1)
    slot_numbers = jnp.arange(EXPERTS * capacity, dtype=jnp.int32)
    picks = [
        (slot_numbers[:, None] == slots[:, which][None, :]).astype(LOW) for which in range(2)
    ]
    picks_both = picks[0] + picks[1]

    def to_owners(buffer):
        buffer = buffer.astype(LOW).reshape(EXPERTS, capacity, D)
        if split_count > 1:
            buffer = jnp.repeat(buffer, split_count, axis=0)
        arrived = lax.all_to_all(buffer, ("a", "f"), split_axis=0, concat_axis=0, tiled=True)
        return arrived.reshape(-1, D)

    def return_rows(results):
        return lax.all_to_all(
            results.reshape(EXPERTS * split_count, -1, D),
            ("a", "f"),
            split_axis=0,
            concat_axis=0,
            tiled=True,
        )

    def from_owners(back, pick_matrices):
        back = back.reshape(EXPERTS, split_count, capacity, D)
        return [
            sum(
                dot(matrix, back[:, part].reshape(-1, D), 0, 0) for part in range(split_count)
            )
            for matrix in pick_matrices
        ]

    tie = lax.optimization_barrier
    share_place = lax.axis_index(("b", "c"))

    def over_groups(values):
        return lax.all_to_all(values, ("a", "b"), split_axis=0, concat_axis=0, tiled=True)

    def over_b(values):
        return crossed(values, "b", b_size, 1)

    def over_c(values):
        return crossed(values, "c", c_size, 1)

    if by_panels:
        group_place = lax.axis_index(("a", "b"))
        share_places = jnp.stack([share_place ^ step for step in range(shares)])
        first_spots, other_spots = a_place * shares + share_places, (
            (1 - a_place) * shares + share_places
        )

        def halves(values):
            return [values[: per // 2], values[per // 2 :]]

        own = jnp.where(a_place == 0, expert_weights[0], expert_weights[1])
        own_halves = halves(own)
        sent = jnp.where(a_place == 0, expert_weights[1], expert_weights[0])
        cuts = [slice(0, per // 2), slice(per // 2, per * 3 // 4), slice(per * 3 // 4, per)]
        across = crossed(attn_weights, "f", f_size, 2)
        own_c = over_c(own)
        got = [shifted(sent[cuts[0]], "a", 2, 1), None]
        own_b = [over_b(own_halves[0]), None]

        def both(spot):
            return [2 * spot, 2 * spot + 1]

        weight_places = [first_spots[0], first_spots[1]] + both(first_spots[2])
        weight_places += both(first_spots[3]) + both(other_spots[0]) + both(other_spots[1])
        weight_places += both(other_spots[2]) + both(other_spots[3])
        weight_places = jnp.stack(weight_places).astype(jnp.int32)
        kept_places = jnp.stack([share_places[step] for step in (0, 2, 1, 3)])
        given_places = [share_places[0], 2 * share_places[1], 2 * share_places[3]]
        given_places += [2 * share_places[2] + 1, 2 * share_places[3] + 1]
        given_places += [2 * share_places[2], 2 * share_places[1] + 1]
        kept_places = kept_places.astype(jnp.int32)
        given_places = jnp.stack(given_places).astype(jnp.int32)
        group_places = jnp.stack([group_place ^ step for step in range(HEAD_GROUPS)])
        group_places = group_places.astype(jnp.int32)
        shard_places = jnp.stack([f_place ^ step for step in range(f_size)]).astype(jnp.int32)
        (across, own_c, got[0], own_b[0], kpb, ends, *tables) = tie(
            (across, own_c, got[0], own_b[0], kpb, ends)
            + (weight_places, kept_places, given_places, group_places, shard_places)
        )
        weight_places, kept_places, given_places, group_places, shard_places = tables
        shards = [
            attn_weights,
            crossed(attn_weights, "f", f_size, 1),
            across,
            crossed(across, "f", f_size, 1),
        ]
        first_low, first_factor, own_queries, own_pairs, w_project = project_kernel(
            inputs, vectors[0:1], shard_places, shards
        )
        w_project = w_project.reshape(D, 3 * D)
        own_pairs, got_next = tie((own_pairs, shifted(sent[cuts[1]], "a", 2, 1)))
        own_b[1] = over_b(own_halves[1])
        own_bc = [over_c(own_b[0]), None]
        got_c = [over_c(got[0]), None]
        mine, own_b[1], own_bc[0], got_c[0] = tie(
            (over_groups(own_pairs), own_b[1], own_bc[0], got_c[0])
        )
        other = over_c(mine)
        queries = over_groups(own_queries)
        got_last = shifted(tie((sent[cuts[2]], mine))[0], "a", 2, 1)
        queries, other, got_last = tie((queries, other, got_last))
        got[1] = jnp.concatenate([got_next, got_last], axis=0)
        pairs = [mine, other]
        first_sent, own_b1, got_0, got_1 = tie((first_low, own_b[1], *got, queries))[:4]
        first_parts = [first_low, None, crossed(first_sent, ("a", "b"), HEAD_GROUPS, 2), None]
        own_bc[1] = over_c(own_b1)
        got_c[1] = over_c(got_1)
        got_b = [over_b(got_0), None]
        w_output = shards[3]
        for step in range(f_size - 1):
            w_output = jnp.where(f_place == 3 - step, shards[step], w_output)
        w_output = to_matrix(w_output, D, D)
        raw, low, lse = attend(kpb, ends, queries, pairs)
        raw, low, lse, first_parts[2], own_bc[1], got_c[1], got_b[0] = tie(
            (raw, low, lse, first_parts[2], own_bc[1], got_c[1], got_b[0])
        )
        got_b[1] = over_b(tie((got[1], low))[0])
    else:
        attn_all = lax.all_gather(attn_weights, "f", axis=0, tiled=True)
        w_project = to_matrix(attn_all[:project_blocks], D, 3 * D)
        w_output = to_matrix(attn_all[project_blocks:], D, D)
        first_norm, first_factor = normalize_parts(inputs, vectors[0])
        first_low = first_norm.astype(LOW)
        projected = jnp.dot(first_low, w_project, preferred_element_type=F32).astype(LOW)
        by_part = projected.reshape(rows, 3, HEAD_GROUPS, GROUP_WIDTH)
        own_queries = by_part[:, 0].transpose(1, 0, 2)
        own_pairs = (
            by_part[:, 1:].transpose(2, 0, 1, 3).reshape(HEAD_GROUPS, rows, 2 * GROUP_WIDTH)
        )
        mine = over_groups(own_pairs)
        pairs = [mine] + [shifted(mine, "c", c_size, step) for step in range(1, c_size)]
        queries = over_groups(pack_rows(own_queries))
        raw, low, lse = attend(kpb, ends, queries, pairs)
        weight_places = jnp.arange(local_slices, dtype=jnp.int32)
        weight_shares = [
            lax.all_gather(expert_weights[number], ("b", "c"), axis=0, tiled=True)
            for number in range(local_slices)
        ]
        weights = (weight_places, weight_shares)
    by_heads = unpack_rows(over_groups(low))
    attended = by_heads.transpose(1, 0, 2).reshape(rows, D)
    middle = inputs + jnp.dot(attended, w_output, preferred_element_type=F32)
    second, second_factor = normalize_parts(middle, vectors[1])
    second_low = second.astype(LOW)
    if by_panels:
        second_low, got_b[1] = tie((second_low, got_b[1]))
        first_sent, *got_bc = tie((first_low, *got_b, second_low))[:3]
        first_parts[1] = crossed(first_sent, ("a", "b"), HEAD_GROUPS, 1)
        got_bc = [over_c(part) for part in got_bc]

    logits = jnp.dot(second_low, router_weights, preferred_element_type=F32)
    picked_logits = jnp.sum(jnp.where(named, logits[:, None, :], 0.0), axis=2)
    route_gates = jax.nn.softmax(picked_logits, axis=-1)
    received = to_owners(dot(picks_both, second_low))
    grad_rows = [
        (route_gates[:, which][:, None] * out_grad).astype(LOW) for which in range(2)
    ]
    if by_panels:
        grad_rows[0], first_parts[1], *got_bc = tie((grad_rows[0], first_parts[1], *got_bc))
    arrived = to_owners(dot(picks[0], grad_rows[0]) + dot(picks[1], grad_rows[1]))
    if by_panels:
        weight_shares = [own, own_c, *own_b, *own_bc, *got, *got_c, *got_b, *got_bc]
        weights = (weight_places, weight_shares)
    result, gate_kept, up_kept, inner = expert_forward(received, weights)
    result = return_rows(result)
    back_rows, gate_grads, up_grads = expert_row_grads(arrived, gate_kept, up_kept, weights)
    if by_panels:
        full, part = per, per // 2
        half = a_place.astype(jnp.int32).reshape(1)
        given, hop_c, hop_b, near_b, near_c = expert_half_grads(
            1 - half,
            given_places,
            received,
            arrived,
            gate_grads,
            up_grads,
            inner,
            [(full,), (part, part), (part, part), (part,), (part,)],
        )
        first_parts[3] = over_b(tie((first_parts[2], arrived))[0])
        back_rows, result, near_b, gate_grads, up_grads, first_parts[3] = tie(
            (back_rows, result, near_b, gate_grads, up_grads, first_parts[3])
        )
        back_rows = return_rows(back_rows)
        kept, kept_far, kept_near, kept_next = expert_half_grads(
            half,
            kept_places,
            received,
            arrived,
            gate_grads,
            up_grads,
            inner,
            [(full,)] * 4,
        )
        back_rows, kept = tie((back_rows, kept))
        hop_c, hop_b = over_c(hop_c), over_b(hop_b)
    else:
        back_rows = return_rows(back_rows)
        grad_shares = expert_weight_grads(
            jnp.arange(shares, dtype=jnp.int32),
            received,
            arrived,
            gate_grads,
            up_grads,
            inner,
            [(per,)] * shares,
        )
    expert_rows = jnp.stack(from_owners(result, picks), axis=1)
    const_member = route_member[:, :, EXPERTS + 2 :]
    copy_member = route_member[:, :, EXPERTS + 1]
    route_values = (
        expert_rows
        + copy_member[:, :, None] * second[:, None, :]
        + jnp.einsum("rkc,cd->rkd", const_member, vectors[2:], precision=PRECISE)
    )
    output = middle + jnp.sum(route_gates[:, :, None] * route_values, axis=1)

    gate_grad = jnp.sum(out_grad[:, None, :] * route_values, axis=2)
    picked_grad = route_gates * (
        gate_grad - jnp.sum(route_gates * gate_grad, axis=1, keepdims=True)
    )
    logit_grad = jnp.sum(route_member * picked_grad[:, :, None], axis=1)
    router_local = lax.dot_general(
        logit_grad, second_low.astype(F32), (((0,), (0,)), ((), ())), precision=PRECISE
    )
    second_grad = jnp.dot(logit_grad, router_weights.astype(F32).T, precision=PRECISE)
    second_grad = second_grad + jnp.sum(route_gates * copy_member, axis=1)[:, None] * out_grad
    const_grad = jnp.einsum("rkc,rk,rd->cd", const_member, route_gates, out_grad, precision=PRECISE)
    second_grad = second_grad + from_owners(back_rows, [picks_both])[0]
    middle_part, second_gain_grad = normalize_back(middle, second_factor, vectors[1], second_grad)
    middle_grad = out_grad + middle_part
    middle_low = middle_grad.astype(LOW)

    flat = (-1, BS, BS)
    expert_stats = [
        item.reshape(flat)
        for item in (
            expert_weights,
            expert_left,
            expert_right,
            expert_left_root,
            expert_right_root,
        )
    ]

    attended_grad = dot(middle_low, w_output, 1, 1).astype(LOW)
    attended_grad = attended_grad.reshape(rows, HEAD_GROUPS, GROUP_WIDTH).transpose(1, 0, 2)
    attended_grad = over_groups(pack_rows(attended_grad))
    if by_panels:
        hop_c, hop_b = tie((hop_c, hop_b, middle_low))[:2]
        given_b = over_b((near_b.astype(F32) + hop_c[part:].astype(F32)).astype(LOW))
        given_c = (near_c.astype(F32) + hop_b[part:].astype(F32)).astype(LOW)
        kept_next = over_c(tie((kept_next, given_c))[0])
        given_c = over_c(given_c)
        early = jnp.concatenate([router_local, second_gain_grad[None], const_grad], axis=0)
        early = direct_sum(early, "f", f_size)
        early = direct_sum(early, ("a", "b"), HEAD_GROUPS)
        attended_grad, given_b, given_c, kept_next, early = tie(
            (attended_grad, given_b, given_c, kept_next, early)
        )
        kept_b = over_b((kept_far.astype(F32) + kept_next.astype(F32)).astype(LOW))
        taken = jnp.concatenate(
            [
                given[:part].astype(F32) + hop_c[:part].astype(F32) + given_b.astype(F32),
                given[part:].astype(F32) + hop_b[:part].astype(F32) + given_c.astype(F32),
            ],
            axis=0,
        )
        taken = shifted(taken.astype(LOW), "a", 2, 1)
        kept_near = over_c(tie((kept_near, attended_grad))[0])
        early = direct_sum(early, "c", c_size)
    back_outs = attend_back(kpb, ends, queries, pairs, attended_grad, raw, lse)
    if by_panels:
        *back_outs, kept_near, taken, early = tie((*back_outs, kept_near, taken, early))
        middle_late = tie((middle_low, back_outs[0]))[0]
        output_panels = jnp.einsum(
            "hrj,rd->hdj", by_heads, middle_late, preferred_element_type=F32
        ).astype(LOW)
        output_panels = over_groups(output_panels)
        expert_outs = shampoo_half(1 - half, [taken], expert_stats, None)
        first_parts = tie((*first_parts, back_outs[0]))[:HEAD_GROUPS]
        first_all = jnp.zeros((HEAD_GROUPS, rows, D), LOW)
        for step, part_rows in enumerate(first_parts):
            first_all = lax.dynamic_update_index_in_dim(
                first_all, part_rows, group_place ^ step, 0
            )
        first_all = first_all.reshape(-1, D)
    query_grad, pair_grad = back_outs[:2]
    for step in range(1, c_size):
        pair_grad = pair_grad + shifted(back_outs[1 + step], "c", c_size, -step).astype(F32)
    group_grad = jnp.concatenate([query_grad, pair_grad.astype(LOW)], axis=2)
    if by_panels:
        group_grad, output_panels, first_all, early, *expert_outs = tie(
            (group_grad, output_panels, first_all, early, *expert_outs)
        )
    if by_panels:
        panels = dot(first_all, group_grad.reshape(-1, 3 * GROUP_WIDTH), 0, 0).astype(LOW)
        group_grad, panels = tie((group_grad, panels))
    project_grad = (
        over_groups(group_grad)
        .reshape(HEAD_GROUPS, rows, 3, GROUP_WIDTH)
        .transpose(1, 2, 0, 3)
        .reshape(rows, 3 * D)
    )
    first_grad = dot(project_grad, w_project, 1, 1)
    input_part, first_gain_grad = normalize_back(inputs, first_factor, vectors[0], first_grad)
    input_grad = middle_grad + input_part

    everywhere = ("a", "b", "c", "f")
    if not by_panels:
        early = jnp.concatenate([router_local, second_gain_grad[None], const_grad], axis=0)
        early = everywhere_sum(early, sizes)
    late = direct_sum(first_gain_grad[None], "f", f_size)
    late = direct_sum(late, "c", c_size)
    late = direct_sum(late, ("a", "b"), a_size * b_size)

    attn_stats = (attn_weights, attn_left, attn_right, attn_left_root, attn_right_root)
    if by_panels:
        panels = panels.reshape(3, D // 3, 3 * GROUP_WIDTH)
        output_panels = jnp.sum(output_panels.astype(F32), axis=0).astype(LOW)
        output_panels = (
            output_panels.reshape(3, D // 3, GROUP_WIDTH)
            .transpose(1, 0, 2)
            .reshape(1, D // 3, 3 * GROUP_WIDTH)
        )
        panels = jnp.concatenate([panels, output_panels], axis=0)
        own_panels = [
            lax.dynamic_index_in_dim(panels, f_place ^ step, 0, False) for step in range(f_size)
        ]
        summed = own_panels[0].astype(F32)
        for step in range(1, f_size):
            summed = summed + crossed(own_panels[step], "f", f_size, step).astype(F32)
        summed = summed.astype(LOW)
        kept = [kept, kept_near, kept_b]
        summed = (summed.astype(F32) + crossed(summed, "c", 2, 1).astype(F32)).astype(LOW)
        group_panels = [
            crossed(summed, ("a", "b"), HEAD_GROUPS, step) for step in range(1, HEAD_GROUPS)
        ]
        kept[0] = tie((kept[0], summed))[0]
        expert_outs = shampoo_half(half, kept, expert_stats, expert_outs)
        late, early, *joined = tie((late, early, *group_panels, *expert_outs))
        group_panels, expert_outs = joined[: HEAD_GROUPS - 1], joined[HEAD_GROUPS - 1 :]
        turn = (f_place == 3).astype(jnp.int32).reshape(1)
        attn_outs = shampoo_panel(
            turn, group_places, [summed, *group_panels], attn_stats
        )
    else:
        output_weight_grad = dot(attended, middle_low, 0, 0)
        project_weight_grad = dot(first_low, project_grad, 0, 0)
        attn_local = jnp.concatenate(
            [to_blocks(project_weight_grad, BS, BS), to_blocks(output_weight_grad, BS, BS)],
            axis=0,
        )
        attn_sum = lax.psum(attn_local, everywhere)
        attn_gradient = lax.dynamic_slice_in_dim(attn_sum, f_place * per_device, per_device, 0)
        block_numbers = f_place * per_device + jnp.arange(per_device, dtype=jnp.int32)
        attn_rates = jnp.where(block_numbers < project_blocks, RATE_PROJECT, RATE_OUTPUT)
        attn_outs = shampoo(attn_rates.astype(F32), attn_gradient, attn_stats)
        expert_gradient = lax.psum_scatter(
            jnp.concatenate(grad_shares, axis=0).reshape(local_slices, -1, BS, BS).astype(F32),
            ("b", "c"),
            scatter_dimension=1,
            tiled=True,
        ).reshape(flat)
        expert_outs = shampoo(
            jnp.full((expert_gradient.shape[0],), RATE_EXPERT, F32), expert_gradient, expert_stats
        )
    expert_grads, expert_left_new, expert_right_new, expert_new = [
        item.reshape(expert_weights.shape) for item in expert_outs
    ]
    attn_grads, attn_left_new, attn_right_new, attn_new = attn_outs
    router_grads = early[:route_count].T
    vector_grads = jnp.concatenate([late, early[route_count:]], axis=0)
    router_left_new, router_right_new, router_moved = shampoo_small(
        to_blocks(router_weights.astype(F32), BS, route_count),
        to_blocks(router_grads, BS, route_count),
        router_left,
        router_right,
        router_left_root,
        router_right_root,
        RATE_ROUTER,
    )
    router_new = to_matrix(router_moved, D, route_count)
    vector_new = vectors - RATE_VECTOR * float(tokens_all) ** (-0.5) * vector_grads
    return (
        output,
        input_grad,
        vector_grads,
        vector_new,
        attn_grads,
        attn_left_new,
        attn_right_new,
        attn_new,
        expert_grads,
        expert_left_new,
        expert_right_new,
        expert_new,
        router_grads,
        router_left_new,
        router_right_new,
        router_new,
    )


def solution(mesh):
    ctx_size = mesh.shape["ctx"]
    f_size = mesh.shape["fsdp"]
    context = ("a", "b", "c")
    token_rows = P(context + ("f",), None)
    group_rows = P("f", None)
    attn = P("f", None, None)
    expert = P("f", context, None, None)
    in_specs = (
        (token_rows, token_rows, P(), group_rows, group_rows, token_rows)
        + (attn,) * 5
        + (expert,) * 5
        + (P(),) * 5
    )
    out_specs = (token_rows, token_rows, P(), P()) + (attn,) * 4 + (expert,) * 4 + (P(),) * 4

    def run(*arrays):
        local_slices = arrays[11].shape[0] // f_size
        a_size = 2 if local_slices == 2 else 1
        b_size = HEAD_GROUPS // a_size
        c_size = ctx_size // HEAD_GROUPS
        sizes = (a_size, b_size, c_size, f_size)
        fine_mesh = jax.sharding.Mesh(mesh.devices.reshape(sizes), ("a", "b", "c", "f"))
        return jax.shard_map(
            functools.partial(body, sizes),
            mesh=fine_mesh,
            in_specs=in_specs,
            out_specs=out_specs,
            check_vma=False,
        )(*arrays)

    return run
```

```python
import functools

import jax
import jax.numpy as jnp
from jax import lax
from jax.experimental import pallas as pl
from jax.experimental.pallas import tpu as pltpu
from jax.sharding import PartitionSpec as P

D = 768
HEADS = 12
HDIM = 64
EXPERTS = 8
ZEROS = 4
BS = 128
SLOTS = 4
HEAD_GROUPS = 4
GROUP_WIDTH = HEADS // HEAD_GROUPS * HDIM
GROUP_HEADS = HEADS // HEAD_GROUPS
CHUNK = 256
TILE = 256
SUB = 32

EPSILON = 1e-06
SCORE_SCALE = 0.125
STAT_DECAY = 0.5
RATE_PROJECT = 0.4
RATE_OUTPUT = 3.0
RATE_EXPERT = 0.4
RATE_ROUTER = 0.2
RATE_VECTOR = 0.1
MASKED_SCORE = -1e30
PRECISE = lax.Precision.HIGHEST
F32 = jnp.float32
LOW = jnp.bfloat16
VMEM_LIMIT = 56 * 1024 * 1024


def to_matrix(blocks, height, breadth):
    block_height = blocks.shape[1]
    block_breadth = blocks.shape[2]
    shaped = blocks.reshape(
        height // block_height, breadth // block_breadth, block_height, block_breadth
    )
    return shaped.transpose(0, 2, 1, 3).reshape(height, breadth)


def to_blocks(matrix, block_height, block_breadth):
    height = matrix.shape[0]
    breadth = matrix.shape[1]
    shaped = matrix.reshape(
        height // block_height, block_height, breadth // block_breadth, block_breadth
    )
    return shaped.transpose(0, 2, 1, 3).reshape(-1, block_height, block_breadth)


def normalize_parts(values, scaling):
    factor = lax.rsqrt(jnp.mean(values * values, axis=-1, keepdims=True) + EPSILON)
    return (values * factor * scaling, factor)


def normalize_back(values, factor, scaling, gradient):
    unit_rows = values * factor
    scaled = gradient * scaling
    value_grad = factor * (
        scaled - unit_rows * jnp.mean(scaled * unit_rows, axis=-1, keepdims=True)
    )
    return (value_grad, jnp.sum(gradient * unit_rows, axis=0))


def dot(left, right, left_dim=1, right_dim=0):
    return lax.dot_general(
        left, right, (((left_dim,), (right_dim,)), ((), ())), preferred_element_type=F32
    )


def vmem_spec():
    return pl.BlockSpec(memory_space=pltpu.VMEM)


def smem_spec():
    return pl.BlockSpec(memory_space=pltpu.SMEM)


def params():
    return pltpu.CompilerParams(vmem_limit_bytes=VMEM_LIMIT)


def project_kernel(rows_in, gain, places, shards):
    rows = rows_in.shape[0]
    owners = len(shards) - 1
    depth = D // owners
    breadth = 3 * D
    block_rows = depth // BS
    block_columns = breadth // BS
    pair = 2 * GROUP_WIDTH

    def kernel(places_ref, rows_ref, gain_ref, *refs):
        shard_refs = refs[: owners + 1]
        first_out, factor_out, query_out, pair_out, matrix, first_s = refs[owners + 1 :]
        for number, shard in enumerate(shard_refs):
            owner = places_ref[number]

            @pl.when(owner < owners)
            def _(owner=owner, shard=shard):
                for row in range(block_rows):
                    for column in range(block_columns):
                        matrix[
                            owner, row * BS : (row + 1) * BS, column * BS : (column + 1) * BS
                        ] = shard[row * block_columns + column]

        def norm(tile, carry):
            at = pl.ds(pl.multiple_of(tile * SUB, SUB), SUB)
            values = rows_ref[at, :]
            factor = lax.rsqrt(jnp.mean(values * values, axis=1, keepdims=True) + EPSILON)
            first = (values * factor * gain_ref[...]).astype(LOW)
            factor_out[at, :] = factor
            first_out[at, :] = first
            for owner in range(owners):
                first_s[owner, at, :] = first[:, owner * depth : (owner + 1) * depth]
            return carry

        lax.fori_loop(0, rows // SUB, norm, 0)
        for tile in range(breadth // pair):
            at = slice(tile * pair, (tile + 1) * pair)
            total = dot(first_s[0], matrix[0, :, at])
            for owner in range(1, owners):
                total = total + dot(first_s[owner], matrix[owner, :, at])
            total = total.astype(LOW)
            part = tile * pair // D
            group = tile * pair % D // GROUP_WIDTH
            for side in range(2):
                piece = total[:, side * GROUP_WIDTH : (side + 1) * GROUP_WIDTH]
                if part == 0:
                    query_out[group + side] = jnp.concatenate(
                        [piece[: rows // 2], piece[rows // 2 :]], axis=1
                    )
                else:
                    pair_out[
                        group + side, :, (part - 1) * GROUP_WIDTH : part * GROUP_WIDTH
                    ] = piece

    return pl.pallas_call(
        kernel,
        in_specs=[smem_spec()] + [vmem_spec()] * (owners + 3),
        out_specs=[vmem_spec()] * 5,
        out_shape=[
            jax.ShapeDtypeStruct((rows, D), LOW),
            jax.ShapeDtypeStruct((rows, 1), F32),
            jax.ShapeDtypeStruct((HEAD_GROUPS, rows // 2, pair), LOW),
            jax.ShapeDtypeStruct((HEAD_GROUPS, rows, pair), LOW),
            jax.ShapeDtypeStruct((owners, depth, breadth), LOW),
        ],
        scratch_shapes=[pltpu.VMEM((owners, rows, depth), LOW)],
        compiler_params=params(),
        cost_estimate=pl.CostEstimate(
            flops=2 * rows * D, bytes_accessed=1_000_000, transcendentals=0
        ),
        name="project",
    )(places, rows_in, gain, *shards)


def head_masks(value):
    lane = lax.broadcasted_iota(jnp.int32, (1, GROUP_WIDTH), 1)
    return [
        jnp.where(lane // HDIM == head, value, 0.0).astype(F32) for head in range(GROUP_HEADS)
    ]


def stack_heads(rows, masks):
    return jnp.concatenate([rows * mask.astype(rows.dtype) for mask in masks], axis=0)


def packed_at(slot, block_rows):
    first_row = slot % 2 * block_rows
    first_lane = slot // 2 * GROUP_WIDTH
    return slice(first_row, first_row + block_rows), slice(first_lane, first_lane + GROUP_WIDTH)


def pack_rows(values):
    groups, rows, width = values.shape
    return values.reshape(groups, 2, rows // 2, width).transpose(0, 2, 1, 3).reshape(
        groups, rows // 2, 2 * width
    )


def unpack_rows(values):
    groups, rows, width = values.shape
    return values.reshape(groups, rows, 2, width // 2).transpose(0, 2, 1, 3).reshape(
        groups, 2 * rows, width // 2
    )


def fill_sorted(kpb, sources, key_sorted, value_sorted, block_rows, block_count):
    key_sorted[0:CHUNK, :] = jnp.zeros((CHUNK, GROUP_WIDTH), LOW)
    value_sorted[0:CHUNK, :] = jnp.zeros((CHUNK, GROUP_WIDTH), LOW)
    for number, source in enumerate(sources):

        def fill(item, carry, source=source, number=number):
            from_row = pl.multiple_of(item % SLOTS * block_rows, block_rows)
            to_row = pl.multiple_of(CHUNK + kpb[number, item] * block_rows, 32)
            rows = source[item // SLOTS, pl.ds(from_row, block_rows), :]
            key_sorted[pl.ds(to_row, block_rows), :] = rows[:, 0:GROUP_WIDTH]
            value_sorted[pl.ds(to_row, block_rows), :] = rows[:, GROUP_WIDTH:]
            return carry

        lax.fori_loop(0, block_count, fill, 0)


def list_steps(kpb, ends, sequences, block_rows, block_count, block_of, place_of):
    def one_block(item, first_step):
        first = kpb[0, item] * block_rows
        lowest = jnp.int32(0)
        for sequence in range(sequences):
            ending = ends[sequence]
            lowest = jnp.where(first >= ending, ending, lowest)
        top = first + block_rows
        count = (top - lowest + CHUNK - 1) // CHUNK

        def one_step(step, carry):
            block_of[first_step + step] = item
            place_of[first_step + step] = top - (step + 1) * CHUNK
            return carry

        lax.fori_loop(0, count, one_step, 0)
        return first_step + count

    return lax.fori_loop(0, block_count, one_block, jnp.int32(0))


def fill_limits(kpb, ends, sequences, block_rows, item, start_s, place_s):
    for tile in range(GROUP_HEADS * block_rows // SUB):
        within = tile * SUB % block_rows
        places = (
            kpb[0, item] * block_rows
            + within
            + lax.broadcasted_iota(jnp.int32, (SUB, BS), 0)
        )
        starts = jnp.zeros_like(places)
        for sequence in range(sequences):
            ending = ends[sequence]
            starts = jnp.where(places >= ending, ending, starts)
        at_rows = slice(tile * SUB, (tile + 1) * SUB)
        start_s[item, at_rows, :] = starts
        place_s[item, at_rows, :] = places


def pipeline(total, scores, middle, products):
    scores(jnp.int32(0), 0)

    def pair(number, carry):
        step = 2 * number
        scores(step + 1, 1)
        middle(step, 0)
        products(step - 1, 1)
        scores(step + 2, 0)
        middle(step + 1, 1)
        products(step, 0)
        return carry

    lax.fori_loop(0, (total + 2) // 2, pair, 0)


def tile_slices(count):
    return [slice(tile * SUB, (tile + 1) * SUB) for tile in range(count)]


def attend_kernel(sources_count, block_rows, sequences, *refs):
    kpb, ends, queries = refs[:3]
    sources = refs[3 : 3 + sources_count]
    raw_out, low_out, lse_out, key_sorted, value_sorted, query_s, start_s, place_s = refs[
        3 + sources_count : 11 + sources_count
    ]
    best_s, total_s, gathered_s, score_0, score_1, weight_0, weight_1, fade_0, fade_1 = refs[
        11 + sources_count : 20 + sources_count
    ]
    block_of, place_of = refs[20 + sources_count :]
    score_s, weight_s, fade_s = (score_0, score_1), (weight_0, weight_1), (fade_0, fade_1)
    block_count = queries.shape[0] * SLOTS
    stacked = GROUP_HEADS * block_rows
    tiles = tile_slices(stacked // SUB)
    fill_sorted(kpb, sources, key_sorted, value_sorted, block_rows, block_count)
    total = list_steps(kpb, ends, sequences, block_rows, block_count, block_of, place_of)
    masks = head_masks(SCORE_SCALE)
    plain = head_masks(1.0)

    def load(group, carry):
        for slot in range(SLOTS):
            rows, lanes = packed_at(slot, block_rows)
            query_s[group * SLOTS + slot] = stack_heads(queries[group, rows, lanes], masks)
        return carry

    lax.fori_loop(0, block_count // SLOTS, load, 0)

    def prepare(item, carry):
        fill_limits(kpb, ends, sequences, block_rows, item, start_s, place_s)
        best_s[item] = jnp.full((stacked, BS), MASKED_SCORE, F32)
        total_s[item] = jnp.zeros((stacked, BS), F32)
        gathered_s[item] = jnp.zeros((stacked, GROUP_WIDTH), F32)
        return carry

    lax.fori_loop(0, block_count, prepare, 0)
    weight_1[...] = jnp.zeros_like(weight_1)
    fade_1[...] = jnp.ones_like(fade_1)

    def find(step):
        inside = jnp.clip(step, 0, total - 1)
        return block_of[inside], place_of[inside]

    def scores(step, side):
        item, low_place = find(step)
        at = pl.multiple_of(low_place + CHUNK, 32)
        score_s[side][...] = dot(query_s[item], key_sorted[pl.ds(at, CHUNK), :], 1, 1)

    def middle(step, side):
        item, low_place = find(step)
        low_place = jnp.where(step < total, low_place, -(1 << 24))
        lanes = low_place + lax.broadcasted_iota(jnp.int32, (1, BS), 1)
        for rows in tiles:
            starts, places = start_s[item, rows, :], place_s[item, rows, :]
            parts = []
            for part in range(CHUNK // BS):
                key_places = lanes + part * BS
                allowed = (key_places >= starts) & (key_places <= places)
                found = score_s[side][rows, part * BS : (part + 1) * BS]
                parts.append(jnp.where(allowed, found, MASKED_SCORE))
            best = best_s[item, rows, :]
            top = jnp.max(functools.reduce(jnp.maximum, parts), axis=1, keepdims=True)
            peak = jnp.maximum(best, top)
            fade = jnp.exp(best - peak)
            so_far = total_s[item, rows, :] * fade
            for part, found in enumerate(parts):
                weights = jnp.exp(found - peak)
                so_far = so_far + weights
                weight_s[side][rows, part * BS : (part + 1) * BS] = weights.astype(LOW)
            best_s[item, rows, :] = peak
            total_s[item, rows, :] = so_far
            fade_s[side][rows, :] = fade

    def products(step, side):
        item, low_place = find(step)
        at = pl.multiple_of(low_place + CHUNK, 32)
        fade = fade_s[side][...]
        fade = jnp.concatenate([fade, fade[:, : GROUP_WIDTH - BS]], axis=1)
        gathered_s[item] = gathered_s[item] * fade + dot(
            weight_s[side][...], value_sorted[pl.ds(at, CHUNK), :]
        )

    pipeline(total, scores, middle, products)

    def finish(group, carry):
        for slot in range(SLOTS):
            item = group * SLOTS + slot
            rows, lanes = packed_at(slot, block_rows)
            sums = jnp.sum(total_s[item], axis=1, keepdims=True)
            gathered = gathered_s[item] / sums
            result = jnp.zeros((block_rows, GROUP_WIDTH), F32)
            for head in range(GROUP_HEADS):
                result = result + (
                    plain[head] * gathered[head * block_rows : (head + 1) * block_rows]
                )
            raw_out[group, slot * block_rows : (slot + 1) * block_rows, :] = result
            low_out[group, rows, lanes] = result.astype(LOW)
            lse_out[item] = best_s[item][:, 0:1] + jnp.log(sums)
        return carry

    lax.fori_loop(0, block_count // SLOTS, finish, 0)


def attend_sizes(queries, pairs):
    groups, rows, _ = pairs[0].shape
    block_rows = rows // SLOTS
    all_rows = groups * rows * len(pairs)
    blocks = groups * SLOTS
    stacked = GROUP_HEADS * block_rows
    return groups, rows, block_rows, all_rows, blocks, stacked


def attend(kpb, ends, queries, pairs):
    groups, rows, block_rows, all_rows, blocks, stacked = attend_sizes(queries, pairs)
    steps = blocks * (all_rows // CHUNK + 1)
    return pl.pallas_call(
        functools.partial(attend_kernel, len(pairs), block_rows, ends.shape[0]),
        in_specs=[smem_spec()] * 2 + [vmem_spec()] * (1 + len(pairs)),
        out_specs=[vmem_spec()] * 3,
        out_shape=[
            jax.ShapeDtypeStruct((groups, rows, GROUP_WIDTH), F32),
            jax.ShapeDtypeStruct((groups, rows // 2, 2 * GROUP_WIDTH), LOW),
            jax.ShapeDtypeStruct((blocks, stacked, 1), F32),
        ],
        scratch_shapes=[
            pltpu.VMEM((CHUNK + all_rows, GROUP_WIDTH), LOW),
            pltpu.VMEM((CHUNK + all_rows, GROUP_WIDTH), LOW),
            pltpu.VMEM((blocks, stacked, GROUP_WIDTH), LOW),
            pltpu.VMEM((blocks, stacked, BS), jnp.int32),
            pltpu.VMEM((blocks, stacked, BS), jnp.int32),
            pltpu.VMEM((blocks, stacked, BS), F32),
            pltpu.VMEM((blocks, stacked, BS), F32),
            pltpu.VMEM((blocks, stacked, GROUP_WIDTH), F32),
            pltpu.VMEM((stacked, CHUNK), F32),
            pltpu.VMEM((stacked, CHUNK), F32),
            pltpu.VMEM((stacked, CHUNK), LOW),
            pltpu.VMEM((stacked, CHUNK), LOW),
            pltpu.VMEM((stacked, BS), F32),
            pltpu.VMEM((stacked, BS), F32),
            pltpu.SMEM((steps,), jnp.int32),
            pltpu.SMEM((steps,), jnp.int32),
        ],
        compiler_params=params(),
        cost_estimate=pl.CostEstimate(
            flops=groups * rows * HDIM,
            bytes_accessed=1_000_000,
            transcendentals=0,
        ),
        name="attend_forward",
    )(kpb, ends, queries, *pairs)


def attend_back_kernel(sources_count, block_rows, sequences, *refs):
    kpb, ends, queries = refs[:3]
    sources = refs[3 : 3 + sources_count]
    out_grad, raw, lse = refs[3 + sources_count : 6 + sources_count]
    query_out = refs[6 + sources_count]
    pair_outs = refs[7 + sources_count : 7 + 2 * sources_count]
    rest = refs[7 + 2 * sources_count :]
    key_sorted, value_sorted, key_grad, value_grad, query_s, grad_s, query_grad = rest[:7]
    start_s, place_s, shift_s, delta_s = rest[7:11]
    score_s, back_s, weight_s, change_s = rest[11:13], rest[13:15], rest[15:17], rest[17:19]
    block_of, place_of = rest[19:]
    block_count = queries.shape[0] * SLOTS
    stacked = GROUP_HEADS * block_rows
    tiles = tile_slices(stacked // SUB)
    fill_sorted(kpb, sources, key_sorted, value_sorted, block_rows, block_count)
    total = list_steps(kpb, ends, sequences, block_rows, block_count, block_of, place_of)
    key_grad[...] = jnp.zeros_like(key_grad)
    value_grad[...] = jnp.zeros_like(value_grad)
    weight_s[1][...] = jnp.zeros_like(weight_s[1])
    change_s[1][...] = jnp.zeros_like(change_s[1])
    masks = head_masks(SCORE_SCALE)
    plain = head_masks(1.0)

    def load(group, carry):
        for slot in range(SLOTS):
            item = group * SLOTS + slot
            rows, lanes = packed_at(slot, block_rows)
            query_s[item] = stack_heads(queries[group, rows, lanes], masks)
            grad = stack_heads(out_grad[group, rows, lanes], plain)
            grad_s[item] = grad
            values = raw[group, slot * block_rows : (slot + 1) * block_rows, :]
            delta = jnp.sum(
                grad.astype(F32) * jnp.concatenate([values] * GROUP_HEADS, axis=0),
                axis=1,
                keepdims=True,
            )
            delta_s[item] = jnp.broadcast_to(delta, (stacked, BS))
        return carry

    lax.fori_loop(0, block_count // SLOTS, load, 0)

    def prepare(item, carry):
        shift_s[item] = jnp.broadcast_to(lse[item], (stacked, BS))
        query_grad[item] = jnp.zeros((stacked, GROUP_WIDTH), F32)
        fill_limits(kpb, ends, sequences, block_rows, item, start_s, place_s)
        return carry

    lax.fori_loop(0, block_count, prepare, 0)

    def find(step):
        inside = jnp.clip(step, 0, total - 1)
        return block_of[inside], place_of[inside]

    def scores(step, side):
        item, low_place = find(step)
        at = pl.ds(pl.multiple_of(low_place + CHUNK, 32), CHUNK)
        score_s[side][...] = dot(query_s[item], key_sorted[at, :], 1, 1)
        back_s[side][...] = dot(grad_s[item], value_sorted[at, :], 1, 1)

    def middle(step, side):
        item, low_place = find(step)
        low_place = jnp.where(step < total, low_place, -(1 << 24))
        lanes = low_place + lax.broadcasted_iota(jnp.int32, (1, BS), 1)
        for rows in tiles:
            starts, places = start_s[item, rows, :], place_s[item, rows, :]
            shift, delta = shift_s[item, rows, :], delta_s[item, rows, :]
            for part in range(CHUNK // BS):
                at_lanes = slice(part * BS, (part + 1) * BS)
                key_places = lanes + part * BS
                allowed = (key_places >= starts) & (key_places <= places)
                found = score_s[side][rows, at_lanes] - shift
                weights = jnp.exp(jnp.where(allowed, found, MASKED_SCORE))
                weight_s[side][rows, at_lanes] = weights.astype(LOW)
                change = weights * (back_s[side][rows, at_lanes] - delta)
                change_s[side][rows, at_lanes] = change.astype(LOW)

    def products(step, side):
        item, low_place = find(step)
        at = pl.ds(pl.multiple_of(low_place + CHUNK, 32), CHUNK)
        value_grad[at, :] += dot(weight_s[side][...], grad_s[item], 0, 0)
        key_grad[at, :] += dot(change_s[side][...], query_s[item], 0, 0)
        query_grad[item] += dot(change_s[side][...], key_sorted[at, :])

    pipeline(total, scores, middle, products)

    def finish(item, carry):
        at = pl.ds(pl.multiple_of(item % SLOTS * block_rows, block_rows), block_rows)
        result = jnp.zeros((block_rows, GROUP_WIDTH), F32)
        for head in range(GROUP_HEADS):
            result = result + masks[head] * (
                query_grad[item, head * block_rows : (head + 1) * block_rows, :]
            )
        query_out[item // SLOTS, at, :] = result.astype(LOW)
        return carry

    lax.fori_loop(0, block_count, finish, 0)
    for number, target in enumerate(pair_outs):

        def drain(item, carry, number=number, target=target):
            to_row = pl.multiple_of(item % SLOTS * block_rows, block_rows)
            from_row = pl.multiple_of(CHUNK + kpb[number, item] * block_rows, 32)
            pair = jnp.concatenate(
                [
                    key_grad[pl.ds(from_row, block_rows), :],
                    value_grad[pl.ds(from_row, block_rows), :],
                ],
                axis=1,
            )
            target[item // SLOTS, pl.ds(to_row, block_rows), :] = pair.astype(target.dtype)
            return carry

        lax.fori_loop(0, block_count, drain, 0)


def attend_back(kpb, ends, queries, pairs, out_grad, raw, lse):
    groups, rows, block_rows, all_rows, blocks, stacked = attend_sizes(queries, pairs)
    steps = blocks * (all_rows // CHUNK + 1)
    limit = pltpu.VMEM((blocks, stacked, BS), jnp.int32)
    row_values = pltpu.VMEM((blocks, stacked, BS), F32)
    sorted_low = pltpu.VMEM((CHUNK + all_rows, GROUP_WIDTH), LOW)
    sorted_sum = pltpu.VMEM((CHUNK + all_rows, GROUP_WIDTH), F32)
    stacked_low = pltpu.VMEM((blocks, stacked, GROUP_WIDTH), LOW)
    square = pltpu.VMEM((stacked, CHUNK), F32)
    square_low = pltpu.VMEM((stacked, CHUNK), LOW)
    return pl.pallas_call(
        functools.partial(attend_back_kernel, len(pairs), block_rows, ends.shape[0]),
        in_specs=[smem_spec()] * 2 + [vmem_spec()] * (4 + len(pairs)),
        out_specs=[vmem_spec()] * (1 + len(pairs)),
        out_shape=[
            jax.ShapeDtypeStruct((groups, rows, GROUP_WIDTH), LOW),
            jax.ShapeDtypeStruct((groups, rows, 2 * GROUP_WIDTH), F32),
        ]
        + [jax.ShapeDtypeStruct((groups, rows, 2 * GROUP_WIDTH), LOW) for _ in pairs[1:]],
        scratch_shapes=[sorted_low] * 2
        + [sorted_sum] * 2
        + [stacked_low] * 2
        + [pltpu.VMEM((blocks, stacked, GROUP_WIDTH), F32)]
        + [limit] * 2
        + [row_values] * 2
        + [square] * 4
        + [square_low] * 4
        + [pltpu.SMEM((steps,), jnp.int32)] * 2,
        compiler_params=params(),
        cost_estimate=pl.CostEstimate(
            flops=groups * rows * HDIM,
            bytes_accessed=1_000_000,
            transcendentals=0,
        ),
        name="attend_backward",
    )(kpb, ends, queries, *pairs, out_grad, raw, lse)


def side_blocks():
    return D // BS


def bring(places, sources, held, done):
    copies = []
    for number, source in enumerate(sources):
        size = source.shape[0]
        target = held.at[pl.ds(places[number] * size, size)]
        copies.append(pltpu.make_async_copy(source, target, done.at[number]))
    for copy in copies:
        copy.start()
    for copy in copies:
        copy.wait()


def wide_tile(held, first, hidden_blocks, step):
    rows = []
    for row in range(side_blocks()):
        at = first + row * hidden_blocks + 2 * step
        rows.append(jnp.concatenate([held[at], held[at + 1]], axis=1))
    return jnp.concatenate(rows, axis=0)


def tall_tile(held, first, step):
    side = side_blocks()
    rows = []
    for half in range(2):
        at = first + (2 * step + half) * side
        rows.append(jnp.concatenate([held[at + column] for column in range(side)], axis=1))
    return jnp.concatenate(rows, axis=0)


def expert_sizes(weights):
    total = sum(array.shape[0] for array in weights[1])
    return total, total // (3 * side_blocks())


def expert_forward(rows_in, weights):
    rows = rows_in.shape[0]
    places, sources = weights
    count = len(sources)
    total_blocks, hidden_blocks = expert_sizes(weights)
    up_first = side_blocks() * hidden_blocks

    def kernel(places_ref, rows_ref, *refs):
        source_refs = refs[:count]
        result, gate_o, up_o, inner_o, total, held, done = refs[count:]
        step = pl.program_id(0)

        @pl.when(step == 0)
        def _():
            bring(places_ref, source_refs, held, done)
            total[...] = jnp.zeros_like(total)

        gate_tile = wide_tile(held, 0, hidden_blocks, step)
        up_tile = wide_tile(held, up_first, hidden_blocks, step)
        down_tile = tall_tile(held, 2 * up_first, step)

        for number in range(rows // TILE):
            first = number * TILE
            at = pl.ds(first, TILE)
            entering = rows_ref[at, :]
            gate_o[at, :] = dot(entering, gate_tile)
            up_o[at, :] = dot(entering, up_tile)
            for sub in range(TILE // SUB):
                now = pl.ds(first + sub * SUB, SUB)
                gate = gate_o[now, :]
                inner_o[now, :] = (gate * jax.nn.sigmoid(gate) * up_o[now, :]).astype(LOW)
            total[at, :] += dot(inner_o[at, :], down_tile)

        @pl.when(step == pl.num_programs(0) - 1)
        def _():
            result[...] = total[...].astype(LOW)

    fixed = pl.BlockSpec((rows, D), lambda step: (0, 0))
    hidden = pl.BlockSpec((rows, TILE), lambda step: (0, step))
    hidden_size = (rows, hidden_blocks * BS)
    return pl.pallas_call(
        kernel,
        grid=(hidden_blocks // 2,),
        in_specs=[smem_spec(), fixed] + [pl.BlockSpec(memory_space=pl.ANY)] * count,
        out_specs=[fixed] + [hidden] * 3,
        out_shape=[
            jax.ShapeDtypeStruct((rows, D), LOW),
            jax.ShapeDtypeStruct(hidden_size, F32),
            jax.ShapeDtypeStruct(hidden_size, F32),
            jax.ShapeDtypeStruct(hidden_size, LOW),
        ],
        scratch_shapes=[
            pltpu.VMEM((rows, D), F32),
            pltpu.VMEM((total_blocks, BS, BS), LOW),
            pltpu.SemaphoreType.DMA((count,)),
        ],
        compiler_params=params(),
        cost_estimate=pl.CostEstimate(
            flops=6 * rows * D * hidden_blocks * BS,
            bytes_accessed=6 * D * hidden_blocks * BS + 4 * rows * D,
            transcendentals=0,
        ),
        name="expert_forward",
    )(places, rows_in, *sources)


def expert_row_grads(grads_in, gate_in, up_in, weights):
    rows = grads_in.shape[0]
    places, sources = weights
    count = len(sources)
    total_blocks, hidden_blocks = expert_sizes(weights)
    up_first = side_blocks() * hidden_blocks

    def kernel(places_ref, grads_ref, gate_i, up_i, *refs):
        source_refs = refs[:count]
        back, gate_s, up_s, total, inner_grad_s, held, done = refs[count:]
        step = pl.program_id(0)

        @pl.when(step == 0)
        def _():
            bring(places_ref, source_refs, held, done)
            total[...] = jnp.zeros_like(total)

        gate_tile = wide_tile(held, 0, hidden_blocks, step)
        up_tile = wide_tile(held, up_first, hidden_blocks, step)
        down_tile = tall_tile(held, 2 * up_first, step)

        for number in range(rows // TILE):
            first = number * TILE
            at = pl.ds(first, TILE)
            inner_grad_s[at, :] = dot(grads_ref[at, :], down_tile, 1, 1)
            for sub in range(TILE // SUB):
                now = pl.ds(first + sub * SUB, SUB)
                gate = gate_i[now, :]
                inner_grad = inner_grad_s[now, :]
                sigmoid = jax.nn.sigmoid(gate)
                up_s[now, :] = (inner_grad * (gate * sigmoid)).astype(LOW)
                gate_s[now, :] = (
                    inner_grad * up_i[now, :] * (sigmoid * (1.0 + gate * (1.0 - sigmoid)))
                ).astype(LOW)
            total[at, :] += dot(gate_s[at, :], gate_tile, 1, 1) + dot(
                up_s[at, :], up_tile, 1, 1
            )

        @pl.when(step == pl.num_programs(0) - 1)
        def _():
            back[...] = total[...].astype(LOW)

    fixed = pl.BlockSpec((rows, D), lambda step: (0, 0))
    hidden = pl.BlockSpec((rows, TILE), lambda step: (0, step))
    hidden_shape = jax.ShapeDtypeStruct((rows, hidden_blocks * BS), LOW)
    return pl.pallas_call(
        kernel,
        grid=(hidden_blocks // 2,),
        in_specs=[smem_spec(), fixed, hidden, hidden]
        + [pl.BlockSpec(memory_space=pl.ANY)] * count,
        out_specs=[fixed] + [hidden] * 2,
        out_shape=[jax.ShapeDtypeStruct((rows, D), LOW)] + [hidden_shape] * 2,
        scratch_shapes=[
            pltpu.VMEM((rows, D), F32),
            pltpu.VMEM((rows, TILE), F32),
            pltpu.VMEM((total_blocks, BS, BS), LOW),
            pltpu.SemaphoreType.DMA((count,)),
        ],
        compiler_params=params(),
        cost_estimate=pl.CostEstimate(
            flops=6 * rows * D * hidden_blocks * BS,
            bytes_accessed=12 * D * hidden_blocks * BS + 6 * rows * D,
            transcendentals=0,
        ),
        name="expert_row_grads",
    )(places, grads_in, gate_in, up_in, *sources)


def expert_weight_grads(places, rows_in, grads_in, gate_grads, up_grads, inner, sizes):
    rows = rows_in.shape[0]
    hidden_blocks = gate_grads.shape[1] // BS
    side = side_blocks()
    total_blocks = 3 * side * hidden_blocks
    count = len(sizes)
    pieces = sum(len(group) for group in sizes)

    def kernel(places_ref, rows_ref, grads_ref, gate_s, up_s, inner_s, *refs):
        outs = refs[:count]
        turned, held, done = refs[count:]
        step = pl.program_id(0)

        @pl.when(step == 0)
        def _():
            turned[...] = rows_ref[...].T

        def wide_out(source, first):
            product = dot(turned[...], source[...]).astype(LOW)
            for row in range(side):
                for column in range(2):
                    held[first + row * hidden_blocks + 2 * step + column] = product[
                        row * BS : (row + 1) * BS, column * BS : (column + 1) * BS
                    ]

        wide_out(gate_s, 0)
        wide_out(up_s, side * hidden_blocks)
        product = dot(inner_s[...], grads_ref[...], 0, 0).astype(LOW)
        for half in range(2):
            for column in range(side):
                held[2 * side * hidden_blocks + (2 * step + half) * side + column] = product[
                    half * BS : (half + 1) * BS, column * BS : (column + 1) * BS
                ]

        @pl.when(step == pl.num_programs(0) - 1)
        def _():
            copies = []
            for target, group in zip(outs, sizes):
                first = 0
                for size in group:
                    number = len(copies)
                    source = held.at[pl.ds(places_ref[number] * size, size)]
                    into = target.at[pl.ds(first, size)]
                    copies.append(pltpu.make_async_copy(source, into, done.at[number]))
                    first += size
            for copy in copies:
                copy.start()
            for copy in copies:
                copy.wait()

    fixed = pl.BlockSpec((rows, D), lambda step: (0, 0))
    hidden = pl.BlockSpec((rows, TILE), lambda step: (0, step))
    return pl.pallas_call(
        kernel,
        grid=(hidden_blocks // 2,),
        in_specs=[smem_spec(), fixed, fixed] + [hidden] * 3,
        out_specs=[pl.BlockSpec(memory_space=pl.ANY)] * count,
        out_shape=[jax.ShapeDtypeStruct((sum(group), BS, BS), LOW) for group in sizes],
        scratch_shapes=[
            pltpu.VMEM((D, rows), LOW),
            pltpu.VMEM((total_blocks, BS, BS), LOW),
            pltpu.SemaphoreType.DMA((pieces,)),
        ],
        compiler_params=params(),
        cost_estimate=pl.CostEstimate(
            flops=6 * rows * D * hidden_blocks * BS,
            bytes_accessed=12 * D * hidden_blocks * BS + 6 * rows * D,
            transcendentals=0,
        ),
        name="expert_weight_grads",
    )(places, rows_in, grads_in, gate_grads, up_grads, inner)


def expert_half_grads(which, places, rows_in, grads_in, gate_grads, up_grads, inner, sizes):
    rows = rows_in.shape[0]
    hidden_blocks = gate_grads.shape[1] // BS
    side = side_blocks()
    middle_row = side // 2
    total_blocks = 3 * side * hidden_blocks // 2
    count = len(sizes)
    pieces = sum(len(group) for group in sizes)

    def kernel(which_ref, places_ref, rows_ref, grads_ref, gate_s, up_s, inner_s, *refs):
        outs = refs[:count]
        turned, held, done = refs[count:]
        step = pl.program_id(0)

        @pl.when(step == 0)
        def _():
            turned[...] = rows_ref[...].T

        def wide_out(source, first_row, last_row, first):
            product = dot(turned[first_row * BS : last_row * BS, :], source[...]).astype(LOW)
            for row in range(last_row - first_row):
                for column in range(2):
                    held[first + row * hidden_blocks + 2 * step + column] = product[
                        row * BS : (row + 1) * BS, column * BS : (column + 1) * BS
                    ]

        @pl.when(which_ref[0] == 0)
        def _():
            wide_out(gate_s, 0, side, 0)
            wide_out(up_s, 0, middle_row, side * hidden_blocks)

        @pl.when(which_ref[0] == 1)
        def _():
            wide_out(up_s, middle_row, side, 0)
            product = dot(inner_s[...], grads_ref[...], 0, 0).astype(LOW)
            for half in range(2):
                for column in range(side):
                    held[middle_row * hidden_blocks + (2 * step + half) * side + column] = product[
                        half * BS : (half + 1) * BS, column * BS : (column + 1) * BS
                    ]

        @pl.when(step == pl.num_programs(0) - 1)
        def _():
            copies = []
            for target, group in zip(outs, sizes):
                first = 0
                for size in group:
                    number = len(copies)
                    source = held.at[pl.ds(places_ref[number] * size, size)]
                    into = target.at[pl.ds(first, size)]
                    copies.append(pltpu.make_async_copy(source, into, done.at[number]))
                    first += size
            for copy in copies:
                copy.start()
            for copy in copies:
                copy.wait()

    fixed = pl.BlockSpec((rows, D), lambda step: (0, 0))
    hidden = pl.BlockSpec((rows, TILE), lambda step: (0, step))
    return pl.pallas_call(
        kernel,
        grid=(hidden_blocks // 2,),
        in_specs=[smem_spec(), smem_spec(), fixed, fixed] + [hidden] * 3,
        out_specs=[pl.BlockSpec(memory_space=pl.ANY)] * count,
        out_shape=[jax.ShapeDtypeStruct((sum(group), BS, BS), LOW) for group in sizes],
        scratch_shapes=[
            pltpu.VMEM((D, rows), LOW),
            pltpu.VMEM((total_blocks, BS, BS), LOW),
            pltpu.SemaphoreType.DMA((pieces,)),
        ],
        compiler_params=params(),
        cost_estimate=pl.CostEstimate(
            flops=3 * rows * D * hidden_blocks * BS,
            bytes_accessed=6 * D * hidden_blocks * BS + 6 * rows * D,
            transcendentals=0,
        ),
        name="expert_half_grads",
    )(which, places, rows_in, grads_in, gate_grads, up_grads, inner)


def split_low(values):
    high = values.astype(LOW)
    return high, (values - high.astype(F32)).astype(LOW)


def renew(gradient, weights, left, right, left_root, right_root, rate):
    short = gradient.astype(LOW)
    left_new = STAT_DECAY * left + (1.0 - STAT_DECAY) * dot(short, short, 1, 1)
    right_new = STAT_DECAY * right + (1.0 - STAT_DECAY) * dot(short, short, 0, 0)
    high, rest = split_low(right_root)
    turned = (dot(short, high) + dot(short, rest)).astype(LOW)
    high, rest = split_low(left_root)
    direction = dot(high, turned) + dot(rest, turned)
    return (gradient, left_new, right_new, weights.astype(F32) - rate * direction)


def block_width(count):
    return 4 if count % 4 == 0 else 3 if count % 3 == 0 else 1


def shampoo_half(half, gradients, stats, filled):
    parts = len(gradients)
    count = gradients[0].shape[0]
    width = block_width(count)
    steps = count // width
    spec = pl.BlockSpec((width, BS, BS), lambda step, half: (half[0] * steps + step, 0, 0))
    grad_spec = pl.BlockSpec((width, BS, BS), lambda step, half: (step, 0, 0))

    def kernel(half_ref, *refs):
        for number in range(width):
            total = refs[0][number].astype(F32)
            for ref in refs[1:parts]:
                total = total + ref[number].astype(F32)
            now = [ref[number] for ref in refs[parts : parts + 5]]
            results = renew(total, *now, RATE_EXPERT)
            for target, result in zip(refs[-4:], results):
                target[number] = result

    shape = jax.ShapeDtypeStruct(stats[0].shape, F32)
    extra = list(filled or ())
    return pl.pallas_call(
        kernel,
        grid_spec=pltpu.PrefetchScalarGridSpec(
            num_scalar_prefetch=1,
            grid=(steps,),
            in_specs=[grad_spec] * parts
            + [spec] * 5
            + [pl.BlockSpec(memory_space=pl.ANY)] * len(extra),
            out_specs=[spec] * 4,
        ),
        out_shape=[shape] * 4,
        input_output_aliases={6 + parts + number: number for number in range(len(extra))},
        compiler_params=params(),
        cost_estimate=pl.CostEstimate(
            flops=count * 24 * BS * BS * BS,
            bytes_accessed=count * BS * BS * (34 + 2 * parts),
            transcendentals=0,
        ),
        name="shampoo_half",
    )(half, *gradients, *stats, *extra)


def shampoo(rates, gradient, stats):
    count = gradient.shape[0]
    width = block_width(count)
    spec = pl.BlockSpec((width, BS, BS), lambda step: (step, 0, 0))
    shape = jax.ShapeDtypeStruct((count, BS, BS), F32)

    def kernel(rates_ref, *refs):
        step = pl.program_id(0)
        for number in range(width):
            gradient_now, *stats_now = [ref[number] for ref in refs[:6]]
            results = renew(
                gradient_now.astype(F32), *stats_now, rates_ref[step * width + number]
            )
            for target, result in zip(refs[6:], results):
                target[number] = result

    return pl.pallas_call(
        kernel,
        grid=(count // width,),
        in_specs=[smem_spec()] + [spec] * 6,
        out_specs=[spec] * 4,
        out_shape=[shape] * 4,
        compiler_params=params(),
        cost_estimate=pl.CostEstimate(
            flops=count * 24 * BS * BS * BS,
            bytes_accessed=count * BS * BS * 38,
            transcendentals=0,
        ),
        name="shampoo_blocks",
    )(rates, gradient, *stats)


def shampoo_panel(turn, places, panels, stats):
    groups = len(panels)
    panel_rows = panels[0].shape[0]
    parts = 3
    breadth = groups * GROUP_WIDTH
    count = stats[0].shape[0]
    width = block_width(count)
    spec = pl.BlockSpec((width, BS, BS), lambda step, turn, places: (step, 0, 0))
    fixed = pl.BlockSpec(panels[0].shape, lambda step, turn, places: (0, 0))
    shape = jax.ShapeDtypeStruct((count, BS, BS), F32)
    per_part = breadth // BS
    per_row = parts * per_part
    side = D // BS

    def kernel(turn_ref, places_ref, *refs):
        step = pl.program_id(0)
        panel_refs = refs[:groups]
        stat_refs = refs[groups : groups + 5]
        outs = refs[groups + 5 : groups + 9]
        ordered, matrix = refs[groups + 9 :]

        @pl.when(step == 0)
        def _():
            for number, panel in enumerate(panel_refs):
                ordered[places_ref[number]] = panel[...]
            for part in range(parts):
                matrix[:, part * breadth : (part + 1) * breadth] = jnp.concatenate(
                    [
                        ordered[group, :, part * GROUP_WIDTH : (part + 1) * GROUP_WIDTH].astype(F32)
                        for group in range(groups)
                    ],
                    axis=1,
                )

        turned = turn_ref[0] == 1
        rate = jnp.where(turned, RATE_OUTPUT, RATE_PROJECT).astype(F32)
        for number in range(width):
            block = step * width + number
            row_now = jnp.where(turned, block % side % 2, block // per_row)
            column_now = jnp.where(
                turned, block % side // 2 * per_part + block // side, block % per_row
            )
            found = matrix[
                pl.ds(pl.multiple_of(row_now * BS, BS), BS),
                pl.ds(pl.multiple_of(column_now * BS, BS), BS),
            ]
            found = jnp.where(turned, found.T, found)
            results = renew(found, *[ref[number] for ref in stat_refs], rate)
            for target, result in zip(outs, results):
                target[number] = result

    return pl.pallas_call(
        kernel,
        grid_spec=pltpu.PrefetchScalarGridSpec(
            num_scalar_prefetch=2,
            grid=(count // width,),
            in_specs=[fixed] * groups + [spec] * 5,
            out_specs=[spec] * 4,
            scratch_shapes=[
                pltpu.VMEM((groups, *panels[0].shape), LOW),
                pltpu.VMEM((panel_rows, parts * breadth), F32),
            ],
        ),
        out_shape=[shape] * 4,
        compiler_params=params(),
        cost_estimate=pl.CostEstimate(
            flops=count * 24 * BS * BS * BS,
            bytes_accessed=count * BS * BS * 38,
            transcendentals=0,
        ),
        name="shampoo_panel",
    )(turn, places, *panels, *stats)


def shampoo_small(weights, gradient, left_stat, right_stat, left_root, right_root, step_rates):
    left_new = STAT_DECAY * left_stat + (1.0 - STAT_DECAY) * jnp.einsum(
        "nij,nkj->nik", gradient, gradient, precision=PRECISE
    )
    right_new = STAT_DECAY * right_stat + (1.0 - STAT_DECAY) * jnp.einsum(
        "nji,njk->nik", gradient, gradient, precision=PRECISE
    )
    turned = jnp.einsum("nij,njk->nik", gradient, right_root, precision=PRECISE)
    direction = jnp.einsum("nij,njk->nik", left_root, turned, precision=PRECISE)
    return (left_new, right_new, weights - step_rates * direction)


def shifted(values, axis, size, distance):
    return lax.ppermute(values, axis, [(i, (i + distance) % size) for i in range(size)])


def crossed(values, axes, size, distance):
    return lax.ppermute(values, axes, [(i, i ^ distance) for i in range(size)])


def direct_sum(values, axes, size):
    terms = [values] + [crossed(values, axes, size, step) for step in range(1, size)]
    while len(terms) > 1:
        terms = [terms[at] + terms[at + 1] for at in range(0, len(terms), 2)]
    return terms[0]


def everywhere_sum(values, sizes):
    a_size, b_size, c_size, f_size = sizes
    values = direct_sum(values, "f", f_size)
    values = direct_sum(values, "c", c_size)
    return direct_sum(values, ("a", "b"), a_size * b_size)


def body(
    sizes,
    inputs,
    out_grad,
    vectors,
    block_order,
    seq_lengths,
    expert_ids,
    attn_weights,
    attn_left,
    attn_right,
    attn_left_root,
    attn_right_root,
    expert_weights,
    expert_left,
    expert_right,
    expert_left_root,
    expert_right_root,
    router_weights,
    router_left,
    router_right,
    router_left_root,
    router_right_root,
):
    a_size, b_size, c_size, f_size = sizes
    rows = inputs.shape[0]
    capacity = rows // 4
    tokens_all = rows * a_size * b_size * c_size * f_size
    per_side = D // BS
    project_blocks = 3 * per_side * per_side
    a_place = lax.axis_index("a")
    c_place = lax.axis_index("c")
    f_place = lax.axis_index("f")
    per_device = attn_weights.shape[0]
    per = expert_weights.shape[1]
    shares = b_size * c_size
    local_slices = expert_weights.shape[0]

    by_panels = f_size == 4 and c_size == 2 and a_size == 2
    ends = jnp.cumsum(seq_lengths[0]).astype(jnp.int32)
    order = block_order[0].reshape(a_size * b_size, c_size, SLOTS)
    kpb = jnp.stack(
        [
            lax.dynamic_index_in_dim(order, (c_place - step) % c_size, 1, False).reshape(-1)
            for step in range(c_size)
        ]
    )

    split_count = expert_weights.shape[0] * f_size // EXPERTS
    numbers = jnp.arange(EXPERTS, dtype=jnp.int32)
    spots = (numbers % a_size) * f_size + numbers // a_size if split_count == 1 else numbers
    route_count = EXPERTS + ZEROS
    named = expert_ids[:, :, None] == jnp.arange(route_count, dtype=jnp.int32)[None, None, :]
    route_member = named.astype(F32)
    chosen = jnp.any(named[:, :, :EXPERTS], axis=1).astype(LOW)
    row_numbers = jnp.arange(rows, dtype=jnp.int32)
    before = (row_numbers[None, :] < row_numbers[:, None]).astype(LOW)
    ranks = jnp.dot(before, chosen, preferred_element_type=F32).astype(jnp.int32)
    slots = jnp.sum(
        jnp.where(named[:, :, :EXPERTS], (spots * capacity)[None, None, :] + ranks[:, None, :], 0),
        axis=2,
    )
    slots = jnp.where(expert_ids < EXPERTS, slots, -1)
    slot_numbers = jnp.arange(EXPERTS * capacity, dtype=jnp.int32)
    picks = [
        (slot_numbers[:, None] == slots[:, which][None, :]).astype(LOW) for which in range(2)
    ]
    picks_both = picks[0] + picks[1]

    def to_owners(buffer):
        buffer = buffer.astype(LOW).reshape(EXPERTS, capacity, D)
        if split_count > 1:
            buffer = jnp.repeat(buffer, split_count, axis=0)
        arrived = lax.all_to_all(buffer, ("a", "f"), split_axis=0, concat_axis=0, tiled=True)
        return arrived.reshape(-1, D)

    def return_rows(results):
        return lax.all_to_all(
            results.reshape(EXPERTS * split_count, -1, D),
            ("a", "f"),
            split_axis=0,
            concat_axis=0,
            tiled=True,
        )

    def from_owners(back, pick_matrices):
        back = back.reshape(EXPERTS, split_count, capacity, D)
        return [
            sum(
                dot(matrix, back[:, part].reshape(-1, D), 0, 0) for part in range(split_count)
            )
            for matrix in pick_matrices
        ]

    tie = lax.optimization_barrier
    share_place = lax.axis_index(("b", "c"))

    def over_groups(values):
        return lax.all_to_all(values, ("a", "b"), split_axis=0, concat_axis=0, tiled=True)

    def over_b(values):
        return crossed(values, "b", b_size, 1)

    def over_c(values):
        return crossed(values, "c", c_size, 1)

    if by_panels:
        group_place = lax.axis_index(("a", "b"))
        share_places = jnp.stack([share_place ^ step for step in range(shares)])
        first_spots, other_spots = a_place * shares + share_places, (
            (1 - a_place) * shares + share_places
        )

        def halves(values):
            return [values[: per // 2], values[per // 2 :]]

        own = jnp.where(a_place == 0, expert_weights[0], expert_weights[1])
        own_halves = halves(own)
        sent = jnp.where(a_place == 0, expert_weights[1], expert_weights[0])
        cuts = [slice(0, per // 2), slice(per // 2, per * 3 // 4), slice(per * 3 // 4, per)]
        across = crossed(attn_weights, "f", f_size, 2)
        own_c = over_c(own)
        got = [shifted(sent[cuts[0]], "a", 2, 1), None]
        own_b = [over_b(own_halves[0]), None]

        def both(spot):
            return [2 * spot, 2 * spot + 1]

        weight_places = [first_spots[0], first_spots[1]] + both(first_spots[2])
        weight_places += both(first_spots[3]) + both(other_spots[0]) + both(other_spots[1])
        weight_places += both(other_spots[2]) + both(other_spots[3])
        weight_places = jnp.stack(weight_places).astype(jnp.int32)
        kept_places = jnp.stack([share_places[step] for step in (0, 2, 1, 3)])
        given_places = [share_places[0], 2 * share_places[1], 2 * share_places[3]]
        given_places += [2 * share_places[2] + 1, 2 * share_places[3] + 1]
        given_places += [2 * share_places[2], 2 * share_places[1] + 1]
        kept_places = kept_places.astype(jnp.int32)
        given_places = jnp.stack(given_places).astype(jnp.int32)
        group_places = jnp.stack([group_place ^ step for step in range(HEAD_GROUPS)])
        group_places = group_places.astype(jnp.int32)
        shard_places = jnp.stack([f_place ^ step for step in range(f_size)]).astype(jnp.int32)
        (across, own_c, got[0], own_b[0], kpb, ends, *tables) = tie(
            (across, own_c, got[0], own_b[0], kpb, ends)
            + (weight_places, kept_places, given_places, group_places, shard_places)
        )
        weight_places, kept_places, given_places, group_places, shard_places = tables
        shards = [
            attn_weights,
            crossed(attn_weights, "f", f_size, 1),
            across,
            crossed(across, "f", f_size, 1),
        ]
        first_low, first_factor, own_queries, own_pairs, w_project = project_kernel(
            inputs, vectors[0:1], shard_places, shards
        )
        w_project = w_project.reshape(D, 3 * D)
        own_pairs, got_next = tie((own_pairs, shifted(sent[cuts[1]], "a", 2, 1)))
        own_b[1] = over_b(own_halves[1])
        own_bc = [over_c(own_b[0]), None]
        got_c = [over_c(got[0]), None]
        mine, own_b[1], own_bc[0], got_c[0] = tie(
            (over_groups(own_pairs), own_b[1], own_bc[0], got_c[0])
        )
        other = over_c(mine)
        queries = over_groups(own_queries)
        got_last = shifted(tie((sent[cuts[2]], mine))[0], "a", 2, 1)
        queries, other, got_last = tie((queries, other, got_last))
        got[1] = jnp.concatenate([got_next, got_last], axis=0)
        pairs = [mine, other]
        first_sent, own_b1, got_0, got_1 = tie((first_low, own_b[1], *got, queries))[:4]
        first_parts = [first_low, None, crossed(first_sent, ("a", "b"), HEAD_GROUPS, 2), None]
        own_bc[1] = over_c(own_b1)
        got_c[1] = over_c(got_1)
        got_b = [over_b(got_0), None]
        w_output = shards[3]
        for step in range(f_size - 1):
            w_output = jnp.where(f_place == 3 - step, shards[step], w_output)
        w_output = to_matrix(w_output, D, D)
        raw, low, lse = attend(kpb, ends, queries, pairs)
        raw, low, lse, first_parts[2], own_bc[1], got_c[1], got_b[0] = tie(
            (raw, low, lse, first_parts[2], own_bc[1], got_c[1], got_b[0])
        )
        got_b[1] = over_b(tie((got[1], low))[0])
    else:
        attn_all = lax.all_gather(attn_weights, "f", axis=0, tiled=True)
        w_project = to_matrix(attn_all[:project_blocks], D, 3 * D)
        w_output = to_matrix(attn_all[project_blocks:], D, D)
        first_norm, first_factor = normalize_parts(inputs, vectors[0])
        first_low = first_norm.astype(LOW)
        projected = jnp.dot(first_low, w_project, preferred_element_type=F32).astype(LOW)
        by_part = projected.reshape(rows, 3, HEAD_GROUPS, GROUP_WIDTH)
        own_queries = by_part[:, 0].transpose(1, 0, 2)
        own_pairs = (
            by_part[:, 1:].transpose(2, 0, 1, 3).reshape(HEAD_GROUPS, rows, 2 * GROUP_WIDTH)
        )
        mine = over_groups(own_pairs)
        pairs = [mine] + [shifted(mine, "c", c_size, step) for step in range(1, c_size)]
        queries = over_groups(pack_rows(own_queries))
        raw, low, lse = attend(kpb, ends, queries, pairs)
        weight_places = jnp.arange(local_slices, dtype=jnp.int32)
        weight_shares = [
            lax.all_gather(expert_weights[number], ("b", "c"), axis=0, tiled=True)
            for number in range(local_slices)
        ]
        weights = (weight_places, weight_shares)
    by_heads = unpack_rows(over_groups(low))
    attended = by_heads.transpose(1, 0, 2).reshape(rows, D)
    middle = inputs + jnp.dot(attended, w_output, preferred_element_type=F32)
    second, second_factor = normalize_parts(middle, vectors[1])
    second_low = second.astype(LOW)
    if by_panels:
        second_low, got_b[1] = tie((second_low, got_b[1]))
        first_sent, *got_bc = tie((first_low, *got_b, second_low))[:3]
        first_parts[1] = crossed(first_sent, ("a", "b"), HEAD_GROUPS, 1)
        got_bc = [over_c(part) for part in got_bc]

    logits = jnp.dot(second_low, router_weights, preferred_element_type=F32)
    picked_logits = jnp.sum(jnp.where(named, logits[:, None, :], 0.0), axis=2)
    route_gates = jax.nn.softmax(picked_logits, axis=-1)
    received = to_owners(dot(picks_both, second_low))
    grad_rows = [
        (route_gates[:, which][:, None] * out_grad).astype(LOW) for which in range(2)
    ]
    if by_panels:
        grad_rows[0], first_parts[1], *got_bc = tie((grad_rows[0], first_parts[1], *got_bc))
    arrived = to_owners(dot(picks[0], grad_rows[0]) + dot(picks[1], grad_rows[1]))
    if by_panels:
        weight_shares = [own, own_c, *own_b, *own_bc, *got, *got_c, *got_b, *got_bc]
        weights = (weight_places, weight_shares)
    result, gate_kept, up_kept, inner = expert_forward(received, weights)
    result = return_rows(result)
    back_rows, gate_grads, up_grads = expert_row_grads(arrived, gate_kept, up_kept, weights)
    if by_panels:
        full, part = per, per // 2
        half = a_place.astype(jnp.int32).reshape(1)
        given, hop_c, hop_b, near_b, near_c = expert_half_grads(
            1 - half,
            given_places,
            received,
            arrived,
            gate_grads,
            up_grads,
            inner,
            [(full,), (part, part), (part, part), (part,), (part,)],
        )
        first_parts[3] = over_b(tie((first_parts[2], arrived))[0])
        back_rows, result, near_b, gate_grads, up_grads, first_parts[3] = tie(
            (back_rows, result, near_b, gate_grads, up_grads, first_parts[3])
        )
        back_rows = return_rows(back_rows)
        kept, kept_far, kept_near, kept_next = expert_half_grads(
            half,
            kept_places,
            received,
            arrived,
            gate_grads,
            up_grads,
            inner,
            [(full,)] * 4,
        )
        back_rows, kept = tie((back_rows, kept))
        hop_c, hop_b = over_c(hop_c), over_b(hop_b)
    else:
        back_rows = return_rows(back_rows)
        grad_shares = expert_weight_grads(
            jnp.arange(shares, dtype=jnp.int32),
            received,
            arrived,
            gate_grads,
            up_grads,
            inner,
            [(per,)] * shares,
        )
    expert_rows = jnp.stack(from_owners(result, picks), axis=1)
    const_member = route_member[:, :, EXPERTS + 2 :]
    copy_member = route_member[:, :, EXPERTS + 1]
    route_values = (
        expert_rows
        + copy_member[:, :, None] * second[:, None, :]
        + jnp.einsum("rkc,cd->rkd", const_member, vectors[2:], precision=PRECISE)
    )
    output = middle + jnp.sum(route_gates[:, :, None] * route_values, axis=1)

    gate_grad = jnp.sum(out_grad[:, None, :] * route_values, axis=2)
    picked_grad = route_gates * (
        gate_grad - jnp.sum(route_gates * gate_grad, axis=1, keepdims=True)
    )
    logit_grad = jnp.sum(route_member * picked_grad[:, :, None], axis=1)
    router_local = lax.dot_general(
        logit_grad, second_low.astype(F32), (((0,), (0,)), ((), ())), precision=PRECISE
    )
    second_grad = jnp.dot(logit_grad, router_weights.astype(F32).T, precision=PRECISE)
    second_grad = second_grad + jnp.sum(route_gates * copy_member, axis=1)[:, None] * out_grad
    const_grad = jnp.einsum("rkc,rk,rd->cd", const_member, route_gates, out_grad, precision=PRECISE)
    second_grad = second_grad + from_owners(back_rows, [picks_both])[0]
    middle_part, second_gain_grad = normalize_back(middle, second_factor, vectors[1], second_grad)
    middle_grad = out_grad + middle_part
    middle_low = middle_grad.astype(LOW)

    flat = (-1, BS, BS)
    expert_stats = [
        item.reshape(flat)
        for item in (
            expert_weights,
            expert_left,
            expert_right,
            expert_left_root,
            expert_right_root,
        )
    ]

    attended_grad = dot(middle_low, w_output, 1, 1).astype(LOW)
    attended_grad = attended_grad.reshape(rows, HEAD_GROUPS, GROUP_WIDTH).transpose(1, 0, 2)
    attended_grad = over_groups(pack_rows(attended_grad))
    if by_panels:
        hop_c, hop_b = tie((hop_c, hop_b, middle_low))[:2]
        given_b = over_b((near_b.astype(F32) + hop_c[part:].astype(F32)).astype(LOW))
        given_c = (near_c.astype(F32) + hop_b[part:].astype(F32)).astype(LOW)
        kept_next = over_c(tie((kept_next, given_c))[0])
        given_c = over_c(given_c)
        early = jnp.concatenate([router_local, second_gain_grad[None], const_grad], axis=0)
        attended_grad, given_b, given_c, kept_next = tie(
            (attended_grad, given_b, given_c, kept_next)
        )
        kept_b = over_b((kept_far.astype(F32) + kept_next.astype(F32)).astype(LOW))
        taken = jnp.concatenate(
            [
                given[:part].astype(F32) + hop_c[:part].astype(F32) + given_b.astype(F32),
                given[part:].astype(F32) + hop_b[:part].astype(F32) + given_c.astype(F32),
            ],
            axis=0,
        )
        taken = shifted(taken.astype(LOW), "a", 2, 1)
        kept_near = over_c(tie((kept_near, attended_grad))[0])
        early = direct_sum(tie((early, attended_grad))[0], "f", f_size)
    back_outs = attend_back(kpb, ends, queries, pairs, attended_grad, raw, lse)
    if by_panels:
        sent_outs = back_outs
        *back_outs, kept_near, taken, kept_b, early = tie(
            (*back_outs, kept_near, taken, kept_b, early)
        )
        early = direct_sum(early, ("a", "b"), HEAD_GROUPS)
        middle_late = tie((middle_low, back_outs[0]))[0]
        output_panels = jnp.einsum(
            "hrj,rd->hdj", by_heads, middle_late, preferred_element_type=F32
        ).astype(LOW)
        output_panels = over_groups(output_panels)
        expert_outs = shampoo_half(1 - half, [taken], expert_stats, None)
        first_parts = tie((*first_parts, back_outs[0]))[:HEAD_GROUPS]
        first_all = jnp.zeros((HEAD_GROUPS, rows, D), LOW)
        for step, part_rows in enumerate(first_parts):
            first_all = lax.dynamic_update_index_in_dim(
                first_all, part_rows, group_place ^ step, 0
            )
        first_all = first_all.reshape(-1, D)
    query_grad, pair_grad = back_outs[:2]
    for step in range(1, c_size):
        sent = sent_outs if by_panels else back_outs
        pair_grad = pair_grad + shifted(sent[1 + step], "c", c_size, -step).astype(F32)
    group_grad = jnp.concatenate([query_grad, pair_grad.astype(LOW)], axis=2)
    if by_panels:
        group_grad, output_panels, first_all, early, *expert_outs = tie(
            (group_grad, output_panels, first_all, early, *expert_outs)
        )
    sent_grad = group_grad
    if by_panels:
        panels = dot(first_all, group_grad.reshape(-1, 3 * GROUP_WIDTH), 0, 0).astype(LOW)
        panels = panels.reshape(3, D // 3, 3 * GROUP_WIDTH)
        output_panels = jnp.sum(output_panels.astype(F32), axis=0).astype(LOW)
        output_panels = (
            output_panels.reshape(3, D // 3, GROUP_WIDTH)
            .transpose(1, 0, 2)
            .reshape(1, D // 3, 3 * GROUP_WIDTH)
        )
        panels = jnp.concatenate([panels, output_panels], axis=0)
        own_panels = [
            lax.dynamic_index_in_dim(panels, f_place ^ step, 0, False) for step in range(f_size)
        ]
        sent_grad, *own_panels = tie((sent_grad, *own_panels))
        summed = own_panels[0].astype(F32)
        for step in range(1, f_size):
            summed = summed + crossed(own_panels[step], "f", f_size, step).astype(F32)
        summed = summed.astype(LOW)
        summed = (summed.astype(F32) + crossed(summed, "c", 2, 1).astype(F32)).astype(LOW)
        early = direct_sum(early, "c", c_size)
    project_grad = over_groups(sent_grad)
    if by_panels:
        project_grad = tie((project_grad, summed))[0]
    project_grad = (
        project_grad
        .reshape(HEAD_GROUPS, rows, 3, GROUP_WIDTH)
        .transpose(1, 2, 0, 3)
        .reshape(rows, 3 * D)
    )
    first_grad = dot(project_grad, w_project, 1, 1)
    input_part, first_gain_grad = normalize_back(inputs, first_factor, vectors[0], first_grad)
    input_grad = middle_grad + input_part

    everywhere = ("a", "b", "c", "f")
    if not by_panels:
        early = jnp.concatenate([router_local, second_gain_grad[None], const_grad], axis=0)
        early = everywhere_sum(early, sizes)
    late = direct_sum(first_gain_grad[None], "f", f_size)
    late = direct_sum(late, "c", c_size)
    late = direct_sum(late, ("a", "b"), a_size * b_size)

    attn_stats = (attn_weights, attn_left, attn_right, attn_left_root, attn_right_root)
    if by_panels:
        kept = [kept, kept_near, kept_b]
        group_panels = [
            crossed(summed, ("a", "b"), HEAD_GROUPS, step) for step in range(1, HEAD_GROUPS)
        ]
        kept[0] = tie((kept[0], summed))[0]
        expert_outs = shampoo_half(half, kept, expert_stats, expert_outs)
        late, *joined = tie((late, *group_panels, *expert_outs))
        group_panels, expert_outs = joined[: HEAD_GROUPS - 1], joined[HEAD_GROUPS - 1 :]
        turn = (f_place == 3).astype(jnp.int32).reshape(1)
        attn_outs = shampoo_panel(
            turn, group_places, [summed, *group_panels], attn_stats
        )
    else:
        output_weight_grad = dot(attended, middle_low, 0, 0)
        project_weight_grad = dot(first_low, project_grad, 0, 0)
        attn_local = jnp.concatenate(
            [to_blocks(project_weight_grad, BS, BS), to_blocks(output_weight_grad, BS, BS)],
            axis=0,
        )
        attn_sum = lax.psum(attn_local, everywhere)
        attn_gradient = lax.dynamic_slice_in_dim(attn_sum, f_place * per_device, per_device, 0)
        block_numbers = f_place * per_device + jnp.arange(per_device, dtype=jnp.int32)
        attn_rates = jnp.where(block_numbers < project_blocks, RATE_PROJECT, RATE_OUTPUT)
        attn_outs = shampoo(attn_rates.astype(F32), attn_gradient, attn_stats)
        expert_gradient = lax.psum_scatter(
            jnp.concatenate(grad_shares, axis=0).reshape(local_slices, -1, BS, BS).astype(F32),
            ("b", "c"),
            scatter_dimension=1,
            tiled=True,
        ).reshape(flat)
        expert_outs = shampoo(
            jnp.full((expert_gradient.shape[0],), RATE_EXPERT, F32), expert_gradient, expert_stats
        )
    expert_grads, expert_left_new, expert_right_new, expert_new = [
        item.reshape(expert_weights.shape) for item in expert_outs
    ]
    attn_grads, attn_left_new, attn_right_new, attn_new = attn_outs
    router_grads = early[:route_count].T
    vector_grads = jnp.concatenate([late, early[route_count:]], axis=0)
    router_left_new, router_right_new, router_moved = shampoo_small(
        to_blocks(router_weights.astype(F32), BS, route_count),
        to_blocks(router_grads, BS, route_count),
        router_left,
        router_right,
        router_left_root,
        router_right_root,
        RATE_ROUTER,
    )
    router_new = to_matrix(router_moved, D, route_count)
    vector_new = vectors - RATE_VECTOR * float(tokens_all) ** (-0.5) * vector_grads
    return (
        output,
        input_grad,
        vector_grads,
        vector_new,
        attn_grads,
        attn_left_new,
        attn_right_new,
        attn_new,
        expert_grads,
        expert_left_new,
        expert_right_new,
        expert_new,
        router_grads,
        router_left_new,
        router_right_new,
        router_new,
    )


def solution(mesh):
    ctx_size = mesh.shape["ctx"]
    f_size = mesh.shape["fsdp"]
    context = ("a", "b", "c")
    token_rows = P(context + ("f",), None)
    group_rows = P("f", None)
    attn = P("f", None, None)
    expert = P("f", context, None, None)
    in_specs = (
        (token_rows, token_rows, P(), group_rows, group_rows, token_rows)
        + (attn,) * 5
        + (expert,) * 5
        + (P(),) * 5
    )
    out_specs = (token_rows, token_rows, P(), P()) + (attn,) * 4 + (expert,) * 4 + (P(),) * 4

    def run(*arrays):
        local_slices = arrays[11].shape[0] // f_size
        a_size = 2 if local_slices == 2 else 1
        b_size = HEAD_GROUPS // a_size
        c_size = ctx_size // HEAD_GROUPS
        sizes = (a_size, b_size, c_size, f_size)
        fine_mesh = jax.sharding.Mesh(mesh.devices.reshape(sizes), ("a", "b", "c", "f"))
        return jax.shard_map(
            functools.partial(body, sizes),
            mesh=fine_mesh,
            in_specs=in_specs,
            out_specs=out_specs,
            check_vma=False,
        )(*arrays)

    return run
```

```python
import functools

import jax
import jax.numpy as jnp
from jax import lax
from jax.experimental import pallas as pl
from jax.experimental.pallas import tpu as pltpu
from jax.sharding import PartitionSpec as P

D = 768
HEADS = 12
HDIM = 64
EXPERTS = 8
ZEROS = 4
BS = 128
SLOTS = 4
HEAD_GROUPS = 4
GROUP_WIDTH = HEADS // HEAD_GROUPS * HDIM
GROUP_HEADS = HEADS // HEAD_GROUPS
CHUNK = 256
TILE = 256
SUB = 32

EPSILON = 1e-06
SCORE_SCALE = 0.125
STAT_DECAY = 0.5
RATE_PROJECT = 0.4
RATE_OUTPUT = 3.0
RATE_EXPERT = 0.4
RATE_ROUTER = 0.2
RATE_VECTOR = 0.1
MASKED_SCORE = -1e30
PRECISE = lax.Precision.HIGHEST
F32 = jnp.float32
LOW = jnp.bfloat16
VMEM_LIMIT = 56 * 1024 * 1024


def to_matrix(blocks, height, breadth):
    block_height = blocks.shape[1]
    block_breadth = blocks.shape[2]
    shaped = blocks.reshape(
        height // block_height, breadth // block_breadth, block_height, block_breadth
    )
    return shaped.transpose(0, 2, 1, 3).reshape(height, breadth)


def to_blocks(matrix, block_height, block_breadth):
    height = matrix.shape[0]
    breadth = matrix.shape[1]
    shaped = matrix.reshape(
        height // block_height, block_height, breadth // block_breadth, block_breadth
    )
    return shaped.transpose(0, 2, 1, 3).reshape(-1, block_height, block_breadth)


def normalize_parts(values, scaling):
    factor = lax.rsqrt(jnp.mean(values * values, axis=-1, keepdims=True) + EPSILON)
    return (values * factor * scaling, factor)


def normalize_back(values, factor, scaling, gradient):
    unit_rows = values * factor
    scaled = gradient * scaling
    value_grad = factor * (
        scaled - unit_rows * jnp.mean(scaled * unit_rows, axis=-1, keepdims=True)
    )
    return (value_grad, jnp.sum(gradient * unit_rows, axis=0))


def dot(left, right, left_dim=1, right_dim=0):
    return lax.dot_general(
        left, right, (((left_dim,), (right_dim,)), ((), ())), preferred_element_type=F32
    )


def vmem_spec():
    return pl.BlockSpec(memory_space=pltpu.VMEM)


def smem_spec():
    return pl.BlockSpec(memory_space=pltpu.SMEM)


def params():
    return pltpu.CompilerParams(vmem_limit_bytes=VMEM_LIMIT)


def project_kernel(rows_in, gain, places, shards):
    rows = rows_in.shape[0]
    owners = len(shards) - 1
    depth = D // owners
    breadth = 3 * D
    block_rows = depth // BS
    block_columns = breadth // BS
    pair = 2 * GROUP_WIDTH

    def kernel(places_ref, rows_ref, gain_ref, *refs):
        shard_refs = refs[: owners + 1]
        first_out, factor_out, query_out, pair_out, matrix, first_s = refs[owners + 1 :]
        for number, shard in enumerate(shard_refs):
            owner = places_ref[number]

            @pl.when(owner < owners)
            def _(owner=owner, shard=shard):
                for row in range(block_rows):
                    for column in range(block_columns):
                        matrix[
                            owner, row * BS : (row + 1) * BS, column * BS : (column + 1) * BS
                        ] = shard[row * block_columns + column]

        def norm(tile, carry):
            at = pl.ds(pl.multiple_of(tile * SUB, SUB), SUB)
            values = rows_ref[at, :]
            factor = lax.rsqrt(jnp.mean(values * values, axis=1, keepdims=True) + EPSILON)
            first = (values * factor * gain_ref[...]).astype(LOW)
            factor_out[at, :] = factor
            first_out[at, :] = first
            for owner in range(owners):
                first_s[owner, at, :] = first[:, owner * depth : (owner + 1) * depth]
            return carry

        lax.fori_loop(0, rows // SUB, norm, 0)
        for tile in range(breadth // pair):
            at = slice(tile * pair, (tile + 1) * pair)
            total = dot(first_s[0], matrix[0, :, at])
            for owner in range(1, owners):
                total = total + dot(first_s[owner], matrix[owner, :, at])
            total = total.astype(LOW)
            part = tile * pair // D
            group = tile * pair % D // GROUP_WIDTH
            for side in range(2):
                piece = total[:, side * GROUP_WIDTH : (side + 1) * GROUP_WIDTH]
                if part == 0:
                    query_out[group + side] = jnp.concatenate(
                        [piece[: rows // 2], piece[rows // 2 :]], axis=1
                    )
                else:
                    pair_out[
                        group + side, :, (part - 1) * GROUP_WIDTH : part * GROUP_WIDTH
                    ] = piece

    return pl.pallas_call(
        kernel,
        in_specs=[smem_spec()] + [vmem_spec()] * (owners + 3),
        out_specs=[vmem_spec()] * 5,
        out_shape=[
            jax.ShapeDtypeStruct((rows, D), LOW),
            jax.ShapeDtypeStruct((rows, 1), F32),
            jax.ShapeDtypeStruct((HEAD_GROUPS, rows // 2, pair), LOW),
            jax.ShapeDtypeStruct((HEAD_GROUPS, rows, pair), LOW),
            jax.ShapeDtypeStruct((owners, depth, breadth), LOW),
        ],
        scratch_shapes=[pltpu.VMEM((owners, rows, depth), LOW)],
        compiler_params=params(),
        cost_estimate=pl.CostEstimate(
            flops=2 * rows * D, bytes_accessed=1_000_000, transcendentals=0
        ),
        name="project",
    )(places, rows_in, gain, *shards)


def head_masks(value):
    lane = lax.broadcasted_iota(jnp.int32, (1, GROUP_WIDTH), 1)
    return [
        jnp.where(lane // HDIM == head, value, 0.0).astype(F32) for head in range(GROUP_HEADS)
    ]


def stack_heads(rows, masks):
    return jnp.concatenate([rows * mask.astype(rows.dtype) for mask in masks], axis=0)


def packed_at(slot, block_rows):
    first_row = slot % 2 * block_rows
    first_lane = slot // 2 * GROUP_WIDTH
    return slice(first_row, first_row + block_rows), slice(first_lane, first_lane + GROUP_WIDTH)


def pack_rows(values):
    groups, rows, width = values.shape
    return values.reshape(groups, 2, rows // 2, width).transpose(0, 2, 1, 3).reshape(
        groups, rows // 2, 2 * width
    )


def unpack_rows(values):
    groups, rows, width = values.shape
    return values.reshape(groups, rows, 2, width // 2).transpose(0, 2, 1, 3).reshape(
        groups, 2 * rows, width // 2
    )


def fill_sorted(kpb, sources, key_sorted, value_sorted, block_rows, block_count):
    key_sorted[0:CHUNK, :] = jnp.zeros((CHUNK, GROUP_WIDTH), LOW)
    value_sorted[0:CHUNK, :] = jnp.zeros((CHUNK, GROUP_WIDTH), LOW)
    for number, source in enumerate(sources):

        def fill(item, carry, source=source, number=number):
            from_row = pl.multiple_of(item % SLOTS * block_rows, block_rows)
            to_row = pl.multiple_of(CHUNK + kpb[number, item] * block_rows, 32)
            rows = source[item // SLOTS, pl.ds(from_row, block_rows), :]
            key_sorted[pl.ds(to_row, block_rows), :] = rows[:, 0:GROUP_WIDTH]
            value_sorted[pl.ds(to_row, block_rows), :] = rows[:, GROUP_WIDTH:]
            return carry

        lax.fori_loop(0, block_count, fill, 0)


def list_steps(kpb, ends, sequences, block_rows, block_count, block_of, place_of):
    def one_block(item, first_step):
        first = kpb[0, item] * block_rows
        lowest = jnp.int32(0)
        for sequence in range(sequences):
            ending = ends[sequence]
            lowest = jnp.where(first >= ending, ending, lowest)
        top = first + block_rows
        count = (top - lowest + CHUNK - 1) // CHUNK

        def one_step(step, carry):
            block_of[first_step + step] = item
            place_of[first_step + step] = top - (step + 1) * CHUNK
            return carry

        lax.fori_loop(0, count, one_step, 0)
        return first_step + count

    return lax.fori_loop(0, block_count, one_block, jnp.int32(0))


def fill_limits(kpb, ends, sequences, block_rows, item, start_s, place_s):
    for tile in range(GROUP_HEADS * block_rows // SUB):
        within = tile * SUB % block_rows
        places = (
            kpb[0, item] * block_rows
            + within
            + lax.broadcasted_iota(jnp.int32, (SUB, BS), 0)
        )
        starts = jnp.zeros_like(places)
        for sequence in range(sequences):
            ending = ends[sequence]
            starts = jnp.where(places >= ending, ending, starts)
        at_rows = slice(tile * SUB, (tile + 1) * SUB)
        start_s[item, at_rows, :] = starts
        place_s[item, at_rows, :] = places


def pipeline(total, scores, middle, products):
    scores(jnp.int32(0), 0)

    def pair(number, carry):
        step = 2 * number
        scores(step + 1, 1)
        middle(step, 0)
        products(step - 1, 1)
        scores(step + 2, 0)
        middle(step + 1, 1)
        products(step, 0)
        return carry

    lax.fori_loop(0, (total + 2) // 2, pair, 0)


def tile_slices(count):
    return [slice(tile * SUB, (tile + 1) * SUB) for tile in range(count)]


def attend_kernel(sources_count, block_rows, sequences, *refs):
    kpb, ends, queries = refs[:3]
    sources = refs[3 : 3 + sources_count]
    raw_out, low_out, lse_out, key_sorted, value_sorted, query_s, start_s, place_s = refs[
        3 + sources_count : 11 + sources_count
    ]
    best_s, total_s, gathered_s, score_0, score_1, weight_0, weight_1, fade_0, fade_1 = refs[
        11 + sources_count : 20 + sources_count
    ]
    block_of, place_of = refs[20 + sources_count :]
    score_s, weight_s, fade_s = (score_0, score_1), (weight_0, weight_1), (fade_0, fade_1)
    block_count = queries.shape[0] * SLOTS
    stacked = GROUP_HEADS * block_rows
    tiles = tile_slices(stacked // SUB)
    fill_sorted(kpb, sources, key_sorted, value_sorted, block_rows, block_count)
    total = list_steps(kpb, ends, sequences, block_rows, block_count, block_of, place_of)
    masks = head_masks(SCORE_SCALE)
    plain = head_masks(1.0)

    def load(group, carry):
        for slot in range(SLOTS):
            rows, lanes = packed_at(slot, block_rows)
            query_s[group * SLOTS + slot] = stack_heads(queries[group, rows, lanes], masks)
        return carry

    lax.fori_loop(0, block_count // SLOTS, load, 0)

    def prepare(item, carry):
        fill_limits(kpb, ends, sequences, block_rows, item, start_s, place_s)
        best_s[item] = jnp.full((stacked, BS), MASKED_SCORE, F32)
        total_s[item] = jnp.zeros((stacked, BS), F32)
        gathered_s[item] = jnp.zeros((stacked, GROUP_WIDTH), F32)
        return carry

    lax.fori_loop(0, block_count, prepare, 0)
    weight_1[...] = jnp.zeros_like(weight_1)
    fade_1[...] = jnp.ones_like(fade_1)

    def find(step):
        inside = jnp.clip(step, 0, total - 1)
        return block_of[inside], place_of[inside]

    def scores(step, side):
        item, low_place = find(step)
        at = pl.multiple_of(low_place + CHUNK, 32)
        score_s[side][...] = dot(query_s[item], key_sorted[pl.ds(at, CHUNK), :], 1, 1)

    def middle(step, side):
        item, low_place = find(step)
        low_place = jnp.where(step < total, low_place, -(1 << 24))
        lanes = low_place + lax.broadcasted_iota(jnp.int32, (1, BS), 1)
        for rows in tiles:
            starts, places = start_s[item, rows, :], place_s[item, rows, :]
            parts = []
            for part in range(CHUNK // BS):
                key_places = lanes + part * BS
                allowed = (key_places >= starts) & (key_places <= places)
                found = score_s[side][rows, part * BS : (part + 1) * BS]
                parts.append(jnp.where(allowed, found, MASKED_SCORE))
            best = best_s[item, rows, :]
            top = jnp.max(functools.reduce(jnp.maximum, parts), axis=1, keepdims=True)
            peak = jnp.maximum(best, top)
            fade = jnp.exp(best - peak)
            so_far = total_s[item, rows, :] * fade
            for part, found in enumerate(parts):
                weights = jnp.exp(found - peak)
                so_far = so_far + weights
                weight_s[side][rows, part * BS : (part + 1) * BS] = weights.astype(LOW)
            best_s[item, rows, :] = peak
            total_s[item, rows, :] = so_far
            fade_s[side][rows, :] = fade

    def products(step, side):
        item, low_place = find(step)
        at = pl.multiple_of(low_place + CHUNK, 32)
        fade = fade_s[side][...]
        fade = jnp.concatenate([fade, fade[:, : GROUP_WIDTH - BS]], axis=1)
        gathered_s[item] = gathered_s[item] * fade + dot(
            weight_s[side][...], value_sorted[pl.ds(at, CHUNK), :]
        )

    pipeline(total, scores, middle, products)

    def finish(group, carry):
        for slot in range(SLOTS):
            item = group * SLOTS + slot
            rows, lanes = packed_at(slot, block_rows)
            sums = jnp.sum(total_s[item], axis=1, keepdims=True)
            gathered = gathered_s[item] / sums
            result = jnp.zeros((block_rows, GROUP_WIDTH), F32)
            for head in range(GROUP_HEADS):
                result = result + (
                    plain[head] * gathered[head * block_rows : (head + 1) * block_rows]
                )
            raw_out[group, slot * block_rows : (slot + 1) * block_rows, :] = result
            low_out[group, rows, lanes] = result.astype(LOW)
            lse_out[item] = best_s[item][:, 0:1] + jnp.log(sums)
        return carry

    lax.fori_loop(0, block_count // SLOTS, finish, 0)


def attend_sizes(queries, pairs):
    groups, rows, _ = pairs[0].shape
    block_rows = rows // SLOTS
    all_rows = groups * rows * len(pairs)
    blocks = groups * SLOTS
    stacked = GROUP_HEADS * block_rows
    return groups, rows, block_rows, all_rows, blocks, stacked


def attend(kpb, ends, queries, pairs):
    groups, rows, block_rows, all_rows, blocks, stacked = attend_sizes(queries, pairs)
    steps = blocks * (all_rows // CHUNK + 1)
    return pl.pallas_call(
        functools.partial(attend_kernel, len(pairs), block_rows, ends.shape[0]),
        in_specs=[smem_spec()] * 2 + [vmem_spec()] * (1 + len(pairs)),
        out_specs=[vmem_spec()] * 3,
        out_shape=[
            jax.ShapeDtypeStruct((groups, rows, GROUP_WIDTH), F32),
            jax.ShapeDtypeStruct((groups, rows // 2, 2 * GROUP_WIDTH), LOW),
            jax.ShapeDtypeStruct((blocks, stacked, 1), F32),
        ],
        scratch_shapes=[
            pltpu.VMEM((CHUNK + all_rows, GROUP_WIDTH), LOW),
            pltpu.VMEM((CHUNK + all_rows, GROUP_WIDTH), LOW),
            pltpu.VMEM((blocks, stacked, GROUP_WIDTH), LOW),
            pltpu.VMEM((blocks, stacked, BS), jnp.int32),
            pltpu.VMEM((blocks, stacked, BS), jnp.int32),
            pltpu.VMEM((blocks, stacked, BS), F32),
            pltpu.VMEM((blocks, stacked, BS), F32),
            pltpu.VMEM((blocks, stacked, GROUP_WIDTH), F32),
            pltpu.VMEM((stacked, CHUNK), F32),
            pltpu.VMEM((stacked, CHUNK), F32),
            pltpu.VMEM((stacked, CHUNK), LOW),
            pltpu.VMEM((stacked, CHUNK), LOW),
            pltpu.VMEM((stacked, BS), F32),
            pltpu.VMEM((stacked, BS), F32),
            pltpu.SMEM((steps,), jnp.int32),
            pltpu.SMEM((steps,), jnp.int32),
        ],
        compiler_params=params(),
        cost_estimate=pl.CostEstimate(
            flops=groups * rows * HDIM,
            bytes_accessed=1_000_000,
            transcendentals=0,
        ),
        name="attend_forward",
    )(kpb, ends, queries, *pairs)


def attend_back_kernel(sources_count, block_rows, sequences, *refs):
    kpb, ends, queries = refs[:3]
    sources = refs[3 : 3 + sources_count]
    out_grad, raw, lse = refs[3 + sources_count : 6 + sources_count]
    query_out = refs[6 + sources_count]
    pair_outs = refs[7 + sources_count : 7 + 2 * sources_count]
    rest = refs[7 + 2 * sources_count :]
    key_sorted, value_sorted, key_grad, value_grad, query_s, grad_s, query_grad = rest[:7]
    start_s, place_s, shift_s, delta_s = rest[7:11]
    score_s, back_s, weight_s, change_s = rest[11:13], rest[13:15], rest[15:17], rest[17:19]
    block_of, place_of = rest[19:]
    block_count = queries.shape[0] * SLOTS
    stacked = GROUP_HEADS * block_rows
    tiles = tile_slices(stacked // SUB)
    fill_sorted(kpb, sources, key_sorted, value_sorted, block_rows, block_count)
    total = list_steps(kpb, ends, sequences, block_rows, block_count, block_of, place_of)
    key_grad[...] = jnp.zeros_like(key_grad)
    value_grad[...] = jnp.zeros_like(value_grad)
    weight_s[1][...] = jnp.zeros_like(weight_s[1])
    change_s[1][...] = jnp.zeros_like(change_s[1])
    masks = head_masks(SCORE_SCALE)
    plain = head_masks(1.0)

    def load(group, carry):
        for slot in range(SLOTS):
            item = group * SLOTS + slot
            rows, lanes = packed_at(slot, block_rows)
            query_s[item] = stack_heads(queries[group, rows, lanes], masks)
            grad = stack_heads(out_grad[group, rows, lanes], plain)
            grad_s[item] = grad
            values = raw[group, slot * block_rows : (slot + 1) * block_rows, :]
            delta = jnp.sum(
                grad.astype(F32) * jnp.concatenate([values] * GROUP_HEADS, axis=0),
                axis=1,
                keepdims=True,
            )
            delta_s[item] = jnp.broadcast_to(delta, (stacked, BS))
        return carry

    lax.fori_loop(0, block_count // SLOTS, load, 0)

    def prepare(item, carry):
        shift_s[item] = jnp.broadcast_to(lse[item], (stacked, BS))
        query_grad[item] = jnp.zeros((stacked, GROUP_WIDTH), F32)
        fill_limits(kpb, ends, sequences, block_rows, item, start_s, place_s)
        return carry

    lax.fori_loop(0, block_count, prepare, 0)

    def find(step):
        inside = jnp.clip(step, 0, total - 1)
        return block_of[inside], place_of[inside]

    def scores(step, side):
        item, low_place = find(step)
        at = pl.ds(pl.multiple_of(low_place + CHUNK, 32), CHUNK)
        score_s[side][...] = dot(query_s[item], key_sorted[at, :], 1, 1)
        back_s[side][...] = dot(grad_s[item], value_sorted[at, :], 1, 1)

    def middle(step, side):
        item, low_place = find(step)
        low_place = jnp.where(step < total, low_place, -(1 << 24))
        lanes = low_place + lax.broadcasted_iota(jnp.int32, (1, BS), 1)
        for rows in tiles:
            starts, places = start_s[item, rows, :], place_s[item, rows, :]
            shift, delta = shift_s[item, rows, :], delta_s[item, rows, :]
            for part in range(CHUNK // BS):
                at_lanes = slice(part * BS, (part + 1) * BS)
                key_places = lanes + part * BS
                allowed = (key_places >= starts) & (key_places <= places)
                found = score_s[side][rows, at_lanes] - shift
                weights = jnp.exp(jnp.where(allowed, found, MASKED_SCORE))
                weight_s[side][rows, at_lanes] = weights.astype(LOW)
                change = weights * (back_s[side][rows, at_lanes] - delta)
                change_s[side][rows, at_lanes] = change.astype(LOW)

    def products(step, side):
        item, low_place = find(step)
        at = pl.ds(pl.multiple_of(low_place + CHUNK, 32), CHUNK)
        value_grad[at, :] += dot(weight_s[side][...], grad_s[item], 0, 0)
        key_grad[at, :] += dot(change_s[side][...], query_s[item], 0, 0)
        query_grad[item] += dot(change_s[side][...], key_sorted[at, :])

    pipeline(total, scores, middle, products)

    def finish(item, carry):
        at = pl.ds(pl.multiple_of(item % SLOTS * block_rows, block_rows), block_rows)
        result = jnp.zeros((block_rows, GROUP_WIDTH), F32)
        for head in range(GROUP_HEADS):
            result = result + masks[head] * (
                query_grad[item, head * block_rows : (head + 1) * block_rows, :]
            )
        query_out[item // SLOTS, at, :] = result.astype(LOW)
        return carry

    lax.fori_loop(0, block_count, finish, 0)
    for number, target in enumerate(pair_outs):

        def drain(item, carry, number=number, target=target):
            to_row = pl.multiple_of(item % SLOTS * block_rows, block_rows)
            from_row = pl.multiple_of(CHUNK + kpb[number, item] * block_rows, 32)
            pair = jnp.concatenate(
                [
                    key_grad[pl.ds(from_row, block_rows), :],
                    value_grad[pl.ds(from_row, block_rows), :],
                ],
                axis=1,
            )
            target[item // SLOTS, pl.ds(to_row, block_rows), :] = pair.astype(target.dtype)
            return carry

        lax.fori_loop(0, block_count, drain, 0)


def attend_back(kpb, ends, queries, pairs, out_grad, raw, lse):
    groups, rows, block_rows, all_rows, blocks, stacked = attend_sizes(queries, pairs)
    steps = blocks * (all_rows // CHUNK + 1)
    limit = pltpu.VMEM((blocks, stacked, BS), jnp.int32)
    row_values = pltpu.VMEM((blocks, stacked, BS), F32)
    sorted_low = pltpu.VMEM((CHUNK + all_rows, GROUP_WIDTH), LOW)
    sorted_sum = pltpu.VMEM((CHUNK + all_rows, GROUP_WIDTH), F32)
    stacked_low = pltpu.VMEM((blocks, stacked, GROUP_WIDTH), LOW)
    square = pltpu.VMEM((stacked, CHUNK), F32)
    square_low = pltpu.VMEM((stacked, CHUNK), LOW)
    return pl.pallas_call(
        functools.partial(attend_back_kernel, len(pairs), block_rows, ends.shape[0]),
        in_specs=[smem_spec()] * 2 + [vmem_spec()] * (4 + len(pairs)),
        out_specs=[vmem_spec()] * (1 + len(pairs)),
        out_shape=[
            jax.ShapeDtypeStruct((groups, rows, GROUP_WIDTH), LOW),
            jax.ShapeDtypeStruct((groups, rows, 2 * GROUP_WIDTH), F32),
        ]
        + [jax.ShapeDtypeStruct((groups, rows, 2 * GROUP_WIDTH), LOW) for _ in pairs[1:]],
        scratch_shapes=[sorted_low] * 2
        + [sorted_sum] * 2
        + [stacked_low] * 2
        + [pltpu.VMEM((blocks, stacked, GROUP_WIDTH), F32)]
        + [limit] * 2
        + [row_values] * 2
        + [square] * 4
        + [square_low] * 4
        + [pltpu.SMEM((steps,), jnp.int32)] * 2,
        compiler_params=params(),
        cost_estimate=pl.CostEstimate(
            flops=groups * rows * HDIM,
            bytes_accessed=1_000_000,
            transcendentals=0,
        ),
        name="attend_backward",
    )(kpb, ends, queries, *pairs, out_grad, raw, lse)


def side_blocks():
    return D // BS


def bring(places, sources, held, done):
    copies = []
    for number, source in enumerate(sources):
        size = source.shape[0]
        target = held.at[pl.ds(places[number] * size, size)]
        copies.append(pltpu.make_async_copy(source, target, done.at[number]))
    for copy in copies:
        copy.start()
    for copy in copies:
        copy.wait()


def wide_tile(held, first, hidden_blocks, step):
    rows = []
    for row in range(side_blocks()):
        at = first + row * hidden_blocks + 2 * step
        rows.append(jnp.concatenate([held[at], held[at + 1]], axis=1))
    return jnp.concatenate(rows, axis=0)


def tall_tile(held, first, step):
    side = side_blocks()
    rows = []
    for half in range(2):
        at = first + (2 * step + half) * side
        rows.append(jnp.concatenate([held[at + column] for column in range(side)], axis=1))
    return jnp.concatenate(rows, axis=0)


def expert_sizes(weights):
    total = sum(array.shape[0] for array in weights[1])
    return total, total // (3 * side_blocks())


def expert_forward(rows_in, weights):
    rows = rows_in.shape[0]
    places, sources = weights
    count = len(sources)
    total_blocks, hidden_blocks = expert_sizes(weights)
    up_first = side_blocks() * hidden_blocks

    def kernel(places_ref, rows_ref, *refs):
        source_refs = refs[:count]
        result, gate_o, up_o, inner_o, total, held, done = refs[count:]
        step = pl.program_id(0)

        @pl.when(step == 0)
        def _():
            bring(places_ref, source_refs, held, done)
            total[...] = jnp.zeros_like(total)

        gate_tile = wide_tile(held, 0, hidden_blocks, step)
        up_tile = wide_tile(held, up_first, hidden_blocks, step)
        down_tile = tall_tile(held, 2 * up_first, step)

        for number in range(rows // TILE):
            first = number * TILE
            at = pl.ds(first, TILE)
            entering = rows_ref[at, :]
            gate_o[at, :] = dot(entering, gate_tile)
            up_o[at, :] = dot(entering, up_tile)
            for sub in range(TILE // SUB):
                now = pl.ds(first + sub * SUB, SUB)
                gate = gate_o[now, :]
                inner_o[now, :] = (gate * jax.nn.sigmoid(gate) * up_o[now, :]).astype(LOW)
            total[at, :] += dot(inner_o[at, :], down_tile)

        @pl.when(step == pl.num_programs(0) - 1)
        def _():
            result[...] = total[...].astype(LOW)

    fixed = pl.BlockSpec((rows, D), lambda step: (0, 0))
    hidden = pl.BlockSpec((rows, TILE), lambda step: (0, step))
    hidden_size = (rows, hidden_blocks * BS)
    return pl.pallas_call(
        kernel,
        grid=(hidden_blocks // 2,),
        in_specs=[smem_spec(), fixed] + [pl.BlockSpec(memory_space=pl.ANY)] * count,
        out_specs=[fixed] + [hidden] * 3,
        out_shape=[
            jax.ShapeDtypeStruct((rows, D), LOW),
            jax.ShapeDtypeStruct(hidden_size, F32),
            jax.ShapeDtypeStruct(hidden_size, F32),
            jax.ShapeDtypeStruct(hidden_size, LOW),
        ],
        scratch_shapes=[
            pltpu.VMEM((rows, D), F32),
            pltpu.VMEM((total_blocks, BS, BS), LOW),
            pltpu.SemaphoreType.DMA((count,)),
        ],
        compiler_params=params(),
        cost_estimate=pl.CostEstimate(
            flops=6 * rows * D * hidden_blocks * BS,
            bytes_accessed=6 * D * hidden_blocks * BS + 4 * rows * D,
            transcendentals=0,
        ),
        name="expert_forward",
    )(places, rows_in, *sources)


def expert_row_grads(grads_in, gate_in, up_in, weights):
    rows = grads_in.shape[0]
    places, sources = weights
    count = len(sources)
    total_blocks, hidden_blocks = expert_sizes(weights)
    up_first = side_blocks() * hidden_blocks

    def kernel(places_ref, grads_ref, gate_i, up_i, *refs):
        source_refs = refs[:count]
        back, gate_s, up_s, total, inner_grad_s, held, done = refs[count:]
        step = pl.program_id(0)

        @pl.when(step == 0)
        def _():
            bring(places_ref, source_refs, held, done)
            total[...] = jnp.zeros_like(total)

        gate_tile = wide_tile(held, 0, hidden_blocks, step)
        up_tile = wide_tile(held, up_first, hidden_blocks, step)
        down_tile = tall_tile(held, 2 * up_first, step)

        for number in range(rows // TILE):
            first = number * TILE
            at = pl.ds(first, TILE)
            inner_grad_s[at, :] = dot(grads_ref[at, :], down_tile, 1, 1)
            for sub in range(TILE // SUB):
                now = pl.ds(first + sub * SUB, SUB)
                gate = gate_i[now, :]
                inner_grad = inner_grad_s[now, :]
                sigmoid = jax.nn.sigmoid(gate)
                up_s[now, :] = (inner_grad * (gate * sigmoid)).astype(LOW)
                gate_s[now, :] = (
                    inner_grad * up_i[now, :] * (sigmoid * (1.0 + gate * (1.0 - sigmoid)))
                ).astype(LOW)
            total[at, :] += dot(gate_s[at, :], gate_tile, 1, 1) + dot(
                up_s[at, :], up_tile, 1, 1
            )

        @pl.when(step == pl.num_programs(0) - 1)
        def _():
            back[...] = total[...].astype(LOW)

    fixed = pl.BlockSpec((rows, D), lambda step: (0, 0))
    hidden = pl.BlockSpec((rows, TILE), lambda step: (0, step))
    hidden_shape = jax.ShapeDtypeStruct((rows, hidden_blocks * BS), LOW)
    return pl.pallas_call(
        kernel,
        grid=(hidden_blocks // 2,),
        in_specs=[smem_spec(), fixed, hidden, hidden]
        + [pl.BlockSpec(memory_space=pl.ANY)] * count,
        out_specs=[fixed] + [hidden] * 2,
        out_shape=[jax.ShapeDtypeStruct((rows, D), LOW)] + [hidden_shape] * 2,
        scratch_shapes=[
            pltpu.VMEM((rows, D), F32),
            pltpu.VMEM((rows, TILE), F32),
            pltpu.VMEM((total_blocks, BS, BS), LOW),
            pltpu.SemaphoreType.DMA((count,)),
        ],
        compiler_params=params(),
        cost_estimate=pl.CostEstimate(
            flops=6 * rows * D * hidden_blocks * BS,
            bytes_accessed=12 * D * hidden_blocks * BS + 6 * rows * D,
            transcendentals=0,
        ),
        name="expert_row_grads",
    )(places, grads_in, gate_in, up_in, *sources)


def expert_weight_grads(places, rows_in, grads_in, gate_grads, up_grads, inner, sizes):
    rows = rows_in.shape[0]
    hidden_blocks = gate_grads.shape[1] // BS
    side = side_blocks()
    total_blocks = 3 * side * hidden_blocks
    count = len(sizes)
    pieces = sum(len(group) for group in sizes)

    def kernel(places_ref, rows_ref, grads_ref, gate_s, up_s, inner_s, *refs):
        outs = refs[:count]
        turned, held, done = refs[count:]
        step = pl.program_id(0)

        @pl.when(step == 0)
        def _():
            turned[...] = rows_ref[...].T

        def wide_out(source, first):
            product = dot(turned[...], source[...]).astype(LOW)
            for row in range(side):
                for column in range(2):
                    held[first + row * hidden_blocks + 2 * step + column] = product[
                        row * BS : (row + 1) * BS, column * BS : (column + 1) * BS
                    ]

        wide_out(gate_s, 0)
        wide_out(up_s, side * hidden_blocks)
        product = dot(inner_s[...], grads_ref[...], 0, 0).astype(LOW)
        for half in range(2):
            for column in range(side):
                held[2 * side * hidden_blocks + (2 * step + half) * side + column] = product[
                    half * BS : (half + 1) * BS, column * BS : (column + 1) * BS
                ]

        @pl.when(step == pl.num_programs(0) - 1)
        def _():
            copies = []
            for target, group in zip(outs, sizes):
                first = 0
                for size in group:
                    number = len(copies)
                    source = held.at[pl.ds(places_ref[number] * size, size)]
                    into = target.at[pl.ds(first, size)]
                    copies.append(pltpu.make_async_copy(source, into, done.at[number]))
                    first += size
            for copy in copies:
                copy.start()
            for copy in copies:
                copy.wait()

    fixed = pl.BlockSpec((rows, D), lambda step: (0, 0))
    hidden = pl.BlockSpec((rows, TILE), lambda step: (0, step))
    return pl.pallas_call(
        kernel,
        grid=(hidden_blocks // 2,),
        in_specs=[smem_spec(), fixed, fixed] + [hidden] * 3,
        out_specs=[pl.BlockSpec(memory_space=pl.ANY)] * count,
        out_shape=[jax.ShapeDtypeStruct((sum(group), BS, BS), LOW) for group in sizes],
        scratch_shapes=[
            pltpu.VMEM((D, rows), LOW),
            pltpu.VMEM((total_blocks, BS, BS), LOW),
            pltpu.SemaphoreType.DMA((pieces,)),
        ],
        compiler_params=params(),
        cost_estimate=pl.CostEstimate(
            flops=6 * rows * D * hidden_blocks * BS,
            bytes_accessed=12 * D * hidden_blocks * BS + 6 * rows * D,
            transcendentals=0,
        ),
        name="expert_weight_grads",
    )(places, rows_in, grads_in, gate_grads, up_grads, inner)


def expert_half_grads(which, places, rows_in, grads_in, gate_grads, up_grads, inner, sizes):
    rows = rows_in.shape[0]
    hidden_blocks = gate_grads.shape[1] // BS
    side = side_blocks()
    middle_row = side // 2
    total_blocks = 3 * side * hidden_blocks // 2
    count = len(sizes)
    pieces = sum(len(group) for group in sizes)

    def kernel(which_ref, places_ref, rows_ref, grads_ref, gate_s, up_s, inner_s, *refs):
        outs = refs[:count]
        turned, held, done = refs[count:]
        step = pl.program_id(0)

        @pl.when(step == 0)
        def _():
            turned[...] = rows_ref[...].T

        def wide_out(source, first_row, last_row, first):
            product = dot(turned[first_row * BS : last_row * BS, :], source[...]).astype(LOW)
            for row in range(last_row - first_row):
                for column in range(2):
                    held[first + row * hidden_blocks + 2 * step + column] = product[
                        row * BS : (row + 1) * BS, column * BS : (column + 1) * BS
                    ]

        @pl.when(which_ref[0] == 0)
        def _():
            wide_out(gate_s, 0, side, 0)
            wide_out(up_s, 0, middle_row, side * hidden_blocks)

        @pl.when(which_ref[0] == 1)
        def _():
            wide_out(up_s, middle_row, side, 0)
            product = dot(inner_s[...], grads_ref[...], 0, 0).astype(LOW)
            for half in range(2):
                for column in range(side):
                    held[middle_row * hidden_blocks + (2 * step + half) * side + column] = product[
                        half * BS : (half + 1) * BS, column * BS : (column + 1) * BS
                    ]

        @pl.when(step == pl.num_programs(0) - 1)
        def _():
            copies = []
            for target, group in zip(outs, sizes):
                first = 0
                for size in group:
                    number = len(copies)
                    source = held.at[pl.ds(places_ref[number] * size, size)]
                    into = target.at[pl.ds(first, size)]
                    copies.append(pltpu.make_async_copy(source, into, done.at[number]))
                    first += size
            for copy in copies:
                copy.start()
            for copy in copies:
                copy.wait()

    fixed = pl.BlockSpec((rows, D), lambda step: (0, 0))
    hidden = pl.BlockSpec((rows, TILE), lambda step: (0, step))
    return pl.pallas_call(
        kernel,
        grid=(hidden_blocks // 2,),
        in_specs=[smem_spec(), smem_spec(), fixed, fixed] + [hidden] * 3,
        out_specs=[pl.BlockSpec(memory_space=pl.ANY)] * count,
        out_shape=[jax.ShapeDtypeStruct((sum(group), BS, BS), LOW) for group in sizes],
        scratch_shapes=[
            pltpu.VMEM((D, rows), LOW),
            pltpu.VMEM((total_blocks, BS, BS), LOW),
            pltpu.SemaphoreType.DMA((pieces,)),
        ],
        compiler_params=params(),
        cost_estimate=pl.CostEstimate(
            flops=3 * rows * D * hidden_blocks * BS,
            bytes_accessed=6 * D * hidden_blocks * BS + 6 * rows * D,
            transcendentals=0,
        ),
        name="expert_half_grads",
    )(which, places, rows_in, grads_in, gate_grads, up_grads, inner)


def split_low(values):
    high = values.astype(LOW)
    return high, (values - high.astype(F32)).astype(LOW)


def renew(gradient, weights, left, right, left_root, right_root, rate):
    short = gradient.astype(LOW)
    left_new = STAT_DECAY * left + (1.0 - STAT_DECAY) * dot(short, short, 1, 1)
    right_new = STAT_DECAY * right + (1.0 - STAT_DECAY) * dot(short, short, 0, 0)
    high, rest = split_low(right_root)
    turned = (dot(short, high) + dot(short, rest)).astype(LOW)
    high, rest = split_low(left_root)
    direction = dot(high, turned) + dot(rest, turned)
    return (gradient, left_new, right_new, weights.astype(F32) - rate * direction)


def block_width(count):
    return 4 if count % 4 == 0 else 3 if count % 3 == 0 else 1


def shampoo_half(half, gradients, stats, filled):
    parts = len(gradients)
    count = gradients[0].shape[0]
    width = block_width(count)
    steps = count // width
    spec = pl.BlockSpec((width, BS, BS), lambda step, half: (half[0] * steps + step, 0, 0))
    grad_spec = pl.BlockSpec((width, BS, BS), lambda step, half: (step, 0, 0))

    def kernel(half_ref, *refs):
        for number in range(width):
            total = refs[0][number].astype(F32)
            for ref in refs[1:parts]:
                total = total + ref[number].astype(F32)
            now = [ref[number] for ref in refs[parts : parts + 5]]
            results = renew(total, *now, RATE_EXPERT)
            for target, result in zip(refs[-4:], results):
                target[number] = result

    shape = jax.ShapeDtypeStruct(stats[0].shape, F32)
    extra = list(filled or ())
    return pl.pallas_call(
        kernel,
        grid_spec=pltpu.PrefetchScalarGridSpec(
            num_scalar_prefetch=1,
            grid=(steps,),
            in_specs=[grad_spec] * parts
            + [spec] * 5
            + [pl.BlockSpec(memory_space=pl.ANY)] * len(extra),
            out_specs=[spec] * 4,
        ),
        out_shape=[shape] * 4,
        input_output_aliases={6 + parts + number: number for number in range(len(extra))},
        compiler_params=params(),
        cost_estimate=pl.CostEstimate(
            flops=count * 24 * BS * BS * BS,
            bytes_accessed=count * BS * BS * (34 + 2 * parts),
            transcendentals=0,
        ),
        name="shampoo_half",
    )(half, *gradients, *stats, *extra)


def shampoo(rates, gradient, stats):
    count = gradient.shape[0]
    width = block_width(count)
    spec = pl.BlockSpec((width, BS, BS), lambda step: (step, 0, 0))
    shape = jax.ShapeDtypeStruct((count, BS, BS), F32)

    def kernel(rates_ref, *refs):
        step = pl.program_id(0)
        for number in range(width):
            gradient_now, *stats_now = [ref[number] for ref in refs[:6]]
            results = renew(
                gradient_now.astype(F32), *stats_now, rates_ref[step * width + number]
            )
            for target, result in zip(refs[6:], results):
                target[number] = result

    return pl.pallas_call(
        kernel,
        grid=(count // width,),
        in_specs=[smem_spec()] + [spec] * 6,
        out_specs=[spec] * 4,
        out_shape=[shape] * 4,
        compiler_params=params(),
        cost_estimate=pl.CostEstimate(
            flops=count * 24 * BS * BS * BS,
            bytes_accessed=count * BS * BS * 38,
            transcendentals=0,
        ),
        name="shampoo_blocks",
    )(rates, gradient, *stats)


def shampoo_panel(turn, places, panels, stats):
    groups = len(panels)
    panel_rows = panels[0].shape[0]
    parts = 3
    breadth = groups * GROUP_WIDTH
    count = stats[0].shape[0]
    width = block_width(count)
    spec = pl.BlockSpec((width, BS, BS), lambda step, turn, places: (step, 0, 0))
    fixed = pl.BlockSpec(panels[0].shape, lambda step, turn, places: (0, 0))
    shape = jax.ShapeDtypeStruct((count, BS, BS), F32)
    per_part = breadth // BS
    per_row = parts * per_part
    side = D // BS

    def kernel(turn_ref, places_ref, *refs):
        step = pl.program_id(0)
        panel_refs = refs[:groups]
        stat_refs = refs[groups : groups + 5]
        outs = refs[groups + 5 : groups + 9]
        ordered, matrix = refs[groups + 9 :]

        @pl.when(step == 0)
        def _():
            for number, panel in enumerate(panel_refs):
                ordered[places_ref[number]] = panel[...]
            for part in range(parts):
                matrix[:, part * breadth : (part + 1) * breadth] = jnp.concatenate(
                    [
                        ordered[group, :, part * GROUP_WIDTH : (part + 1) * GROUP_WIDTH].astype(F32)
                        for group in range(groups)
                    ],
                    axis=1,
                )

        turned = turn_ref[0] == 1
        rate = jnp.where(turned, RATE_OUTPUT, RATE_PROJECT).astype(F32)
        for number in range(width):
            block = step * width + number
            row_now = jnp.where(turned, block % side % 2, block // per_row)
            column_now = jnp.where(
                turned, block % side // 2 * per_part + block // side, block % per_row
            )
            found = matrix[
                pl.ds(pl.multiple_of(row_now * BS, BS), BS),
                pl.ds(pl.multiple_of(column_now * BS, BS), BS),
            ]
            found = jnp.where(turned, found.T, found)
            results = renew(found, *[ref[number] for ref in stat_refs], rate)
            for target, result in zip(outs, results):
                target[number] = result

    return pl.pallas_call(
        kernel,
        grid_spec=pltpu.PrefetchScalarGridSpec(
            num_scalar_prefetch=2,
            grid=(count // width,),
            in_specs=[fixed] * groups + [spec] * 5,
            out_specs=[spec] * 4,
            scratch_shapes=[
                pltpu.VMEM((groups, *panels[0].shape), LOW),
                pltpu.VMEM((panel_rows, parts * breadth), F32),
            ],
        ),
        out_shape=[shape] * 4,
        compiler_params=params(),
        cost_estimate=pl.CostEstimate(
            flops=count * 24 * BS * BS * BS,
            bytes_accessed=count * BS * BS * 38,
            transcendentals=0,
        ),
        name="shampoo_panel",
    )(turn, places, *panels, *stats)


def shampoo_small(weights, gradient, left_stat, right_stat, left_root, right_root, step_rates):
    left_new = STAT_DECAY * left_stat + (1.0 - STAT_DECAY) * jnp.einsum(
        "nij,nkj->nik", gradient, gradient, precision=PRECISE
    )
    right_new = STAT_DECAY * right_stat + (1.0 - STAT_DECAY) * jnp.einsum(
        "nji,njk->nik", gradient, gradient, precision=PRECISE
    )
    turned = jnp.einsum("nij,njk->nik", gradient, right_root, precision=PRECISE)
    direction = jnp.einsum("nij,njk->nik", left_root, turned, precision=PRECISE)
    return (left_new, right_new, weights - step_rates * direction)


def shifted(values, axis, size, distance):
    return lax.ppermute(values, axis, [(i, (i + distance) % size) for i in range(size)])


def crossed(values, axes, size, distance):
    return lax.ppermute(values, axes, [(i, i ^ distance) for i in range(size)])


def direct_sum(values, axes, size):
    terms = [values] + [crossed(values, axes, size, step) for step in range(1, size)]
    while len(terms) > 1:
        terms = [terms[at] + terms[at + 1] for at in range(0, len(terms), 2)]
    return terms[0]


def everywhere_sum(values, sizes):
    a_size, b_size, c_size, f_size = sizes
    values = direct_sum(values, "f", f_size)
    values = direct_sum(values, "c", c_size)
    return direct_sum(values, ("a", "b"), a_size * b_size)


def body(
    sizes,
    inputs,
    out_grad,
    vectors,
    block_order,
    seq_lengths,
    expert_ids,
    attn_weights,
    attn_left,
    attn_right,
    attn_left_root,
    attn_right_root,
    expert_weights,
    expert_left,
    expert_right,
    expert_left_root,
    expert_right_root,
    router_weights,
    router_left,
    router_right,
    router_left_root,
    router_right_root,
):
    a_size, b_size, c_size, f_size = sizes
    rows = inputs.shape[0]
    capacity = rows // 4
    tokens_all = rows * a_size * b_size * c_size * f_size
    per_side = D // BS
    project_blocks = 3 * per_side * per_side
    a_place = lax.axis_index("a")
    c_place = lax.axis_index("c")
    f_place = lax.axis_index("f")
    per_device = attn_weights.shape[0]
    per = expert_weights.shape[1]
    shares = b_size * c_size
    local_slices = expert_weights.shape[0]

    by_panels = f_size == 4 and c_size == 2 and a_size == 2
    ends = jnp.cumsum(seq_lengths[0]).astype(jnp.int32)
    order = block_order[0].reshape(a_size * b_size, c_size, SLOTS)
    kpb = jnp.stack(
        [
            lax.dynamic_index_in_dim(order, (c_place - step) % c_size, 1, False).reshape(-1)
            for step in range(c_size)
        ]
    )

    split_count = expert_weights.shape[0] * f_size // EXPERTS
    numbers = jnp.arange(EXPERTS, dtype=jnp.int32)
    spots = (numbers % a_size) * f_size + numbers // a_size if split_count == 1 else numbers
    route_count = EXPERTS + ZEROS
    named = expert_ids[:, :, None] == jnp.arange(route_count, dtype=jnp.int32)[None, None, :]
    route_member = named.astype(F32)
    chosen = jnp.any(named[:, :, :EXPERTS], axis=1).astype(LOW)
    row_numbers = jnp.arange(rows, dtype=jnp.int32)
    before = (row_numbers[None, :] < row_numbers[:, None]).astype(LOW)
    ranks = jnp.dot(before, chosen, preferred_element_type=F32).astype(jnp.int32)
    slots = jnp.sum(
        jnp.where(named[:, :, :EXPERTS], (spots * capacity)[None, None, :] + ranks[:, None, :], 0),
        axis=2,
    )
    slots = jnp.where(expert_ids < EXPERTS, slots, -1)
    slot_numbers = jnp.arange(EXPERTS * capacity, dtype=jnp.int32)
    picks = [
        (slot_numbers[:, None] == slots[:, which][None, :]).astype(LOW) for which in range(2)
    ]
    picks_both = picks[0] + picks[1]

    def to_owners(buffer):
        buffer = buffer.astype(LOW).reshape(EXPERTS, capacity, D)
        if split_count > 1:
            buffer = jnp.repeat(buffer, split_count, axis=0)
        arrived = lax.all_to_all(buffer, ("a", "f"), split_axis=0, concat_axis=0, tiled=True)
        return arrived.reshape(-1, D)

    def return_rows(results):
        return lax.all_to_all(
            results.reshape(EXPERTS * split_count, -1, D),
            ("a", "f"),
            split_axis=0,
            concat_axis=0,
            tiled=True,
        )

    def from_owners(back, pick_matrices):
        back = back.reshape(EXPERTS, split_count, capacity, D)
        return [
            sum(
                dot(matrix, back[:, part].reshape(-1, D), 0, 0) for part in range(split_count)
            )
            for matrix in pick_matrices
        ]

    tie = lax.optimization_barrier
    share_place = lax.axis_index(("b", "c"))

    def over_groups(values):
        return lax.all_to_all(values, ("a", "b"), split_axis=0, concat_axis=0, tiled=True)

    def over_b(values):
        return crossed(values, "b", b_size, 1)

    def over_c(values):
        return crossed(values, "c", c_size, 1)

    if by_panels:
        group_place = lax.axis_index(("a", "b"))
        share_places = jnp.stack([share_place ^ step for step in range(shares)])
        first_spots, other_spots = a_place * shares + share_places, (
            (1 - a_place) * shares + share_places
        )

        def halves(values):
            return [values[: per // 2], values[per // 2 :]]

        own = jnp.where(a_place == 0, expert_weights[0], expert_weights[1])
        own_halves = halves(own)
        sent = jnp.where(a_place == 0, expert_weights[1], expert_weights[0])
        cuts = [slice(0, per // 2), slice(per // 2, per * 3 // 4), slice(per * 3 // 4, per)]
        across = crossed(attn_weights, "f", f_size, 2)
        own_c = over_c(own)
        got = [shifted(sent[cuts[0]], "a", 2, 1), None]
        own_b = [over_b(own_halves[0]), None]

        def both(spot):
            return [2 * spot, 2 * spot + 1]

        weight_places = [first_spots[0], first_spots[1]] + both(first_spots[2])
        weight_places += both(first_spots[3]) + both(other_spots[0]) + both(other_spots[1])
        weight_places += both(other_spots[2]) + both(other_spots[3])
        weight_places = jnp.stack(weight_places).astype(jnp.int32)
        kept_places = jnp.stack([share_places[step] for step in (0, 2, 1, 3)])
        given_places = [share_places[0], 2 * share_places[1], 2 * share_places[3]]
        given_places += [2 * share_places[2] + 1, 2 * share_places[3] + 1]
        given_places += [2 * share_places[2], 2 * share_places[1] + 1]
        kept_places = kept_places.astype(jnp.int32)
        given_places = jnp.stack(given_places).astype(jnp.int32)
        group_places = jnp.stack([group_place ^ step for step in range(HEAD_GROUPS)])
        group_places = group_places.astype(jnp.int32)
        shard_places = jnp.stack([f_place ^ step for step in range(f_size)]).astype(jnp.int32)
        (across, own_c, got[0], own_b[0], kpb, ends, *tables) = tie(
            (across, own_c, got[0], own_b[0], kpb, ends)
            + (weight_places, kept_places, given_places, group_places, shard_places)
        )
        weight_places, kept_places, given_places, group_places, shard_places = tables
        shards = [
            attn_weights,
            crossed(attn_weights, "f", f_size, 1),
            across,
            crossed(across, "f", f_size, 1),
        ]
        first_low, first_factor, own_queries, own_pairs, w_project = project_kernel(
            inputs, vectors[0:1], shard_places, shards
        )
        w_project = w_project.reshape(D, 3 * D)
        own_pairs, got_next = tie((own_pairs, shifted(sent[cuts[1]], "a", 2, 1)))
        own_b[1] = over_b(own_halves[1])
        own_bc = [over_c(own_b[0]), None]
        got_c = [over_c(got[0]), None]
        mine, own_b[1], own_bc[0], got_c[0] = tie(
            (over_groups(own_pairs), own_b[1], own_bc[0], got_c[0])
        )
        other = over_c(mine)
        queries = over_groups(own_queries)
        got_last = shifted(tie((sent[cuts[2]], mine))[0], "a", 2, 1)
        queries, other, got_last = tie((queries, other, got_last))
        got[1] = jnp.concatenate([got_next, got_last], axis=0)
        pairs = [mine, other]
        first_sent, own_b1, got_0, got_1 = tie((first_low, own_b[1], *got, queries))[:4]
        first_parts = [first_low, None, crossed(first_sent, ("a", "b"), HEAD_GROUPS, 2), None]
        own_bc[1] = over_c(own_b1)
        got_c[1] = over_c(got_1)
        got_b = [over_b(got_0), None]
        w_output = shards[3]
        for step in range(f_size - 1):
            w_output = jnp.where(f_place == 3 - step, shards[step], w_output)
        w_output = to_matrix(w_output, D, D)
        raw, low, lse = attend(kpb, ends, queries, pairs)
        raw, low, lse, first_parts[2], own_bc[1], got_c[1], got_b[0] = tie(
            (raw, low, lse, first_parts[2], own_bc[1], got_c[1], got_b[0])
        )
        got_b[1] = over_b(tie((got[1], low))[0])
    else:
        attn_all = lax.all_gather(attn_weights, "f", axis=0, tiled=True)
        w_project = to_matrix(attn_all[:project_blocks], D, 3 * D)
        w_output = to_matrix(attn_all[project_blocks:], D, D)
        first_norm, first_factor = normalize_parts(inputs, vectors[0])
        first_low = first_norm.astype(LOW)
        projected = jnp.dot(first_low, w_project, preferred_element_type=F32).astype(LOW)
        by_part = projected.reshape(rows, 3, HEAD_GROUPS, GROUP_WIDTH)
        own_queries = by_part[:, 0].transpose(1, 0, 2)
        own_pairs = (
            by_part[:, 1:].transpose(2, 0, 1, 3).reshape(HEAD_GROUPS, rows, 2 * GROUP_WIDTH)
        )
        mine = over_groups(own_pairs)
        pairs = [mine] + [shifted(mine, "c", c_size, step) for step in range(1, c_size)]
        queries = over_groups(pack_rows(own_queries))
        raw, low, lse = attend(kpb, ends, queries, pairs)
        weight_places = jnp.arange(local_slices, dtype=jnp.int32)
        weight_shares = [
            lax.all_gather(expert_weights[number], ("b", "c"), axis=0, tiled=True)
            for number in range(local_slices)
        ]
        weights = (weight_places, weight_shares)
    by_heads = unpack_rows(over_groups(low))
    attended = by_heads.transpose(1, 0, 2).reshape(rows, D)
    middle = inputs + jnp.dot(attended, w_output, preferred_element_type=F32)
    second, second_factor = normalize_parts(middle, vectors[1])
    second_low = second.astype(LOW)
    if by_panels:
        second_low, got_b[1] = tie((second_low, got_b[1]))
        first_sent, *got_bc = tie((first_low, *got_b, second_low))[:3]
        first_parts[1] = crossed(first_sent, ("a", "b"), HEAD_GROUPS, 1)
        got_bc = [over_c(part) for part in got_bc]

    logits = jnp.dot(second_low, router_weights, preferred_element_type=F32)
    picked_logits = jnp.sum(jnp.where(named, logits[:, None, :], 0.0), axis=2)
    route_gates = jax.nn.softmax(picked_logits, axis=-1)
    received = to_owners(dot(picks_both, second_low))
    grad_rows = [
        (route_gates[:, which][:, None] * out_grad).astype(LOW) for which in range(2)
    ]
    if by_panels:
        grad_rows[0], first_parts[1], *got_bc = tie((grad_rows[0], first_parts[1], *got_bc))
    arrived = to_owners(dot(picks[0], grad_rows[0]) + dot(picks[1], grad_rows[1]))
    if by_panels:
        weight_shares = [own, own_c, *own_b, *own_bc, *got, *got_c, *got_b, *got_bc]
        weights = (weight_places, weight_shares)
    result, gate_kept, up_kept, inner = expert_forward(received, weights)
    result = return_rows(result)
    back_rows, gate_grads, up_grads = expert_row_grads(arrived, gate_kept, up_kept, weights)
    if by_panels:
        full, part = per, per // 2
        half = a_place.astype(jnp.int32).reshape(1)
        given, hop_c, hop_b, near_b, near_c = expert_half_grads(
            1 - half,
            given_places,
            received,
            arrived,
            gate_grads,
            up_grads,
            inner,
            [(full,), (part, part), (part, part), (part,), (part,)],
        )
        first_parts[3] = over_b(tie((first_parts[2], arrived))[0])
        back_rows, result, near_b, gate_grads, up_grads, first_parts[3] = tie(
            (back_rows, result, near_b, gate_grads, up_grads, first_parts[3])
        )
        back_rows = return_rows(back_rows)
        kept, kept_far, kept_near, kept_next = expert_half_grads(
            half,
            kept_places,
            received,
            arrived,
            gate_grads,
            up_grads,
            inner,
            [(full,)] * 4,
        )
        back_rows, kept = tie((back_rows, kept))
        hop_c, hop_b = over_c(hop_c), over_b(hop_b)
    else:
        back_rows = return_rows(back_rows)
        grad_shares = expert_weight_grads(
            jnp.arange(shares, dtype=jnp.int32),
            received,
            arrived,
            gate_grads,
            up_grads,
            inner,
            [(per,)] * shares,
        )
    expert_rows = jnp.stack(from_owners(result, picks), axis=1)
    const_member = route_member[:, :, EXPERTS + 2 :]
    copy_member = route_member[:, :, EXPERTS + 1]
    route_values = (
        expert_rows
        + copy_member[:, :, None] * second[:, None, :]
        + jnp.einsum("rkc,cd->rkd", const_member, vectors[2:], precision=PRECISE)
    )
    output = middle + jnp.sum(route_gates[:, :, None] * route_values, axis=1)

    gate_grad = jnp.sum(out_grad[:, None, :] * route_values, axis=2)
    picked_grad = route_gates * (
        gate_grad - jnp.sum(route_gates * gate_grad, axis=1, keepdims=True)
    )
    logit_grad = jnp.sum(route_member * picked_grad[:, :, None], axis=1)
    router_local = lax.dot_general(
        logit_grad, second_low.astype(F32), (((0,), (0,)), ((), ())), precision=PRECISE
    )
    second_grad = jnp.dot(logit_grad, router_weights.astype(F32).T, precision=PRECISE)
    second_grad = second_grad + jnp.sum(route_gates * copy_member, axis=1)[:, None] * out_grad
    const_grad = jnp.einsum("rkc,rk,rd->cd", const_member, route_gates, out_grad, precision=PRECISE)
    second_grad = second_grad + from_owners(back_rows, [picks_both])[0]
    middle_part, second_gain_grad = normalize_back(middle, second_factor, vectors[1], second_grad)
    middle_grad = out_grad + middle_part
    middle_low = middle_grad.astype(LOW)

    flat = (-1, BS, BS)
    expert_stats = [
        item.reshape(flat)
        for item in (
            expert_weights,
            expert_left,
            expert_right,
            expert_left_root,
            expert_right_root,
        )
    ]

    attended_grad = dot(middle_low, w_output, 1, 1).astype(LOW)
    attended_grad = attended_grad.reshape(rows, HEAD_GROUPS, GROUP_WIDTH).transpose(1, 0, 2)
    attended_grad = over_groups(pack_rows(attended_grad))
    if by_panels:
        hop_c, hop_b = tie((hop_c, hop_b, middle_low))[:2]
        given_b = over_b((near_b.astype(F32) + hop_c[part:].astype(F32)).astype(LOW))
        given_c = (near_c.astype(F32) + hop_b[part:].astype(F32)).astype(LOW)
        kept_next = over_c(tie((kept_next, given_c))[0])
        given_c = over_c(given_c)
        early = jnp.concatenate([router_local, second_gain_grad[None], const_grad], axis=0)
        early = direct_sum(early, "f", f_size)
        early = direct_sum(early, ("a", "b"), HEAD_GROUPS)
        attended_grad, given_b, given_c, kept_next, early = tie(
            (attended_grad, given_b, given_c, kept_next, early)
        )
        kept_b = over_b((kept_far.astype(F32) + kept_next.astype(F32)).astype(LOW))
        taken = jnp.concatenate(
            [
                given[:part].astype(F32) + hop_c[:part].astype(F32) + given_b.astype(F32),
                given[part:].astype(F32) + hop_b[:part].astype(F32) + given_c.astype(F32),
            ],
            axis=0,
        )
        taken = shifted(taken.astype(LOW), "a", 2, 1)
        kept_near = over_c(tie((kept_near, attended_grad))[0])
    back_outs = attend_back(kpb, ends, queries, pairs, attended_grad, raw, lse)
    if by_panels:
        sent_outs = back_outs
        *back_outs, kept_near, taken, kept_b = tie((*back_outs, kept_near, taken, kept_b))
        middle_late = tie((middle_low, back_outs[0]))[0]
        output_panels = jnp.einsum(
            "hrj,rd->hdj", by_heads, middle_late, preferred_element_type=F32
        ).astype(LOW)
        output_panels = over_groups(output_panels)
        expert_outs = shampoo_half(1 - half, [taken], expert_stats, None)
        first_parts = tie((*first_parts, back_outs[0]))[:HEAD_GROUPS]
        first_all = jnp.zeros((HEAD_GROUPS, rows, D), LOW)
        for step, part_rows in enumerate(first_parts):
            first_all = lax.dynamic_update_index_in_dim(
                first_all, part_rows, group_place ^ step, 0
            )
        first_all = first_all.reshape(-1, D)
    query_grad, pair_grad = back_outs[:2]
    for step in range(1, c_size):
        sent = sent_outs if by_panels else back_outs
        pair_grad = pair_grad + shifted(sent[1 + step], "c", c_size, -step).astype(F32)
    group_grad = jnp.concatenate([query_grad, pair_grad.astype(LOW)], axis=2)
    if by_panels:
        group_grad, output_panels, first_all, *expert_outs = tie(
            (group_grad, output_panels, first_all, *expert_outs)
        )
    if by_panels:
        panels = dot(first_all, group_grad.reshape(-1, 3 * GROUP_WIDTH), 0, 0).astype(LOW)
        group_grad, panels = tie((group_grad, panels))
    project_grad = over_groups(group_grad)
    if by_panels:
        panels = panels.reshape(3, D // 3, 3 * GROUP_WIDTH)
        output_panels = jnp.sum(output_panels.astype(F32), axis=0).astype(LOW)
        output_panels = (
            output_panels.reshape(3, D // 3, GROUP_WIDTH)
            .transpose(1, 0, 2)
            .reshape(1, D // 3, 3 * GROUP_WIDTH)
        )
        panels = jnp.concatenate([panels, output_panels], axis=0)
        own_panels = [
            lax.dynamic_index_in_dim(panels, f_place ^ step, 0, False) for step in range(f_size)
        ]
        summed = own_panels[0].astype(F32)
        for step in range(1, f_size):
            summed = summed + crossed(own_panels[step], "f", f_size, step).astype(F32)
        summed = summed.astype(LOW)
        summed = (summed.astype(F32) + crossed(summed, "c", 2, 1).astype(F32)).astype(LOW)
        group_panels = [
            crossed(summed, ("a", "b"), HEAD_GROUPS, step) for step in range(1, HEAD_GROUPS)
        ]
        early = direct_sum(tie((early, summed))[0], "c", c_size)
        project_grad, *group_panels = tie((project_grad, *group_panels))
    project_grad = (
        project_grad.reshape(HEAD_GROUPS, rows, 3, GROUP_WIDTH)
        .transpose(1, 2, 0, 3)
        .reshape(rows, 3 * D)
    )
    first_grad = dot(project_grad, w_project, 1, 1)
    input_part, first_gain_grad = normalize_back(inputs, first_factor, vectors[0], first_grad)
    input_grad = middle_grad + input_part

    everywhere = ("a", "b", "c", "f")
    if not by_panels:
        early = jnp.concatenate([router_local, second_gain_grad[None], const_grad], axis=0)
        early = everywhere_sum(early, sizes)
    late = direct_sum(first_gain_grad[None], "f", f_size)
    late = direct_sum(late, "c", c_size)

    attn_stats = (attn_weights, attn_left, attn_right, attn_left_root, attn_right_root)
    if by_panels:
        kept = [tie((kept, summed))[0], kept_near, kept_b]
        expert_outs = shampoo_half(half, kept, expert_stats, expert_outs)
        turn = (f_place == 3).astype(jnp.int32).reshape(1)
        attn_outs = shampoo_panel(
            turn, group_places, [summed, *group_panels], attn_stats
        )
    else:
        output_weight_grad = dot(attended, middle_low, 0, 0)
        project_weight_grad = dot(first_low, project_grad, 0, 0)
        attn_local = jnp.concatenate(
            [to_blocks(project_weight_grad, BS, BS), to_blocks(output_weight_grad, BS, BS)],
            axis=0,
        )
        attn_sum = lax.psum(attn_local, everywhere)
        attn_gradient = lax.dynamic_slice_in_dim(attn_sum, f_place * per_device, per_device, 0)
        block_numbers = f_place * per_device + jnp.arange(per_device, dtype=jnp.int32)
        attn_rates = jnp.where(block_numbers < project_blocks, RATE_PROJECT, RATE_OUTPUT)
        attn_outs = shampoo(attn_rates.astype(F32), attn_gradient, attn_stats)
        expert_gradient = lax.psum_scatter(
            jnp.concatenate(grad_shares, axis=0).reshape(local_slices, -1, BS, BS).astype(F32),
            ("b", "c"),
            scatter_dimension=1,
            tiled=True,
        ).reshape(flat)
        expert_outs = shampoo(
            jnp.full((expert_gradient.shape[0],), RATE_EXPERT, F32), expert_gradient, expert_stats
        )
    expert_grads, expert_left_new, expert_right_new, expert_new = [
        item.reshape(expert_weights.shape) for item in expert_outs
    ]
    late, *attn_outs = tie((late, *attn_outs))
    late = direct_sum(late, ("a", "b"), a_size * b_size)
    attn_grads, attn_left_new, attn_right_new, attn_new = attn_outs
    router_grads = early[:route_count].T
    vector_grads = jnp.concatenate([late, early[route_count:]], axis=0)
    router_left_new, router_right_new, router_moved = shampoo_small(
        to_blocks(router_weights.astype(F32), BS, route_count),
        to_blocks(router_grads, BS, route_count),
        router_left,
        router_right,
        router_left_root,
        router_right_root,
        RATE_ROUTER,
    )
    router_new = to_matrix(router_moved, D, route_count)
    vector_new = vectors - RATE_VECTOR * float(tokens_all) ** (-0.5) * vector_grads
    return (
        output,
        input_grad,
        vector_grads,
        vector_new,
        attn_grads,
        attn_left_new,
        attn_right_new,
        attn_new,
        expert_grads,
        expert_left_new,
        expert_right_new,
        expert_new,
        router_grads,
        router_left_new,
        router_right_new,
        router_new,
    )


def solution(mesh):
    ctx_size = mesh.shape["ctx"]
    f_size = mesh.shape["fsdp"]
    context = ("a", "b", "c")
    token_rows = P(context + ("f",), None)
    group_rows = P("f", None)
    attn = P("f", None, None)
    expert = P("f", context, None, None)
    in_specs = (
        (token_rows, token_rows, P(), group_rows, group_rows, token_rows)
        + (attn,) * 5
        + (expert,) * 5
        + (P(),) * 5
    )
    out_specs = (token_rows, token_rows, P(), P()) + (attn,) * 4 + (expert,) * 4 + (P(),) * 4

    def run(*arrays):
        local_slices = arrays[11].shape[0] // f_size
        a_size = 2 if local_slices == 2 else 1
        b_size = HEAD_GROUPS // a_size
        c_size = ctx_size // HEAD_GROUPS
        sizes = (a_size, b_size, c_size, f_size)
        fine_mesh = jax.sharding.Mesh(mesh.devices.reshape(sizes), ("a", "b", "c", "f"))
        return jax.shard_map(
            functools.partial(body, sizes),
            mesh=fine_mesh,
            in_specs=in_specs,
            out_specs=out_specs,
            check_vma=False,
        )(*arrays)

    return run
```

```python
import functools

import jax
import jax.numpy as jnp
from jax import lax
from jax.experimental import pallas as pl
from jax.experimental.pallas import tpu as pltpu
from jax.sharding import PartitionSpec as P

D = 768
HEADS = 12
HDIM = 64
EXPERTS = 8
ZEROS = 4
BS = 128
SLOTS = 4
HEAD_GROUPS = 4
GROUP_WIDTH = HEADS // HEAD_GROUPS * HDIM
GROUP_HEADS = HEADS // HEAD_GROUPS
CHUNK = 256
TILE = 256
SUB = 32

EPSILON = 1e-06
SCORE_SCALE = 0.125
STAT_DECAY = 0.5
RATE_PROJECT = 0.4
RATE_OUTPUT = 3.0
RATE_EXPERT = 0.4
RATE_ROUTER = 0.2
RATE_VECTOR = 0.1
MASKED_SCORE = -1e30
PRECISE = lax.Precision.HIGHEST
F32 = jnp.float32
LOW = jnp.bfloat16
VMEM_LIMIT = 56 * 1024 * 1024


def to_matrix(blocks, height, breadth):
    block_height = blocks.shape[1]
    block_breadth = blocks.shape[2]
    shaped = blocks.reshape(
        height // block_height, breadth // block_breadth, block_height, block_breadth
    )
    return shaped.transpose(0, 2, 1, 3).reshape(height, breadth)


def to_blocks(matrix, block_height, block_breadth):
    height = matrix.shape[0]
    breadth = matrix.shape[1]
    shaped = matrix.reshape(
        height // block_height, block_height, breadth // block_breadth, block_breadth
    )
    return shaped.transpose(0, 2, 1, 3).reshape(-1, block_height, block_breadth)


def normalize_parts(values, scaling):
    factor = lax.rsqrt(jnp.mean(values * values, axis=-1, keepdims=True) + EPSILON)
    return (values * factor * scaling, factor)


def normalize_back(values, factor, scaling, gradient):
    unit_rows = values * factor
    scaled = gradient * scaling
    value_grad = factor * (
        scaled - unit_rows * jnp.mean(scaled * unit_rows, axis=-1, keepdims=True)
    )
    return (value_grad, jnp.sum(gradient * unit_rows, axis=0))


def dot(left, right, left_dim=1, right_dim=0):
    return lax.dot_general(
        left, right, (((left_dim,), (right_dim,)), ((), ())), preferred_element_type=F32
    )


def vmem_spec():
    return pl.BlockSpec(memory_space=pltpu.VMEM)


def smem_spec():
    return pl.BlockSpec(memory_space=pltpu.SMEM)


def params():
    return pltpu.CompilerParams(vmem_limit_bytes=VMEM_LIMIT)


def project_kernel(rows_in, gain, places, shards):
    rows = rows_in.shape[0]
    owners = len(shards) - 1
    depth = D // owners
    breadth = 3 * D
    block_rows = depth // BS
    block_columns = breadth // BS
    pair = 2 * GROUP_WIDTH

    def kernel(places_ref, rows_ref, gain_ref, *refs):
        shard_refs = refs[: owners + 1]
        first_out, factor_out, query_out, pair_out, matrix, first_s = refs[owners + 1 :]
        for number, shard in enumerate(shard_refs):
            owner = places_ref[number]

            @pl.when(owner < owners)
            def _(owner=owner, shard=shard):
                for row in range(block_rows):
                    for column in range(block_columns):
                        matrix[
                            owner, row * BS : (row + 1) * BS, column * BS : (column + 1) * BS
                        ] = shard[row * block_columns + column]

        def norm(tile, carry):
            at = pl.ds(pl.multiple_of(tile * SUB, SUB), SUB)
            values = rows_ref[at, :]
            factor = lax.rsqrt(jnp.mean(values * values, axis=1, keepdims=True) + EPSILON)
            first = (values * factor * gain_ref[...]).astype(LOW)
            factor_out[at, :] = factor
            first_out[at, :] = first
            for owner in range(owners):
                first_s[owner, at, :] = first[:, owner * depth : (owner + 1) * depth]
            return carry

        lax.fori_loop(0, rows // SUB, norm, 0)
        for tile in range(breadth // pair):
            at = slice(tile * pair, (tile + 1) * pair)
            total = dot(first_s[0], matrix[0, :, at])
            for owner in range(1, owners):
                total = total + dot(first_s[owner], matrix[owner, :, at])
            total = total.astype(LOW)
            part = tile * pair // D
            group = tile * pair % D // GROUP_WIDTH
            for side in range(2):
                piece = total[:, side * GROUP_WIDTH : (side + 1) * GROUP_WIDTH]
                if part == 0:
                    query_out[group + side] = jnp.concatenate(
                        [piece[: rows // 2], piece[rows // 2 :]], axis=1
                    )
                else:
                    pair_out[
                        group + side, :, (part - 1) * GROUP_WIDTH : part * GROUP_WIDTH
                    ] = piece

    return pl.pallas_call(
        kernel,
        in_specs=[smem_spec()] + [vmem_spec()] * (owners + 3),
        out_specs=[vmem_spec()] * 5,
        out_shape=[
            jax.ShapeDtypeStruct((rows, D), LOW),
            jax.ShapeDtypeStruct((rows, 1), F32),
            jax.ShapeDtypeStruct((HEAD_GROUPS, rows // 2, pair), LOW),
            jax.ShapeDtypeStruct((HEAD_GROUPS, rows, pair), LOW),
            jax.ShapeDtypeStruct((owners, depth, breadth), LOW),
        ],
        scratch_shapes=[pltpu.VMEM((owners, rows, depth), LOW)],
        compiler_params=params(),
        cost_estimate=pl.CostEstimate(
            flops=2 * rows * D, bytes_accessed=1_000_000, transcendentals=0
        ),
        name="project",
    )(places, rows_in, gain, *shards)


def head_masks(value):
    lane = lax.broadcasted_iota(jnp.int32, (1, GROUP_WIDTH), 1)
    return [
        jnp.where(lane // HDIM == head, value, 0.0).astype(F32) for head in range(GROUP_HEADS)
    ]


def stack_heads(rows, masks):
    return jnp.concatenate([rows * mask.astype(rows.dtype) for mask in masks], axis=0)


def packed_at(slot, block_rows):
    first_row = slot % 2 * block_rows
    first_lane = slot // 2 * GROUP_WIDTH
    return slice(first_row, first_row + block_rows), slice(first_lane, first_lane + GROUP_WIDTH)


def pack_rows(values):
    groups, rows, width = values.shape
    return values.reshape(groups, 2, rows // 2, width).transpose(0, 2, 1, 3).reshape(
        groups, rows // 2, 2 * width
    )


def unpack_rows(values):
    groups, rows, width = values.shape
    return values.reshape(groups, rows, 2, width // 2).transpose(0, 2, 1, 3).reshape(
        groups, 2 * rows, width // 2
    )


def fill_sorted(kpb, sources, key_sorted, value_sorted, block_rows, block_count):
    key_sorted[0:CHUNK, :] = jnp.zeros((CHUNK, GROUP_WIDTH), LOW)
    value_sorted[0:CHUNK, :] = jnp.zeros((CHUNK, GROUP_WIDTH), LOW)
    for number, source in enumerate(sources):

        def fill(item, carry, source=source, number=number):
            from_row = pl.multiple_of(item % SLOTS * block_rows, block_rows)
            to_row = pl.multiple_of(CHUNK + kpb[number, item] * block_rows, 32)
            rows = source[item // SLOTS, pl.ds(from_row, block_rows), :]
            key_sorted[pl.ds(to_row, block_rows), :] = rows[:, 0:GROUP_WIDTH]
            value_sorted[pl.ds(to_row, block_rows), :] = rows[:, GROUP_WIDTH:]
            return carry

        lax.fori_loop(0, block_count, fill, 0)


def list_steps(kpb, ends, sequences, block_rows, block_count, block_of, place_of):
    def one_block(item, first_step):
        first = kpb[0, item] * block_rows
        lowest = jnp.int32(0)
        for sequence in range(sequences):
            ending = ends[sequence]
            lowest = jnp.where(first >= ending, ending, lowest)
        top = first + block_rows
        count = (top - lowest + CHUNK - 1) // CHUNK

        def one_step(step, carry):
            block_of[first_step + step] = item
            place_of[first_step + step] = top - (step + 1) * CHUNK
            return carry

        lax.fori_loop(0, count, one_step, 0)
        return first_step + count

    return lax.fori_loop(0, block_count, one_block, jnp.int32(0))


def fill_limits(kpb, ends, sequences, block_rows, item, start_s, place_s):
    for tile in range(GROUP_HEADS * block_rows // SUB):
        within = tile * SUB % block_rows
        places = (
            kpb[0, item] * block_rows
            + within
            + lax.broadcasted_iota(jnp.int32, (SUB, BS), 0)
        )
        starts = jnp.zeros_like(places)
        for sequence in range(sequences):
            ending = ends[sequence]
            starts = jnp.where(places >= ending, ending, starts)
        at_rows = slice(tile * SUB, (tile + 1) * SUB)
        start_s[item, at_rows, :] = starts
        place_s[item, at_rows, :] = places


def pipeline(total, scores, middle, products):
    scores(jnp.int32(0), 0)

    def pair(number, carry):
        step = 2 * number
        scores(step + 1, 1)
        middle(step, 0)
        products(step - 1, 1)
        scores(step + 2, 0)
        middle(step + 1, 1)
        products(step, 0)
        return carry

    lax.fori_loop(0, (total + 2) // 2, pair, 0)


def tile_slices(count):
    return [slice(tile * SUB, (tile + 1) * SUB) for tile in range(count)]


def attend_kernel(sources_count, block_rows, sequences, *refs):
    kpb, ends, queries = refs[:3]
    sources = refs[3 : 3 + sources_count]
    raw_out, low_out, lse_out, key_sorted, value_sorted, query_s, start_s, place_s = refs[
        3 + sources_count : 11 + sources_count
    ]
    best_s, total_s, gathered_s, score_0, score_1, weight_0, weight_1, fade_0, fade_1 = refs[
        11 + sources_count : 20 + sources_count
    ]
    block_of, place_of = refs[20 + sources_count :]
    score_s, weight_s, fade_s = (score_0, score_1), (weight_0, weight_1), (fade_0, fade_1)
    block_count = queries.shape[0] * SLOTS
    stacked = GROUP_HEADS * block_rows
    tiles = tile_slices(stacked // SUB)
    fill_sorted(kpb, sources, key_sorted, value_sorted, block_rows, block_count)
    total = list_steps(kpb, ends, sequences, block_rows, block_count, block_of, place_of)
    masks = head_masks(SCORE_SCALE)
    plain = head_masks(1.0)

    def load(group, carry):
        for slot in range(SLOTS):
            rows, lanes = packed_at(slot, block_rows)
            query_s[group * SLOTS + slot] = stack_heads(queries[group, rows, lanes], masks)
        return carry

    lax.fori_loop(0, block_count // SLOTS, load, 0)

    def prepare(item, carry):
        fill_limits(kpb, ends, sequences, block_rows, item, start_s, place_s)
        best_s[item] = jnp.full((stacked, BS), MASKED_SCORE, F32)
        total_s[item] = jnp.zeros((stacked, BS), F32)
        gathered_s[item] = jnp.zeros((stacked, GROUP_WIDTH), F32)
        return carry

    lax.fori_loop(0, block_count, prepare, 0)
    weight_1[...] = jnp.zeros_like(weight_1)
    fade_1[...] = jnp.ones_like(fade_1)

    def find(step):
        inside = jnp.clip(step, 0, total - 1)
        return block_of[inside], place_of[inside]

    def scores(step, side):
        item, low_place = find(step)
        at = pl.multiple_of(low_place + CHUNK, 32)
        score_s[side][...] = dot(query_s[item], key_sorted[pl.ds(at, CHUNK), :], 1, 1)

    def middle(step, side):
        item, low_place = find(step)
        low_place = jnp.where(step < total, low_place, -(1 << 24))
        lanes = low_place + lax.broadcasted_iota(jnp.int32, (1, BS), 1)
        for rows in tiles:
            starts, places = start_s[item, rows, :], place_s[item, rows, :]
            parts = []
            for part in range(CHUNK // BS):
                key_places = lanes + part * BS
                allowed = (key_places >= starts) & (key_places <= places)
                found = score_s[side][rows, part * BS : (part + 1) * BS]
                parts.append(jnp.where(allowed, found, MASKED_SCORE))
            best = best_s[item, rows, :]
            top = jnp.max(functools.reduce(jnp.maximum, parts), axis=1, keepdims=True)
            peak = jnp.maximum(best, top)
            fade = jnp.exp(best - peak)
            so_far = total_s[item, rows, :] * fade
            for part, found in enumerate(parts):
                weights = jnp.exp(found - peak)
                so_far = so_far + weights
                weight_s[side][rows, part * BS : (part + 1) * BS] = weights.astype(LOW)
            best_s[item, rows, :] = peak
            total_s[item, rows, :] = so_far
            fade_s[side][rows, :] = fade

    def products(step, side):
        item, low_place = find(step)
        at = pl.multiple_of(low_place + CHUNK, 32)
        fade = fade_s[side][...]
        fade = jnp.concatenate([fade, fade[:, : GROUP_WIDTH - BS]], axis=1)
        gathered_s[item] = gathered_s[item] * fade + dot(
            weight_s[side][...], value_sorted[pl.ds(at, CHUNK), :]
        )

    pipeline(total, scores, middle, products)

    def finish(group, carry):
        for slot in range(SLOTS):
            item = group * SLOTS + slot
            rows, lanes = packed_at(slot, block_rows)
            sums = jnp.sum(total_s[item], axis=1, keepdims=True)
            gathered = gathered_s[item] / sums
            result = jnp.zeros((block_rows, GROUP_WIDTH), F32)
            for head in range(GROUP_HEADS):
                result = result + (
                    plain[head] * gathered[head * block_rows : (head + 1) * block_rows]
                )
            raw_out[group, slot * block_rows : (slot + 1) * block_rows, :] = result
            low_out[group, rows, lanes] = result.astype(LOW)
            lse_out[item] = best_s[item][:, 0:1] + jnp.log(sums)
        return carry

    lax.fori_loop(0, block_count // SLOTS, finish, 0)


def attend_sizes(queries, pairs):
    groups, rows, _ = pairs[0].shape
    block_rows = rows // SLOTS
    all_rows = groups * rows * len(pairs)
    blocks = groups * SLOTS
    stacked = GROUP_HEADS * block_rows
    return groups, rows, block_rows, all_rows, blocks, stacked


def attend(kpb, ends, queries, pairs):
    groups, rows, block_rows, all_rows, blocks, stacked = attend_sizes(queries, pairs)
    steps = blocks * (all_rows // CHUNK + 1)
    return pl.pallas_call(
        functools.partial(attend_kernel, len(pairs), block_rows, ends.shape[0]),
        in_specs=[smem_spec()] * 2 + [vmem_spec()] * (1 + len(pairs)),
        out_specs=[vmem_spec()] * 3,
        out_shape=[
            jax.ShapeDtypeStruct((groups, rows, GROUP_WIDTH), F32),
            jax.ShapeDtypeStruct((groups, rows // 2, 2 * GROUP_WIDTH), LOW),
            jax.ShapeDtypeStruct((blocks, stacked, 1), F32),
        ],
        scratch_shapes=[
            pltpu.VMEM((CHUNK + all_rows, GROUP_WIDTH), LOW),
            pltpu.VMEM((CHUNK + all_rows, GROUP_WIDTH), LOW),
            pltpu.VMEM((blocks, stacked, GROUP_WIDTH), LOW),
            pltpu.VMEM((blocks, stacked, BS), jnp.int32),
            pltpu.VMEM((blocks, stacked, BS), jnp.int32),
            pltpu.VMEM((blocks, stacked, BS), F32),
            pltpu.VMEM((blocks, stacked, BS), F32),
            pltpu.VMEM((blocks, stacked, GROUP_WIDTH), F32),
            pltpu.VMEM((stacked, CHUNK), F32),
            pltpu.VMEM((stacked, CHUNK), F32),
            pltpu.VMEM((stacked, CHUNK), LOW),
            pltpu.VMEM((stacked, CHUNK), LOW),
            pltpu.VMEM((stacked, BS), F32),
            pltpu.VMEM((stacked, BS), F32),
            pltpu.SMEM((steps,), jnp.int32),
            pltpu.SMEM((steps,), jnp.int32),
        ],
        compiler_params=params(),
        cost_estimate=pl.CostEstimate(
            flops=groups * rows * HDIM,
            bytes_accessed=1_000_000,
            transcendentals=0,
        ),
        name="attend_forward",
    )(kpb, ends, queries, *pairs)


def attend_back_kernel(sources_count, block_rows, sequences, *refs):
    kpb, ends, queries = refs[:3]
    sources = refs[3 : 3 + sources_count]
    out_grad, raw, lse = refs[3 + sources_count : 6 + sources_count]
    query_out = refs[6 + sources_count]
    pair_outs = refs[7 + sources_count : 7 + 2 * sources_count]
    rest = refs[7 + 2 * sources_count :]
    key_sorted, value_sorted, key_grad, value_grad, query_s, grad_s, query_grad = rest[:7]
    start_s, place_s, shift_s, delta_s = rest[7:11]
    score_s, back_s, weight_s, change_s = rest[11:13], rest[13:15], rest[15:17], rest[17:19]
    block_of, place_of = rest[19:]
    block_count = queries.shape[0] * SLOTS
    stacked = GROUP_HEADS * block_rows
    tiles = tile_slices(stacked // SUB)
    fill_sorted(kpb, sources, key_sorted, value_sorted, block_rows, block_count)
    total = list_steps(kpb, ends, sequences, block_rows, block_count, block_of, place_of)
    key_grad[...] = jnp.zeros_like(key_grad)
    value_grad[...] = jnp.zeros_like(value_grad)
    weight_s[1][...] = jnp.zeros_like(weight_s[1])
    change_s[1][...] = jnp.zeros_like(change_s[1])
    masks = head_masks(SCORE_SCALE)
    plain = head_masks(1.0)

    def load(group, carry):
        for slot in range(SLOTS):
            item = group * SLOTS + slot
            rows, lanes = packed_at(slot, block_rows)
            query_s[item] = stack_heads(queries[group, rows, lanes], masks)
            grad = stack_heads(out_grad[group, rows, lanes], plain)
            grad_s[item] = grad
            values = raw[group, slot * block_rows : (slot + 1) * block_rows, :]
            delta = jnp.sum(
                grad.astype(F32) * jnp.concatenate([values] * GROUP_HEADS, axis=0),
                axis=1,
                keepdims=True,
            )
            delta_s[item] = jnp.broadcast_to(delta, (stacked, BS))
        return carry

    lax.fori_loop(0, block_count // SLOTS, load, 0)

    def prepare(item, carry):
        shift_s[item] = jnp.broadcast_to(lse[item], (stacked, BS))
        query_grad[item] = jnp.zeros((stacked, GROUP_WIDTH), F32)
        fill_limits(kpb, ends, sequences, block_rows, item, start_s, place_s)
        return carry

    lax.fori_loop(0, block_count, prepare, 0)

    def find(step):
        inside = jnp.clip(step, 0, total - 1)
        return block_of[inside], place_of[inside]

    def scores(step, side):
        item, low_place = find(step)
        at = pl.ds(pl.multiple_of(low_place + CHUNK, 32), CHUNK)
        score_s[side][...] = dot(query_s[item], key_sorted[at, :], 1, 1)
        back_s[side][...] = dot(grad_s[item], value_sorted[at, :], 1, 1)

    def middle(step, side):
        item, low_place = find(step)
        low_place = jnp.where(step < total, low_place, -(1 << 24))
        lanes = low_place + lax.broadcasted_iota(jnp.int32, (1, BS), 1)
        for rows in tiles:
            starts, places = start_s[item, rows, :], place_s[item, rows, :]
            shift, delta = shift_s[item, rows, :], delta_s[item, rows, :]
            for part in range(CHUNK // BS):
                at_lanes = slice(part * BS, (part + 1) * BS)
                key_places = lanes + part * BS
                allowed = (key_places >= starts) & (key_places <= places)
                found = score_s[side][rows, at_lanes] - shift
                weights = jnp.exp(jnp.where(allowed, found, MASKED_SCORE))
                weight_s[side][rows, at_lanes] = weights.astype(LOW)
                change = weights * (back_s[side][rows, at_lanes] - delta)
                change_s[side][rows, at_lanes] = change.astype(LOW)

    def products(step, side):
        item, low_place = find(step)
        at = pl.ds(pl.multiple_of(low_place + CHUNK, 32), CHUNK)
        value_grad[at, :] += dot(weight_s[side][...], grad_s[item], 0, 0)
        key_grad[at, :] += dot(change_s[side][...], query_s[item], 0, 0)
        query_grad[item] += dot(change_s[side][...], key_sorted[at, :])

    pipeline(total, scores, middle, products)

    def finish(item, carry):
        at = pl.ds(pl.multiple_of(item % SLOTS * block_rows, block_rows), block_rows)
        result = jnp.zeros((block_rows, GROUP_WIDTH), F32)
        for head in range(GROUP_HEADS):
            result = result + masks[head] * (
                query_grad[item, head * block_rows : (head + 1) * block_rows, :]
            )
        query_out[item // SLOTS, at, :] = result.astype(LOW)
        return carry

    lax.fori_loop(0, block_count, finish, 0)
    for number, target in enumerate(pair_outs):

        def drain(item, carry, number=number, target=target):
            to_row = pl.multiple_of(item % SLOTS * block_rows, block_rows)
            from_row = pl.multiple_of(CHUNK + kpb[number, item] * block_rows, 32)
            pair = jnp.concatenate(
                [
                    key_grad[pl.ds(from_row, block_rows), :],
                    value_grad[pl.ds(from_row, block_rows), :],
                ],
                axis=1,
            )
            target[item // SLOTS, pl.ds(to_row, block_rows), :] = pair.astype(target.dtype)
            return carry

        lax.fori_loop(0, block_count, drain, 0)


def attend_back(kpb, ends, queries, pairs, out_grad, raw, lse):
    groups, rows, block_rows, all_rows, blocks, stacked = attend_sizes(queries, pairs)
    steps = blocks * (all_rows // CHUNK + 1)
    limit = pltpu.VMEM((blocks, stacked, BS), jnp.int32)
    row_values = pltpu.VMEM((blocks, stacked, BS), F32)
    sorted_low = pltpu.VMEM((CHUNK + all_rows, GROUP_WIDTH), LOW)
    sorted_sum = pltpu.VMEM((CHUNK + all_rows, GROUP_WIDTH), F32)
    stacked_low = pltpu.VMEM((blocks, stacked, GROUP_WIDTH), LOW)
    square = pltpu.VMEM((stacked, CHUNK), F32)
    square_low = pltpu.VMEM((stacked, CHUNK), LOW)
    return pl.pallas_call(
        functools.partial(attend_back_kernel, len(pairs), block_rows, ends.shape[0]),
        in_specs=[smem_spec()] * 2 + [vmem_spec()] * (4 + len(pairs)),
        out_specs=[vmem_spec()] * (1 + len(pairs)),
        out_shape=[
            jax.ShapeDtypeStruct((groups, rows, GROUP_WIDTH), LOW),
            jax.ShapeDtypeStruct((groups, rows, 2 * GROUP_WIDTH), F32),
        ]
        + [jax.ShapeDtypeStruct((groups, rows, 2 * GROUP_WIDTH), LOW) for _ in pairs[1:]],
        scratch_shapes=[sorted_low] * 2
        + [sorted_sum] * 2
        + [stacked_low] * 2
        + [pltpu.VMEM((blocks, stacked, GROUP_WIDTH), F32)]
        + [limit] * 2
        + [row_values] * 2
        + [square] * 4
        + [square_low] * 4
        + [pltpu.SMEM((steps,), jnp.int32)] * 2,
        compiler_params=params(),
        cost_estimate=pl.CostEstimate(
            flops=groups * rows * HDIM,
            bytes_accessed=1_000_000,
            transcendentals=0,
        ),
        name="attend_backward",
    )(kpb, ends, queries, *pairs, out_grad, raw, lse)


def side_blocks():
    return D // BS


def bring(places, sources, held, done):
    copies = []
    for number, source in enumerate(sources):
        size = source.shape[0]
        target = held.at[pl.ds(places[number] * size, size)]
        copies.append(pltpu.make_async_copy(source, target, done.at[number]))
    for copy in copies:
        copy.start()
    for copy in copies:
        copy.wait()


def wide_tile(held, first, hidden_blocks, step):
    rows = []
    for row in range(side_blocks()):
        at = first + row * hidden_blocks + 2 * step
        rows.append(jnp.concatenate([held[at], held[at + 1]], axis=1))
    return jnp.concatenate(rows, axis=0)


def tall_tile(held, first, step):
    side = side_blocks()
    rows = []
    for half in range(2):
        at = first + (2 * step + half) * side
        rows.append(jnp.concatenate([held[at + column] for column in range(side)], axis=1))
    return jnp.concatenate(rows, axis=0)


def expert_sizes(weights):
    total = sum(array.shape[0] for array in weights[1])
    return total, total // (3 * side_blocks())


def expert_forward(rows_in, weights):
    rows = rows_in.shape[0]
    places, sources = weights
    count = len(sources)
    total_blocks, hidden_blocks = expert_sizes(weights)
    up_first = side_blocks() * hidden_blocks

    def kernel(places_ref, rows_ref, *refs):
        source_refs = refs[:count]
        result, gate_o, up_o, inner_o, total, held, done = refs[count:]
        step = pl.program_id(0)

        @pl.when(step == 0)
        def _():
            bring(places_ref, source_refs, held, done)
            total[...] = jnp.zeros_like(total)

        gate_tile = wide_tile(held, 0, hidden_blocks, step)
        up_tile = wide_tile(held, up_first, hidden_blocks, step)
        down_tile = tall_tile(held, 2 * up_first, step)

        for number in range(rows // TILE):
            first = number * TILE
            at = pl.ds(first, TILE)
            entering = rows_ref[at, :]
            gate_o[at, :] = dot(entering, gate_tile)
            up_o[at, :] = dot(entering, up_tile)
            for sub in range(TILE // SUB):
                now = pl.ds(first + sub * SUB, SUB)
                gate = gate_o[now, :]
                inner_o[now, :] = (gate * jax.nn.sigmoid(gate) * up_o[now, :]).astype(LOW)
            total[at, :] += dot(inner_o[at, :], down_tile)

        @pl.when(step == pl.num_programs(0) - 1)
        def _():
            result[...] = total[...].astype(LOW)

    fixed = pl.BlockSpec((rows, D), lambda step: (0, 0))
    hidden = pl.BlockSpec((rows, TILE), lambda step: (0, step))
    hidden_size = (rows, hidden_blocks * BS)
    return pl.pallas_call(
        kernel,
        grid=(hidden_blocks // 2,),
        in_specs=[smem_spec(), fixed] + [pl.BlockSpec(memory_space=pl.ANY)] * count,
        out_specs=[fixed] + [hidden] * 3,
        out_shape=[
            jax.ShapeDtypeStruct((rows, D), LOW),
            jax.ShapeDtypeStruct(hidden_size, F32),
            jax.ShapeDtypeStruct(hidden_size, F32),
            jax.ShapeDtypeStruct(hidden_size, LOW),
        ],
        scratch_shapes=[
            pltpu.VMEM((rows, D), F32),
            pltpu.VMEM((total_blocks, BS, BS), LOW),
            pltpu.SemaphoreType.DMA((count,)),
        ],
        compiler_params=params(),
        cost_estimate=pl.CostEstimate(
            flops=6 * rows * D * hidden_blocks * BS,
            bytes_accessed=6 * D * hidden_blocks * BS + 4 * rows * D,
            transcendentals=0,
        ),
        name="expert_forward",
    )(places, rows_in, *sources)


def expert_row_grads(grads_in, gate_in, up_in, weights):
    rows = grads_in.shape[0]
    places, sources = weights
    count = len(sources)
    total_blocks, hidden_blocks = expert_sizes(weights)
    up_first = side_blocks() * hidden_blocks

    def kernel(places_ref, grads_ref, gate_i, up_i, *refs):
        source_refs = refs[:count]
        back, gate_s, up_s, total, inner_grad_s, held, done = refs[count:]
        step = pl.program_id(0)

        @pl.when(step == 0)
        def _():
            bring(places_ref, source_refs, held, done)
            total[...] = jnp.zeros_like(total)

        gate_tile = wide_tile(held, 0, hidden_blocks, step)
        up_tile = wide_tile(held, up_first, hidden_blocks, step)
        down_tile = tall_tile(held, 2 * up_first, step)

        for number in range(rows // TILE):
            first = number * TILE
            at = pl.ds(first, TILE)
            inner_grad_s[at, :] = dot(grads_ref[at, :], down_tile, 1, 1)
            for sub in range(TILE // SUB):
                now = pl.ds(first + sub * SUB, SUB)
                gate = gate_i[now, :]
                inner_grad = inner_grad_s[now, :]
                sigmoid = jax.nn.sigmoid(gate)
                up_s[now, :] = (inner_grad * (gate * sigmoid)).astype(LOW)
                gate_s[now, :] = (
                    inner_grad * up_i[now, :] * (sigmoid * (1.0 + gate * (1.0 - sigmoid)))
                ).astype(LOW)
            total[at, :] += dot(gate_s[at, :], gate_tile, 1, 1) + dot(
                up_s[at, :], up_tile, 1, 1
            )

        @pl.when(step == pl.num_programs(0) - 1)
        def _():
            back[...] = total[...].astype(LOW)

    fixed = pl.BlockSpec((rows, D), lambda step: (0, 0))
    hidden = pl.BlockSpec((rows, TILE), lambda step: (0, step))
    hidden_shape = jax.ShapeDtypeStruct((rows, hidden_blocks * BS), LOW)
    return pl.pallas_call(
        kernel,
        grid=(hidden_blocks // 2,),
        in_specs=[smem_spec(), fixed, hidden, hidden]
        + [pl.BlockSpec(memory_space=pl.ANY)] * count,
        out_specs=[fixed] + [hidden] * 2,
        out_shape=[jax.ShapeDtypeStruct((rows, D), LOW)] + [hidden_shape] * 2,
        scratch_shapes=[
            pltpu.VMEM((rows, D), F32),
            pltpu.VMEM((rows, TILE), F32),
            pltpu.VMEM((total_blocks, BS, BS), LOW),
            pltpu.SemaphoreType.DMA((count,)),
        ],
        compiler_params=params(),
        cost_estimate=pl.CostEstimate(
            flops=6 * rows * D * hidden_blocks * BS,
            bytes_accessed=12 * D * hidden_blocks * BS + 6 * rows * D,
            transcendentals=0,
        ),
        name="expert_row_grads",
    )(places, grads_in, gate_in, up_in, *sources)


def expert_weight_grads(places, rows_in, grads_in, gate_grads, up_grads, inner, sizes):
    rows = rows_in.shape[0]
    hidden_blocks = gate_grads.shape[1] // BS
    side = side_blocks()
    total_blocks = 3 * side * hidden_blocks
    count = len(sizes)
    pieces = sum(len(group) for group in sizes)

    def kernel(places_ref, rows_ref, grads_ref, gate_s, up_s, inner_s, *refs):
        outs = refs[:count]
        turned, held, done = refs[count:]
        step = pl.program_id(0)

        @pl.when(step == 0)
        def _():
            turned[...] = rows_ref[...].T

        def wide_out(source, first):
            product = dot(turned[...], source[...]).astype(LOW)
            for row in range(side):
                for column in range(2):
                    held[first + row * hidden_blocks + 2 * step + column] = product[
                        row * BS : (row + 1) * BS, column * BS : (column + 1) * BS
                    ]

        wide_out(gate_s, 0)
        wide_out(up_s, side * hidden_blocks)
        product = dot(inner_s[...], grads_ref[...], 0, 0).astype(LOW)
        for half in range(2):
            for column in range(side):
                held[2 * side * hidden_blocks + (2 * step + half) * side + column] = product[
                    half * BS : (half + 1) * BS, column * BS : (column + 1) * BS
                ]

        @pl.when(step == pl.num_programs(0) - 1)
        def _():
            copies = []
            for target, group in zip(outs, sizes):
                first = 0
                for size in group:
                    number = len(copies)
                    source = held.at[pl.ds(places_ref[number] * size, size)]
                    into = target.at[pl.ds(first, size)]
                    copies.append(pltpu.make_async_copy(source, into, done.at[number]))
                    first += size
            for copy in copies:
                copy.start()
            for copy in copies:
                copy.wait()

    fixed = pl.BlockSpec((rows, D), lambda step: (0, 0))
    hidden = pl.BlockSpec((rows, TILE), lambda step: (0, step))
    return pl.pallas_call(
        kernel,
        grid=(hidden_blocks // 2,),
        in_specs=[smem_spec(), fixed, fixed] + [hidden] * 3,
        out_specs=[pl.BlockSpec(memory_space=pl.ANY)] * count,
        out_shape=[jax.ShapeDtypeStruct((sum(group), BS, BS), LOW) for group in sizes],
        scratch_shapes=[
            pltpu.VMEM((D, rows), LOW),
            pltpu.VMEM((total_blocks, BS, BS), LOW),
            pltpu.SemaphoreType.DMA((pieces,)),
        ],
        compiler_params=params(),
        cost_estimate=pl.CostEstimate(
            flops=6 * rows * D * hidden_blocks * BS,
            bytes_accessed=12 * D * hidden_blocks * BS + 6 * rows * D,
            transcendentals=0,
        ),
        name="expert_weight_grads",
    )(places, rows_in, grads_in, gate_grads, up_grads, inner)


def expert_half_grads(which, places, rows_in, grads_in, gate_grads, up_grads, inner, sizes):
    rows = rows_in.shape[0]
    hidden_blocks = gate_grads.shape[1] // BS
    side = side_blocks()
    middle_row = side // 2
    total_blocks = 3 * side * hidden_blocks // 2
    count = len(sizes)
    pieces = sum(len(group) for group in sizes)

    def kernel(which_ref, places_ref, rows_ref, grads_ref, gate_s, up_s, inner_s, *refs):
        outs = refs[:count]
        turned, held, done = refs[count:]
        step = pl.program_id(0)

        @pl.when(step == 0)
        def _():
            turned[...] = rows_ref[...].T

        def wide_out(source, first_row, last_row, first):
            product = dot(turned[first_row * BS : last_row * BS, :], source[...]).astype(LOW)
            for row in range(last_row - first_row):
                for column in range(2):
                    held[first + row * hidden_blocks + 2 * step + column] = product[
                        row * BS : (row + 1) * BS, column * BS : (column + 1) * BS
                    ]

        @pl.when(which_ref[0] == 0)
        def _():
            wide_out(gate_s, 0, side, 0)
            wide_out(up_s, 0, middle_row, side * hidden_blocks)

        @pl.when(which_ref[0] == 1)
        def _():
            wide_out(up_s, middle_row, side, 0)
            product = dot(inner_s[...], grads_ref[...], 0, 0).astype(LOW)
            for half in range(2):
                for column in range(side):
                    held[middle_row * hidden_blocks + (2 * step + half) * side + column] = product[
                        half * BS : (half + 1) * BS, column * BS : (column + 1) * BS
                    ]

        @pl.when(step == pl.num_programs(0) - 1)
        def _():
            copies = []
            for target, group in zip(outs, sizes):
                first = 0
                for size in group:
                    number = len(copies)
                    source = held.at[pl.ds(places_ref[number] * size, size)]
                    into = target.at[pl.ds(first, size)]
                    copies.append(pltpu.make_async_copy(source, into, done.at[number]))
                    first += size
            for copy in copies:
                copy.start()
            for copy in copies:
                copy.wait()

    fixed = pl.BlockSpec((rows, D), lambda step: (0, 0))
    hidden = pl.BlockSpec((rows, TILE), lambda step: (0, step))
    return pl.pallas_call(
        kernel,
        grid=(hidden_blocks // 2,),
        in_specs=[smem_spec(), smem_spec(), fixed, fixed] + [hidden] * 3,
        out_specs=[pl.BlockSpec(memory_space=pl.ANY)] * count,
        out_shape=[jax.ShapeDtypeStruct((sum(group), BS, BS), LOW) for group in sizes],
        scratch_shapes=[
            pltpu.VMEM((D, rows), LOW),
            pltpu.VMEM((total_blocks, BS, BS), LOW),
            pltpu.SemaphoreType.DMA((pieces,)),
        ],
        compiler_params=params(),
        cost_estimate=pl.CostEstimate(
            flops=3 * rows * D * hidden_blocks * BS,
            bytes_accessed=6 * D * hidden_blocks * BS + 6 * rows * D,
            transcendentals=0,
        ),
        name="expert_half_grads",
    )(which, places, rows_in, grads_in, gate_grads, up_grads, inner)


def split_low(values):
    high = values.astype(LOW)
    return high, (values - high.astype(F32)).astype(LOW)


def renew(gradient, weights, left, right, left_root, right_root, rate):
    short = gradient.astype(LOW)
    left_new = STAT_DECAY * left + (1.0 - STAT_DECAY) * dot(short, short, 1, 1)
    right_new = STAT_DECAY * right + (1.0 - STAT_DECAY) * dot(short, short, 0, 0)
    high, rest = split_low(right_root)
    turned = (dot(short, high) + dot(short, rest)).astype(LOW)
    high, rest = split_low(left_root)
    direction = dot(high, turned) + dot(rest, turned)
    return (gradient, left_new, right_new, weights.astype(F32) - rate * direction)


def block_width(count):
    return 4 if count % 4 == 0 else 3 if count % 3 == 0 else 1


def shampoo_half(half, gradients, stats, filled):
    parts = len(gradients)
    count = gradients[0].shape[0]
    width = block_width(count)
    steps = count // width
    spec = pl.BlockSpec((width, BS, BS), lambda step, half: (half[0] * steps + step, 0, 0))
    grad_spec = pl.BlockSpec((width, BS, BS), lambda step, half: (step, 0, 0))

    def kernel(half_ref, *refs):
        for number in range(width):
            total = refs[0][number].astype(F32)
            for ref in refs[1:parts]:
                total = total + ref[number].astype(F32)
            now = [ref[number] for ref in refs[parts : parts + 5]]
            results = renew(total, *now, RATE_EXPERT)
            for target, result in zip(refs[-4:], results):
                target[number] = result

    shape = jax.ShapeDtypeStruct(stats[0].shape, F32)
    extra = list(filled or ())
    return pl.pallas_call(
        kernel,
        grid_spec=pltpu.PrefetchScalarGridSpec(
            num_scalar_prefetch=1,
            grid=(steps,),
            in_specs=[grad_spec] * parts
            + [spec] * 5
            + [pl.BlockSpec(memory_space=pl.ANY)] * len(extra),
            out_specs=[spec] * 4,
        ),
        out_shape=[shape] * 4,
        input_output_aliases={6 + parts + number: number for number in range(len(extra))},
        compiler_params=params(),
        cost_estimate=pl.CostEstimate(
            flops=count * 24 * BS * BS * BS,
            bytes_accessed=count * BS * BS * (34 + 2 * parts),
            transcendentals=0,
        ),
        name="shampoo_half",
    )(half, *gradients, *stats, *extra)


def shampoo(rates, gradient, stats):
    count = gradient.shape[0]
    width = block_width(count)
    spec = pl.BlockSpec((width, BS, BS), lambda step: (step, 0, 0))
    shape = jax.ShapeDtypeStruct((count, BS, BS), F32)

    def kernel(rates_ref, *refs):
        step = pl.program_id(0)
        for number in range(width):
            gradient_now, *stats_now = [ref[number] for ref in refs[:6]]
            results = renew(
                gradient_now.astype(F32), *stats_now, rates_ref[step * width + number]
            )
            for target, result in zip(refs[6:], results):
                target[number] = result

    return pl.pallas_call(
        kernel,
        grid=(count // width,),
        in_specs=[smem_spec()] + [spec] * 6,
        out_specs=[spec] * 4,
        out_shape=[shape] * 4,
        compiler_params=params(),
        cost_estimate=pl.CostEstimate(
            flops=count * 24 * BS * BS * BS,
            bytes_accessed=count * BS * BS * 38,
            transcendentals=0,
        ),
        name="shampoo_blocks",
    )(rates, gradient, *stats)


def shampoo_panel(turn, places, panels, stats):
    groups = len(panels)
    panel_rows = panels[0].shape[0]
    parts = 3
    breadth = groups * GROUP_WIDTH
    count = stats[0].shape[0]
    width = block_width(count)
    spec = pl.BlockSpec((width, BS, BS), lambda step, turn, places: (step, 0, 0))
    fixed = pl.BlockSpec(panels[0].shape, lambda step, turn, places: (0, 0))
    shape = jax.ShapeDtypeStruct((count, BS, BS), F32)
    per_part = breadth // BS
    per_row = parts * per_part
    side = D // BS

    def kernel(turn_ref, places_ref, *refs):
        step = pl.program_id(0)
        panel_refs = refs[:groups]
        stat_refs = refs[groups : groups + 5]
        outs = refs[groups + 5 : groups + 9]
        ordered, matrix = refs[groups + 9 :]

        @pl.when(step == 0)
        def _():
            for number, panel in enumerate(panel_refs):
                ordered[places_ref[number]] = panel[...]
            for part in range(parts):
                matrix[:, part * breadth : (part + 1) * breadth] = jnp.concatenate(
                    [
                        ordered[group, :, part * GROUP_WIDTH : (part + 1) * GROUP_WIDTH].astype(F32)
                        for group in range(groups)
                    ],
                    axis=1,
                )

        turned = turn_ref[0] == 1
        rate = jnp.where(turned, RATE_OUTPUT, RATE_PROJECT).astype(F32)
        for number in range(width):
            block = step * width + number
            row_now = jnp.where(turned, block % side % 2, block // per_row)
            column_now = jnp.where(
                turned, block % side // 2 * per_part + block // side, block % per_row
            )
            found = matrix[
                pl.ds(pl.multiple_of(row_now * BS, BS), BS),
                pl.ds(pl.multiple_of(column_now * BS, BS), BS),
            ]
            found = jnp.where(turned, found.T, found)
            results = renew(found, *[ref[number] for ref in stat_refs], rate)
            for target, result in zip(outs, results):
                target[number] = result

    return pl.pallas_call(
        kernel,
        grid_spec=pltpu.PrefetchScalarGridSpec(
            num_scalar_prefetch=2,
            grid=(count // width,),
            in_specs=[fixed] * groups + [spec] * 5,
            out_specs=[spec] * 4,
            scratch_shapes=[
                pltpu.VMEM((groups, *panels[0].shape), LOW),
                pltpu.VMEM((panel_rows, parts * breadth), F32),
            ],
        ),
        out_shape=[shape] * 4,
        compiler_params=params(),
        cost_estimate=pl.CostEstimate(
            flops=count * 24 * BS * BS * BS,
            bytes_accessed=count * BS * BS * 38,
            transcendentals=0,
        ),
        name="shampoo_panel",
    )(turn, places, *panels, *stats)


def shampoo_small(weights, gradient, left_stat, right_stat, left_root, right_root, step_rates):
    left_new = STAT_DECAY * left_stat + (1.0 - STAT_DECAY) * jnp.einsum(
        "nij,nkj->nik", gradient, gradient, precision=PRECISE
    )
    right_new = STAT_DECAY * right_stat + (1.0 - STAT_DECAY) * jnp.einsum(
        "nji,njk->nik", gradient, gradient, precision=PRECISE
    )
    turned = jnp.einsum("nij,njk->nik", gradient, right_root, precision=PRECISE)
    direction = jnp.einsum("nij,njk->nik", left_root, turned, precision=PRECISE)
    return (left_new, right_new, weights - step_rates * direction)


def shifted(values, axis, size, distance):
    return lax.ppermute(values, axis, [(i, (i + distance) % size) for i in range(size)])


def crossed(values, axes, size, distance):
    return lax.ppermute(values, axes, [(i, i ^ distance) for i in range(size)])


def direct_sum(values, axes, size):
    terms = [values] + [crossed(values, axes, size, step) for step in range(1, size)]
    while len(terms) > 1:
        terms = [terms[at] + terms[at + 1] for at in range(0, len(terms), 2)]
    return terms[0]


def everywhere_sum(values, sizes):
    a_size, b_size, c_size, f_size = sizes
    values = direct_sum(values, "f", f_size)
    values = direct_sum(values, "c", c_size)
    return direct_sum(values, ("a", "b"), a_size * b_size)


def body(
    sizes,
    inputs,
    out_grad,
    vectors,
    block_order,
    seq_lengths,
    expert_ids,
    attn_weights,
    attn_left,
    attn_right,
    attn_left_root,
    attn_right_root,
    expert_weights,
    expert_left,
    expert_right,
    expert_left_root,
    expert_right_root,
    router_weights,
    router_left,
    router_right,
    router_left_root,
    router_right_root,
):
    a_size, b_size, c_size, f_size = sizes
    rows = inputs.shape[0]
    capacity = rows // 4
    tokens_all = rows * a_size * b_size * c_size * f_size
    per_side = D // BS
    project_blocks = 3 * per_side * per_side
    a_place = lax.axis_index("a")
    c_place = lax.axis_index("c")
    f_place = lax.axis_index("f")
    per_device = attn_weights.shape[0]
    per = expert_weights.shape[1]
    shares = b_size * c_size
    local_slices = expert_weights.shape[0]

    by_panels = f_size == 4 and c_size == 2 and a_size == 2
    ends = jnp.cumsum(seq_lengths[0]).astype(jnp.int32)
    order = block_order[0].reshape(a_size * b_size, c_size, SLOTS)
    kpb = jnp.stack(
        [
            lax.dynamic_index_in_dim(order, (c_place - step) % c_size, 1, False).reshape(-1)
            for step in range(c_size)
        ]
    )

    split_count = expert_weights.shape[0] * f_size // EXPERTS
    numbers = jnp.arange(EXPERTS, dtype=jnp.int32)
    spots = (numbers % a_size) * f_size + numbers // a_size if split_count == 1 else numbers
    route_count = EXPERTS + ZEROS
    named = expert_ids[:, :, None] == jnp.arange(route_count, dtype=jnp.int32)[None, None, :]
    route_member = named.astype(F32)
    chosen = jnp.any(named[:, :, :EXPERTS], axis=1).astype(LOW)
    row_numbers = jnp.arange(rows, dtype=jnp.int32)
    before = (row_numbers[None, :] < row_numbers[:, None]).astype(LOW)
    ranks = jnp.dot(before, chosen, preferred_element_type=F32).astype(jnp.int32)
    slots = jnp.sum(
        jnp.where(named[:, :, :EXPERTS], (spots * capacity)[None, None, :] + ranks[:, None, :], 0),
        axis=2,
    )
    slots = jnp.where(expert_ids < EXPERTS, slots, -1)
    slot_numbers = jnp.arange(EXPERTS * capacity, dtype=jnp.int32)
    picks = [
        (slot_numbers[:, None] == slots[:, which][None, :]).astype(LOW) for which in range(2)
    ]
    picks_both = picks[0] + picks[1]

    def to_owners(buffer):
        buffer = buffer.astype(LOW).reshape(EXPERTS, capacity, D)
        if split_count > 1:
            buffer = jnp.repeat(buffer, split_count, axis=0)
        arrived = lax.all_to_all(buffer, ("a", "f"), split_axis=0, concat_axis=0, tiled=True)
        return arrived.reshape(-1, D)

    def return_rows(results):
        return lax.all_to_all(
            results.reshape(EXPERTS * split_count, -1, D),
            ("a", "f"),
            split_axis=0,
            concat_axis=0,
            tiled=True,
        )

    def from_owners(back, pick_matrices):
        back = back.reshape(EXPERTS, split_count, capacity, D)
        return [
            sum(
                dot(matrix, back[:, part].reshape(-1, D), 0, 0) for part in range(split_count)
            )
            for matrix in pick_matrices
        ]

    tie = lax.optimization_barrier
    share_place = lax.axis_index(("b", "c"))

    def over_groups(values):
        return lax.all_to_all(values, ("a", "b"), split_axis=0, concat_axis=0, tiled=True)

    def over_b(values):
        return crossed(values, "b", b_size, 1)

    def over_c(values):
        return crossed(values, "c", c_size, 1)

    if by_panels:
        group_place = lax.axis_index(("a", "b"))
        share_places = jnp.stack([share_place ^ step for step in range(shares)])
        first_spots, other_spots = a_place * shares + share_places, (
            (1 - a_place) * shares + share_places
        )

        def halves(values):
            return [values[: per // 2], values[per // 2 :]]

        own = jnp.where(a_place == 0, expert_weights[0], expert_weights[1])
        own_halves = halves(own)
        sent = jnp.where(a_place == 0, expert_weights[1], expert_weights[0])
        cuts = [slice(0, per // 2), slice(per // 2, per * 3 // 4), slice(per * 3 // 4, per)]
        across = crossed(attn_weights, "f", f_size, 2)
        own_c = over_c(own)
        got = [shifted(sent[cuts[0]], "a", 2, 1), None]
        own_b = [over_b(own_halves[0]), None]

        def both(spot):
            return [2 * spot, 2 * spot + 1]

        weight_places = [first_spots[0], first_spots[1]] + both(first_spots[2])
        weight_places += both(first_spots[3]) + both(other_spots[0]) + both(other_spots[1])
        weight_places += both(other_spots[2]) + both(other_spots[3])
        weight_places = jnp.stack(weight_places).astype(jnp.int32)
        kept_places = jnp.stack([share_places[step] for step in (0, 2, 1, 3)])
        given_places = [share_places[0], 2 * share_places[1], 2 * share_places[3]]
        given_places += [2 * share_places[2] + 1, 2 * share_places[3] + 1]
        given_places += [2 * share_places[2], 2 * share_places[1] + 1]
        kept_places = kept_places.astype(jnp.int32)
        given_places = jnp.stack(given_places).astype(jnp.int32)
        group_places = jnp.stack([group_place ^ step for step in range(HEAD_GROUPS)])
        group_places = group_places.astype(jnp.int32)
        shard_places = jnp.stack([f_place ^ step for step in range(f_size)]).astype(jnp.int32)
        (across, own_c, got[0], own_b[0], kpb, ends, *tables) = tie(
            (across, own_c, got[0], own_b[0], kpb, ends)
            + (weight_places, kept_places, given_places, group_places, shard_places)
        )
        weight_places, kept_places, given_places, group_places, shard_places = tables
        shards = [
            attn_weights,
            crossed(attn_weights, "f", f_size, 1),
            across,
            crossed(across, "f", f_size, 1),
        ]
        first_low, first_factor, own_queries, own_pairs, w_project = project_kernel(
            inputs, vectors[0:1], shard_places, shards
        )
        w_project = w_project.reshape(D, 3 * D)
        own_pairs, got_next = tie((own_pairs, shifted(sent[cuts[1]], "a", 2, 1)))
        own_b[1] = over_b(own_halves[1])
        own_bc = [over_c(own_b[0]), None]
        got_c = [over_c(got[0]), None]
        mine, own_b[1], own_bc[0], got_c[0] = tie(
            (over_groups(own_pairs), own_b[1], own_bc[0], got_c[0])
        )
        other = over_c(mine)
        queries = over_groups(own_queries)
        got_last = shifted(tie((sent[cuts[2]], mine))[0], "a", 2, 1)
        queries, other, got_last = tie((queries, other, got_last))
        got[1] = jnp.concatenate([got_next, got_last], axis=0)
        pairs = [mine, other]
        first_sent, own_b1, got_0, got_1 = tie((first_low, own_b[1], *got, queries))[:4]
        first_parts = [first_low, None, crossed(first_sent, ("a", "b"), HEAD_GROUPS, 2), None]
        own_bc[1] = over_c(own_b1)
        got_c[1] = over_c(got_1)
        got_b = [over_b(got_0), None]
        w_output = shards[3]
        for step in range(f_size - 1):
            w_output = jnp.where(f_place == 3 - step, shards[step], w_output)
        w_output = to_matrix(w_output, D, D)
        raw, low, lse = attend(kpb, ends, queries, pairs)
        raw, low, lse, first_parts[2], own_bc[1], got_c[1], got_b[0] = tie(
            (raw, low, lse, first_parts[2], own_bc[1], got_c[1], got_b[0])
        )
        got_b[1] = over_b(tie((got[1], low))[0])
    else:
        attn_all = lax.all_gather(attn_weights, "f", axis=0, tiled=True)
        w_project = to_matrix(attn_all[:project_blocks], D, 3 * D)
        w_output = to_matrix(attn_all[project_blocks:], D, D)
        first_norm, first_factor = normalize_parts(inputs, vectors[0])
        first_low = first_norm.astype(LOW)
        projected = jnp.dot(first_low, w_project, preferred_element_type=F32).astype(LOW)
        by_part = projected.reshape(rows, 3, HEAD_GROUPS, GROUP_WIDTH)
        own_queries = by_part[:, 0].transpose(1, 0, 2)
        own_pairs = (
            by_part[:, 1:].transpose(2, 0, 1, 3).reshape(HEAD_GROUPS, rows, 2 * GROUP_WIDTH)
        )
        mine = over_groups(own_pairs)
        pairs = [mine] + [shifted(mine, "c", c_size, step) for step in range(1, c_size)]
        queries = over_groups(pack_rows(own_queries))
        raw, low, lse = attend(kpb, ends, queries, pairs)
        weight_places = jnp.arange(local_slices, dtype=jnp.int32)
        weight_shares = [
            lax.all_gather(expert_weights[number], ("b", "c"), axis=0, tiled=True)
            for number in range(local_slices)
        ]
        weights = (weight_places, weight_shares)
    by_heads = unpack_rows(over_groups(low))
    attended = by_heads.transpose(1, 0, 2).reshape(rows, D)
    middle = inputs + jnp.dot(attended, w_output, preferred_element_type=F32)
    second, second_factor = normalize_parts(middle, vectors[1])
    second_low = second.astype(LOW)
    if by_panels:
        second_low, got_b[1] = tie((second_low, got_b[1]))
        first_sent, *got_bc = tie((first_low, *got_b, second_low))[:3]
        first_parts[1] = crossed(first_sent, ("a", "b"), HEAD_GROUPS, 1)
        got_bc = [over_c(part) for part in got_bc]

    logits = jnp.dot(second_low, router_weights, preferred_element_type=F32)
    picked_logits = jnp.sum(jnp.where(named, logits[:, None, :], 0.0), axis=2)
    route_gates = jax.nn.softmax(picked_logits, axis=-1)
    received = to_owners(dot(picks_both, second_low))
    grad_rows = [
        (route_gates[:, which][:, None] * out_grad).astype(LOW) for which in range(2)
    ]
    if by_panels:
        grad_rows[0], first_parts[1], *got_bc = tie((grad_rows[0], first_parts[1], *got_bc))
    arrived = to_owners(dot(picks[0], grad_rows[0]) + dot(picks[1], grad_rows[1]))
    if by_panels:
        weight_shares = [own, own_c, *own_b, *own_bc, *got, *got_c, *got_b, *got_bc]
        weights = (weight_places, weight_shares)
    result, gate_kept, up_kept, inner = expert_forward(received, weights)
    result = return_rows(result)
    back_rows, gate_grads, up_grads = expert_row_grads(arrived, gate_kept, up_kept, weights)
    if by_panels:
        full, part = per, per // 2
        half = a_place.astype(jnp.int32).reshape(1)
        given, hop_c, hop_b, near_b, near_c = expert_half_grads(
            1 - half,
            given_places,
            received,
            arrived,
            gate_grads,
            up_grads,
            inner,
            [(full,), (part, part), (part, part), (part,), (part,)],
        )
        first_parts[3] = over_b(tie((first_parts[2], arrived))[0])
        back_rows, result, near_b, gate_grads, up_grads, first_parts[3] = tie(
            (back_rows, result, near_b, gate_grads, up_grads, first_parts[3])
        )
        back_rows = return_rows(back_rows)
        kept, kept_far, kept_near, kept_next = expert_half_grads(
            half,
            kept_places,
            received,
            arrived,
            gate_grads,
            up_grads,
            inner,
            [(full,)] * 4,
        )
        back_rows, kept = tie((back_rows, kept))
        hop_c, hop_b = over_c(hop_c), over_b(hop_b)
    else:
        back_rows = return_rows(back_rows)
        grad_shares = expert_weight_grads(
            jnp.arange(shares, dtype=jnp.int32),
            received,
            arrived,
            gate_grads,
            up_grads,
            inner,
            [(per,)] * shares,
        )
    expert_rows = jnp.stack(from_owners(result, picks), axis=1)
    const_member = route_member[:, :, EXPERTS + 2 :]
    copy_member = route_member[:, :, EXPERTS + 1]
    route_values = (
        expert_rows
        + copy_member[:, :, None] * second[:, None, :]
        + jnp.einsum("rkc,cd->rkd", const_member, vectors[2:], precision=PRECISE)
    )
    output = middle + jnp.sum(route_gates[:, :, None] * route_values, axis=1)

    gate_grad = jnp.sum(out_grad[:, None, :] * route_values, axis=2)
    picked_grad = route_gates * (
        gate_grad - jnp.sum(route_gates * gate_grad, axis=1, keepdims=True)
    )
    logit_grad = jnp.sum(route_member * picked_grad[:, :, None], axis=1)
    router_local = lax.dot_general(
        logit_grad, second_low.astype(F32), (((0,), (0,)), ((), ())), precision=PRECISE
    )
    second_grad = jnp.dot(logit_grad, router_weights.astype(F32).T, precision=PRECISE)
    second_grad = second_grad + jnp.sum(route_gates * copy_member, axis=1)[:, None] * out_grad
    const_grad = jnp.einsum("rkc,rk,rd->cd", const_member, route_gates, out_grad, precision=PRECISE)
    second_grad = second_grad + from_owners(back_rows, [picks_both])[0]
    middle_part, second_gain_grad = normalize_back(middle, second_factor, vectors[1], second_grad)
    middle_grad = out_grad + middle_part
    middle_low = middle_grad.astype(LOW)

    flat = (-1, BS, BS)
    expert_stats = [
        item.reshape(flat)
        for item in (
            expert_weights,
            expert_left,
            expert_right,
            expert_left_root,
            expert_right_root,
        )
    ]

    attended_grad = dot(middle_low, w_output, 1, 1).astype(LOW)
    attended_grad = attended_grad.reshape(rows, HEAD_GROUPS, GROUP_WIDTH).transpose(1, 0, 2)
    attended_grad = over_groups(pack_rows(attended_grad))
    if by_panels:
        hop_c, hop_b = tie((hop_c, hop_b, middle_low))[:2]
        given_b = over_b((near_b.astype(F32) + hop_c[part:].astype(F32)).astype(LOW))
        given_c = (near_c.astype(F32) + hop_b[part:].astype(F32)).astype(LOW)
        kept_next = over_c(tie((kept_next, given_c))[0])
        given_c = over_c(given_c)
        early = jnp.concatenate([router_local, second_gain_grad[None], const_grad], axis=0)
        early = direct_sum(early, "f", f_size)
        early = direct_sum(early, ("a", "b"), HEAD_GROUPS)
        attended_grad, given_b, given_c, kept_next, early = tie(
            (attended_grad, given_b, given_c, kept_next, early)
        )
        kept_sum = (kept_far.astype(F32) + kept_next.astype(F32)).astype(LOW)
        taken = jnp.concatenate(
            [
                given[:part].astype(F32) + hop_c[:part].astype(F32) + given_b.astype(F32),
                given[part:].astype(F32) + hop_b[:part].astype(F32) + given_c.astype(F32),
            ],
            axis=0,
        )
        taken = shifted(taken.astype(LOW), "a", 2, 1)
        kept_near = over_c(tie((kept_near, attended_grad))[0])
        early = direct_sum(early, "c", c_size)
    back_outs = attend_back(kpb, ends, queries, pairs, attended_grad, raw, lse)
    if by_panels:
        *back_outs, kept_near, taken, early = tie((*back_outs, kept_near, taken, early))
        middle_late = tie((middle_low, back_outs[0]))[0]
        output_panels = jnp.einsum(
            "hrj,rd->hdj", by_heads, middle_late, preferred_element_type=F32
        ).astype(LOW)
        output_panels = over_groups(output_panels)
        expert_outs = shampoo_half(1 - half, [taken], expert_stats, None)
        first_parts = tie((*first_parts, back_outs[0]))[:HEAD_GROUPS]
        first_all = jnp.zeros((HEAD_GROUPS, rows, D), LOW)
        for step, part_rows in enumerate(first_parts):
            first_all = lax.dynamic_update_index_in_dim(
                first_all, part_rows, group_place ^ step, 0
            )
        first_all = first_all.reshape(-1, D)
    query_grad, pair_grad = back_outs[:2]
    for step in range(1, c_size):
        pair_grad = pair_grad + shifted(back_outs[1 + step], "c", c_size, -step).astype(F32)
    group_grad = jnp.concatenate([query_grad, pair_grad.astype(LOW)], axis=2)
    if by_panels:
        group_grad, output_panels, first_all, early, *expert_outs = tie(
            (group_grad, output_panels, first_all, early, *expert_outs)
        )
    if by_panels:
        panels = dot(first_all, group_grad.reshape(-1, 3 * GROUP_WIDTH), 0, 0).astype(LOW)
        group_grad, panels = tie((group_grad, panels))
    project_grad = over_groups(group_grad)
    if by_panels:
        panels = panels.reshape(3, D // 3, 3 * GROUP_WIDTH)
        output_panels = jnp.sum(output_panels.astype(F32), axis=0).astype(LOW)
        output_panels = (
            output_panels.reshape(3, D // 3, GROUP_WIDTH)
            .transpose(1, 0, 2)
            .reshape(1, D // 3, 3 * GROUP_WIDTH)
        )
        panels = jnp.concatenate([panels, output_panels], axis=0)
        own_panels = [
            lax.dynamic_index_in_dim(panels, f_place ^ step, 0, False) for step in range(f_size)
        ]
        summed = own_panels[0].astype(F32)
        for step in range(1, f_size):
            summed = summed + crossed(own_panels[step], "f", f_size, step).astype(F32)
        summed = summed.astype(LOW)
        summed = (summed.astype(F32) + crossed(summed, "c", 2, 1).astype(F32)).astype(LOW)
        group_panels = [
            crossed(summed, ("a", "b"), HEAD_GROUPS, step) for step in range(1, HEAD_GROUPS)
        ]
        project_grad, *group_panels = tie((project_grad, *group_panels))
        kept_b = over_b(tie((kept_sum, summed))[0])
    project_grad = (
        project_grad.reshape(HEAD_GROUPS, rows, 3, GROUP_WIDTH)
        .transpose(1, 2, 0, 3)
        .reshape(rows, 3 * D)
    )
    first_grad = dot(project_grad, w_project, 1, 1)
    input_part, first_gain_grad = normalize_back(inputs, first_factor, vectors[0], first_grad)
    input_grad = middle_grad + input_part

    everywhere = ("a", "b", "c", "f")
    if not by_panels:
        early = jnp.concatenate([router_local, second_gain_grad[None], const_grad], axis=0)
        early = everywhere_sum(early, sizes)
    late = direct_sum(first_gain_grad[None], "f", f_size)

    attn_stats = (attn_weights, attn_left, attn_right, attn_left_root, attn_right_root)
    if by_panels:
        turn = (f_place == 3).astype(jnp.int32).reshape(1)
        attn_outs = shampoo_panel(
            turn, group_places, [summed, *group_panels], attn_stats
        )
        late, kept, *attn_outs = tie((late, kept, *attn_outs))
        late, kept = tie((direct_sum(late, "c", c_size), kept))
        expert_outs = shampoo_half(half, [kept, kept_near, kept_b], expert_stats, expert_outs)
    else:
        output_weight_grad = dot(attended, middle_low, 0, 0)
        project_weight_grad = dot(first_low, project_grad, 0, 0)
        attn_local = jnp.concatenate(
            [to_blocks(project_weight_grad, BS, BS), to_blocks(output_weight_grad, BS, BS)],
            axis=0,
        )
        attn_sum = lax.psum(attn_local, everywhere)
        attn_gradient = lax.dynamic_slice_in_dim(attn_sum, f_place * per_device, per_device, 0)
        block_numbers = f_place * per_device + jnp.arange(per_device, dtype=jnp.int32)
        attn_rates = jnp.where(block_numbers < project_blocks, RATE_PROJECT, RATE_OUTPUT)
        attn_outs = shampoo(attn_rates.astype(F32), attn_gradient, attn_stats)
        expert_gradient = lax.psum_scatter(
            jnp.concatenate(grad_shares, axis=0).reshape(local_slices, -1, BS, BS).astype(F32),
            ("b", "c"),
            scatter_dimension=1,
            tiled=True,
        ).reshape(flat)
        expert_outs = shampoo(
            jnp.full((expert_gradient.shape[0],), RATE_EXPERT, F32), expert_gradient, expert_stats
        )
    expert_grads, expert_left_new, expert_right_new, expert_new = [
        item.reshape(expert_weights.shape) for item in expert_outs
    ]
    if not by_panels:
        late = direct_sum(late, "c", c_size)
    late = direct_sum(late, ("a", "b"), a_size * b_size)
    attn_grads, attn_left_new, attn_right_new, attn_new = attn_outs
    router_grads = early[:route_count].T
    vector_grads = jnp.concatenate([late, early[route_count:]], axis=0)
    router_left_new, router_right_new, router_moved = shampoo_small(
        to_blocks(router_weights.astype(F32), BS, route_count),
        to_blocks(router_grads, BS, route_count),
        router_left,
        router_right,
        router_left_root,
        router_right_root,
        RATE_ROUTER,
    )
    router_new = to_matrix(router_moved, D, route_count)
    vector_new = vectors - RATE_VECTOR * float(tokens_all) ** (-0.5) * vector_grads
    return (
        output,
        input_grad,
        vector_grads,
        vector_new,
        attn_grads,
        attn_left_new,
        attn_right_new,
        attn_new,
        expert_grads,
        expert_left_new,
        expert_right_new,
        expert_new,
        router_grads,
        router_left_new,
        router_right_new,
        router_new,
    )


def solution(mesh):
    ctx_size = mesh.shape["ctx"]
    f_size = mesh.shape["fsdp"]
    context = ("a", "b", "c")
    token_rows = P(context + ("f",), None)
    group_rows = P("f", None)
    attn = P("f", None, None)
    expert = P("f", context, None, None)
    in_specs = (
        (token_rows, token_rows, P(), group_rows, group_rows, token_rows)
        + (attn,) * 5
        + (expert,) * 5
        + (P(),) * 5
    )
    out_specs = (token_rows, token_rows, P(), P()) + (attn,) * 4 + (expert,) * 4 + (P(),) * 4

    def run(*arrays):
        local_slices = arrays[11].shape[0] // f_size
        a_size = 2 if local_slices == 2 else 1
        b_size = HEAD_GROUPS // a_size
        c_size = ctx_size // HEAD_GROUPS
        sizes = (a_size, b_size, c_size, f_size)
        fine_mesh = jax.sharding.Mesh(mesh.devices.reshape(sizes), ("a", "b", "c", "f"))
        return jax.shard_map(
            functools.partial(body, sizes),
            mesh=fine_mesh,
            in_specs=in_specs,
            out_specs=out_specs,
            check_vma=False,
        )(*arrays)

    return run
```

```python
import functools

import jax
import jax.numpy as jnp
from jax import lax
from jax.experimental import pallas as pl
from jax.experimental.pallas import tpu as pltpu
from jax.sharding import PartitionSpec as P

D = 768
HEADS = 12
HDIM = 64
EXPERTS = 8
ZEROS = 4
BS = 128
SLOTS = 4
HEAD_GROUPS = 4
GROUP_WIDTH = HEADS // HEAD_GROUPS * HDIM
GROUP_HEADS = HEADS // HEAD_GROUPS
CHUNK = 256
TILE = 256
SUB = 32

EPSILON = 1e-06
SCORE_SCALE = 0.125
STAT_DECAY = 0.5
RATE_PROJECT = 0.4
RATE_OUTPUT = 3.0
RATE_EXPERT = 0.4
RATE_ROUTER = 0.2
RATE_VECTOR = 0.1
MASKED_SCORE = -1e30
PRECISE = lax.Precision.HIGHEST
F32 = jnp.float32
LOW = jnp.bfloat16
VMEM_LIMIT = 56 * 1024 * 1024


def to_matrix(blocks, height, breadth):
    block_height = blocks.shape[1]
    block_breadth = blocks.shape[2]
    shaped = blocks.reshape(
        height // block_height, breadth // block_breadth, block_height, block_breadth
    )
    return shaped.transpose(0, 2, 1, 3).reshape(height, breadth)


def to_blocks(matrix, block_height, block_breadth):
    height = matrix.shape[0]
    breadth = matrix.shape[1]
    shaped = matrix.reshape(
        height // block_height, block_height, breadth // block_breadth, block_breadth
    )
    return shaped.transpose(0, 2, 1, 3).reshape(-1, block_height, block_breadth)


def normalize_parts(values, scaling):
    factor = lax.rsqrt(jnp.mean(values * values, axis=-1, keepdims=True) + EPSILON)
    return (values * factor * scaling, factor)


def normalize_back(values, factor, scaling, gradient):
    unit_rows = values * factor
    scaled = gradient * scaling
    value_grad = factor * (
        scaled - unit_rows * jnp.mean(scaled * unit_rows, axis=-1, keepdims=True)
    )
    return (value_grad, jnp.sum(gradient * unit_rows, axis=0))


def dot(left, right, left_dim=1, right_dim=0):
    return lax.dot_general(
        left, right, (((left_dim,), (right_dim,)), ((), ())), preferred_element_type=F32
    )


def vmem_spec():
    return pl.BlockSpec(memory_space=pltpu.VMEM)


def smem_spec():
    return pl.BlockSpec(memory_space=pltpu.SMEM)


def params():
    return pltpu.CompilerParams(vmem_limit_bytes=VMEM_LIMIT)


def project_kernel(rows_in, gain, places, shards):
    rows = rows_in.shape[0]
    owners = len(shards) - 1
    depth = D // owners
    breadth = 3 * D
    block_rows = depth // BS
    block_columns = breadth // BS
    pair = 2 * GROUP_WIDTH

    def kernel(places_ref, rows_ref, gain_ref, *refs):
        shard_refs = refs[: owners + 1]
        first_out, factor_out, query_out, pair_out, matrix, first_s = refs[owners + 1 :]
        for number, shard in enumerate(shard_refs):
            owner = places_ref[number]

            @pl.when(owner < owners)
            def _(owner=owner, shard=shard):
                for row in range(block_rows):
                    for column in range(block_columns):
                        matrix[
                            owner, row * BS : (row + 1) * BS, column * BS : (column + 1) * BS
                        ] = shard[row * block_columns + column]

        def norm(tile, carry):
            at = pl.ds(pl.multiple_of(tile * SUB, SUB), SUB)
            values = rows_ref[at, :]
            factor = lax.rsqrt(jnp.mean(values * values, axis=1, keepdims=True) + EPSILON)
            first = (values * factor * gain_ref[...]).astype(LOW)
            factor_out[at, :] = factor
            first_out[at, :] = first
            for owner in range(owners):
                first_s[owner, at, :] = first[:, owner * depth : (owner + 1) * depth]
            return carry

        lax.fori_loop(0, rows // SUB, norm, 0)
        for tile in range(breadth // pair):
            at = slice(tile * pair, (tile + 1) * pair)
            total = dot(first_s[0], matrix[0, :, at])
            for owner in range(1, owners):
                total = total + dot(first_s[owner], matrix[owner, :, at])
            total = total.astype(LOW)
            part = tile * pair // D
            group = tile * pair % D // GROUP_WIDTH
            for side in range(2):
                piece = total[:, side * GROUP_WIDTH : (side + 1) * GROUP_WIDTH]
                if part == 0:
                    query_out[group + side] = jnp.concatenate(
                        [piece[: rows // 2], piece[rows // 2 :]], axis=1
                    )
                else:
                    pair_out[
                        group + side, :, (part - 1) * GROUP_WIDTH : part * GROUP_WIDTH
                    ] = piece

    return pl.pallas_call(
        kernel,
        in_specs=[smem_spec()] + [vmem_spec()] * (owners + 3),
        out_specs=[vmem_spec()] * 5,
        out_shape=[
            jax.ShapeDtypeStruct((rows, D), LOW),
            jax.ShapeDtypeStruct((rows, 1), F32),
            jax.ShapeDtypeStruct((HEAD_GROUPS, rows // 2, pair), LOW),
            jax.ShapeDtypeStruct((HEAD_GROUPS, rows, pair), LOW),
            jax.ShapeDtypeStruct((owners, depth, breadth), LOW),
        ],
        scratch_shapes=[pltpu.VMEM((owners, rows, depth), LOW)],
        compiler_params=params(),
        cost_estimate=pl.CostEstimate(
            flops=2 * rows * D, bytes_accessed=1_000_000, transcendentals=0
        ),
        name="project",
    )(places, rows_in, gain, *shards)


def head_masks(value):
    lane = lax.broadcasted_iota(jnp.int32, (1, GROUP_WIDTH), 1)
    return [
        jnp.where(lane // HDIM == head, value, 0.0).astype(F32) for head in range(GROUP_HEADS)
    ]


def stack_heads(rows, masks):
    return jnp.concatenate([rows * mask.astype(rows.dtype) for mask in masks], axis=0)


def packed_at(slot, block_rows):
    first_row = slot % 2 * block_rows
    first_lane = slot // 2 * GROUP_WIDTH
    return slice(first_row, first_row + block_rows), slice(first_lane, first_lane + GROUP_WIDTH)


def pack_rows(values):
    groups, rows, width = values.shape
    return values.reshape(groups, 2, rows // 2, width).transpose(0, 2, 1, 3).reshape(
        groups, rows // 2, 2 * width
    )


def unpack_rows(values):
    groups, rows, width = values.shape
    return values.reshape(groups, rows, 2, width // 2).transpose(0, 2, 1, 3).reshape(
        groups, 2 * rows, width // 2
    )


def fill_sorted(kpb, sources, key_sorted, value_sorted, block_rows, block_count):
    key_sorted[0:CHUNK, :] = jnp.zeros((CHUNK, GROUP_WIDTH), LOW)
    value_sorted[0:CHUNK, :] = jnp.zeros((CHUNK, GROUP_WIDTH), LOW)
    for number, source in enumerate(sources):

        def fill(item, carry, source=source, number=number):
            from_row = pl.multiple_of(item % SLOTS * block_rows, block_rows)
            to_row = pl.multiple_of(CHUNK + kpb[number, item] * block_rows, 32)
            rows = source[item // SLOTS, pl.ds(from_row, block_rows), :]
            key_sorted[pl.ds(to_row, block_rows), :] = rows[:, 0:GROUP_WIDTH]
            value_sorted[pl.ds(to_row, block_rows), :] = rows[:, GROUP_WIDTH:]
            return carry

        lax.fori_loop(0, block_count, fill, 0)


def list_steps(kpb, ends, sequences, block_rows, block_count, block_of, place_of):
    def one_block(item, first_step):
        first = kpb[0, item] * block_rows
        lowest = jnp.int32(0)
        for sequence in range(sequences):
            ending = ends[sequence]
            lowest = jnp.where(first >= ending, ending, lowest)
        top = first + block_rows
        count = (top - lowest + CHUNK - 1) // CHUNK

        def one_step(step, carry):
            block_of[first_step + step] = item
            place_of[first_step + step] = top - (step + 1) * CHUNK
            return carry

        lax.fori_loop(0, count, one_step, 0)
        return first_step + count

    return lax.fori_loop(0, block_count, one_block, jnp.int32(0))


def fill_limits(kpb, ends, sequences, block_rows, item, start_s, place_s):
    for tile in range(GROUP_HEADS * block_rows // SUB):
        within = tile * SUB % block_rows
        places = (
            kpb[0, item] * block_rows
            + within
            + lax.broadcasted_iota(jnp.int32, (SUB, BS), 0)
        )
        starts = jnp.zeros_like(places)
        for sequence in range(sequences):
            ending = ends[sequence]
            starts = jnp.where(places >= ending, ending, starts)
        at_rows = slice(tile * SUB, (tile + 1) * SUB)
        start_s[item, at_rows, :] = starts
        place_s[item, at_rows, :] = places


def pipeline(total, scores, middle, products):
    scores(jnp.int32(0), 0)

    def pair(number, carry):
        step = 2 * number
        scores(step + 1, 1)
        middle(step, 0)
        products(step - 1, 1)
        scores(step + 2, 0)
        middle(step + 1, 1)
        products(step, 0)
        return carry

    lax.fori_loop(0, (total + 2) // 2, pair, 0)


def tile_slices(count):
    return [slice(tile * SUB, (tile + 1) * SUB) for tile in range(count)]


def attend_kernel(sources_count, block_rows, sequences, *refs):
    kpb, ends, queries = refs[:3]
    sources = refs[3 : 3 + sources_count]
    raw_out, low_out, lse_out, key_sorted, value_sorted, query_s, start_s, place_s = refs[
        3 + sources_count : 11 + sources_count
    ]
    best_s, total_s, gathered_s, score_0, score_1, weight_0, weight_1, fade_0, fade_1 = refs[
        11 + sources_count : 20 + sources_count
    ]
    block_of, place_of = refs[20 + sources_count :]
    score_s, weight_s, fade_s = (score_0, score_1), (weight_0, weight_1), (fade_0, fade_1)
    block_count = queries.shape[0] * SLOTS
    stacked = GROUP_HEADS * block_rows
    tiles = tile_slices(stacked // SUB)
    fill_sorted(kpb, sources, key_sorted, value_sorted, block_rows, block_count)
    total = list_steps(kpb, ends, sequences, block_rows, block_count, block_of, place_of)
    masks = head_masks(SCORE_SCALE)
    plain = head_masks(1.0)

    def load(group, carry):
        for slot in range(SLOTS):
            rows, lanes = packed_at(slot, block_rows)
            query_s[group * SLOTS + slot] = stack_heads(queries[group, rows, lanes], masks)
        return carry

    lax.fori_loop(0, block_count // SLOTS, load, 0)

    def prepare(item, carry):
        fill_limits(kpb, ends, sequences, block_rows, item, start_s, place_s)
        best_s[item] = jnp.full((stacked, BS), MASKED_SCORE, F32)
        total_s[item] = jnp.zeros((stacked, BS), F32)
        gathered_s[item] = jnp.zeros((stacked, GROUP_WIDTH), F32)
        return carry

    lax.fori_loop(0, block_count, prepare, 0)
    weight_1[...] = jnp.zeros_like(weight_1)
    fade_1[...] = jnp.ones_like(fade_1)

    def find(step):
        inside = jnp.clip(step, 0, total - 1)
        return block_of[inside], place_of[inside]

    def scores(step, side):
        item, low_place = find(step)
        at = pl.multiple_of(low_place + CHUNK, 32)
        score_s[side][...] = dot(query_s[item], key_sorted[pl.ds(at, CHUNK), :], 1, 1)

    def middle(step, side):
        item, low_place = find(step)
        low_place = jnp.where(step < total, low_place, -(1 << 24))
        lanes = low_place + lax.broadcasted_iota(jnp.int32, (1, BS), 1)
        for rows in tiles:
            starts, places = start_s[item, rows, :], place_s[item, rows, :]
            parts = []
            for part in range(CHUNK // BS):
                key_places = lanes + part * BS
                allowed = (key_places >= starts) & (key_places <= places)
                found = score_s[side][rows, part * BS : (part + 1) * BS]
                parts.append(jnp.where(allowed, found, MASKED_SCORE))
            best = best_s[item, rows, :]
            top = jnp.max(functools.reduce(jnp.maximum, parts), axis=1, keepdims=True)
            peak = jnp.maximum(best, top)
            fade = jnp.exp(best - peak)
            so_far = total_s[item, rows, :] * fade
            for part, found in enumerate(parts):
                weights = jnp.exp(found - peak)
                so_far = so_far + weights
                weight_s[side][rows, part * BS : (part + 1) * BS] = weights.astype(LOW)
            best_s[item, rows, :] = peak
            total_s[item, rows, :] = so_far
            fade_s[side][rows, :] = fade

    def products(step, side):
        item, low_place = find(step)
        at = pl.multiple_of(low_place + CHUNK, 32)
        fade = fade_s[side][...]
        fade = jnp.concatenate([fade, fade[:, : GROUP_WIDTH - BS]], axis=1)
        gathered_s[item] = gathered_s[item] * fade + dot(
            weight_s[side][...], value_sorted[pl.ds(at, CHUNK), :]
        )

    pipeline(total, scores, middle, products)

    def finish(group, carry):
        for slot in range(SLOTS):
            item = group * SLOTS + slot
            rows, lanes = packed_at(slot, block_rows)
            sums = jnp.sum(total_s[item], axis=1, keepdims=True)
            gathered = gathered_s[item] / sums
            result = jnp.zeros((block_rows, GROUP_WIDTH), F32)
            for head in range(GROUP_HEADS):
                result = result + (
                    plain[head] * gathered[head * block_rows : (head + 1) * block_rows]
                )
            raw_out[group, slot * block_rows : (slot + 1) * block_rows, :] = result
            low_out[group, rows, lanes] = result.astype(LOW)
            lse_out[item] = best_s[item][:, 0:1] + jnp.log(sums)
        return carry

    lax.fori_loop(0, block_count // SLOTS, finish, 0)


def attend_sizes(queries, pairs):
    groups, rows, _ = pairs[0].shape
    block_rows = rows // SLOTS
    all_rows = groups * rows * len(pairs)
    blocks = groups * SLOTS
    stacked = GROUP_HEADS * block_rows
    return groups, rows, block_rows, all_rows, blocks, stacked


def attend(kpb, ends, queries, pairs):
    groups, rows, block_rows, all_rows, blocks, stacked = attend_sizes(queries, pairs)
    steps = blocks * (all_rows // CHUNK + 1)
    return pl.pallas_call(
        functools.partial(attend_kernel, len(pairs), block_rows, ends.shape[0]),
        in_specs=[smem_spec()] * 2 + [vmem_spec()] * (1 + len(pairs)),
        out_specs=[vmem_spec()] * 3,
        out_shape=[
            jax.ShapeDtypeStruct((groups, rows, GROUP_WIDTH), F32),
            jax.ShapeDtypeStruct((groups, rows // 2, 2 * GROUP_WIDTH), LOW),
            jax.ShapeDtypeStruct((blocks, stacked, 1), F32),
        ],
        scratch_shapes=[
            pltpu.VMEM((CHUNK + all_rows, GROUP_WIDTH), LOW),
            pltpu.VMEM((CHUNK + all_rows, GROUP_WIDTH), LOW),
            pltpu.VMEM((blocks, stacked, GROUP_WIDTH), LOW),
            pltpu.VMEM((blocks, stacked, BS), jnp.int32),
            pltpu.VMEM((blocks, stacked, BS), jnp.int32),
            pltpu.VMEM((blocks, stacked, BS), F32),
            pltpu.VMEM((blocks, stacked, BS), F32),
            pltpu.VMEM((blocks, stacked, GROUP_WIDTH), F32),
            pltpu.VMEM((stacked, CHUNK), F32),
            pltpu.VMEM((stacked, CHUNK), F32),
            pltpu.VMEM((stacked, CHUNK), LOW),
            pltpu.VMEM((stacked, CHUNK), LOW),
            pltpu.VMEM((stacked, BS), F32),
            pltpu.VMEM((stacked, BS), F32),
            pltpu.SMEM((steps,), jnp.int32),
            pltpu.SMEM((steps,), jnp.int32),
        ],
        compiler_params=params(),
        cost_estimate=pl.CostEstimate(
            flops=groups * rows * HDIM,
            bytes_accessed=1_000_000,
            transcendentals=0,
        ),
        name="attend_forward",
    )(kpb, ends, queries, *pairs)


def attend_back_kernel(sources_count, block_rows, sequences, *refs):
    kpb, ends, queries = refs[:3]
    sources = refs[3 : 3 + sources_count]
    out_grad, raw, lse = refs[3 + sources_count : 6 + sources_count]
    query_out = refs[6 + sources_count]
    pair_outs = refs[7 + sources_count : 7 + 2 * sources_count]
    rest = refs[7 + 2 * sources_count :]
    key_sorted, value_sorted, key_grad, value_grad, query_s, grad_s, query_grad = rest[:7]
    start_s, place_s, shift_s, delta_s = rest[7:11]
    score_s, back_s, weight_s, change_s = rest[11:13], rest[13:15], rest[15:17], rest[17:19]
    block_of, place_of = rest[19:]
    block_count = queries.shape[0] * SLOTS
    stacked = GROUP_HEADS * block_rows
    tiles = tile_slices(stacked // SUB)
    fill_sorted(kpb, sources, key_sorted, value_sorted, block_rows, block_count)
    total = list_steps(kpb, ends, sequences, block_rows, block_count, block_of, place_of)
    key_grad[...] = jnp.zeros_like(key_grad)
    value_grad[...] = jnp.zeros_like(value_grad)
    weight_s[1][...] = jnp.zeros_like(weight_s[1])
    change_s[1][...] = jnp.zeros_like(change_s[1])
    masks = head_masks(SCORE_SCALE)
    plain = head_masks(1.0)

    def load(group, carry):
        for slot in range(SLOTS):
            item = group * SLOTS + slot
            rows, lanes = packed_at(slot, block_rows)
            query_s[item] = stack_heads(queries[group, rows, lanes], masks)
            grad = stack_heads(out_grad[group, rows, lanes], plain)
            grad_s[item] = grad
            values = raw[group, slot * block_rows : (slot + 1) * block_rows, :]
            delta = jnp.sum(
                grad.astype(F32) * jnp.concatenate([values] * GROUP_HEADS, axis=0),
                axis=1,
                keepdims=True,
            )
            delta_s[item] = jnp.broadcast_to(delta, (stacked, BS))
        return carry

    lax.fori_loop(0, block_count // SLOTS, load, 0)

    def prepare(item, carry):
        shift_s[item] = jnp.broadcast_to(lse[item], (stacked, BS))
        query_grad[item] = jnp.zeros((stacked, GROUP_WIDTH), F32)
        fill_limits(kpb, ends, sequences, block_rows, item, start_s, place_s)
        return carry

    lax.fori_loop(0, block_count, prepare, 0)

    def find(step):
        inside = jnp.clip(step, 0, total - 1)
        return block_of[inside], place_of[inside]

    def scores(step, side):
        item, low_place = find(step)
        at = pl.ds(pl.multiple_of(low_place + CHUNK, 32), CHUNK)
        score_s[side][...] = dot(query_s[item], key_sorted[at, :], 1, 1)
        back_s[side][...] = dot(grad_s[item], value_sorted[at, :], 1, 1)

    def middle(step, side):
        item, low_place = find(step)
        low_place = jnp.where(step < total, low_place, -(1 << 24))
        lanes = low_place + lax.broadcasted_iota(jnp.int32, (1, BS), 1)
        for rows in tiles:
            starts, places = start_s[item, rows, :], place_s[item, rows, :]
            shift, delta = shift_s[item, rows, :], delta_s[item, rows, :]
            for part in range(CHUNK // BS):
                at_lanes = slice(part * BS, (part + 1) * BS)
                key_places = lanes + part * BS
                allowed = (key_places >= starts) & (key_places <= places)
                found = score_s[side][rows, at_lanes] - shift
                weights = jnp.exp(jnp.where(allowed, found, MASKED_SCORE))
                weight_s[side][rows, at_lanes] = weights.astype(LOW)
                change = weights * (back_s[side][rows, at_lanes] - delta)
                change_s[side][rows, at_lanes] = change.astype(LOW)

    def products(step, side):
        item, low_place = find(step)
        at = pl.ds(pl.multiple_of(low_place + CHUNK, 32), CHUNK)
        value_grad[at, :] += dot(weight_s[side][...], grad_s[item], 0, 0)
        key_grad[at, :] += dot(change_s[side][...], query_s[item], 0, 0)
        query_grad[item] += dot(change_s[side][...], key_sorted[at, :])

    pipeline(total, scores, middle, products)

    def finish(item, carry):
        at = pl.ds(pl.multiple_of(item % SLOTS * block_rows, block_rows), block_rows)
        result = jnp.zeros((block_rows, GROUP_WIDTH), F32)
        for head in range(GROUP_HEADS):
            result = result + masks[head] * (
                query_grad[item, head * block_rows : (head + 1) * block_rows, :]
            )
        query_out[item // SLOTS, at, :] = result.astype(LOW)
        return carry

    lax.fori_loop(0, block_count, finish, 0)
    for number, target in enumerate(pair_outs):

        def drain(item, carry, number=number, target=target):
            to_row = pl.multiple_of(item % SLOTS * block_rows, block_rows)
            from_row = pl.multiple_of(CHUNK + kpb[number, item] * block_rows, 32)
            pair = jnp.concatenate(
                [
                    key_grad[pl.ds(from_row, block_rows), :],
                    value_grad[pl.ds(from_row, block_rows), :],
                ],
                axis=1,
            )
            target[item // SLOTS, pl.ds(to_row, block_rows), :] = pair.astype(target.dtype)
            return carry

        lax.fori_loop(0, block_count, drain, 0)


def attend_back(kpb, ends, queries, pairs, out_grad, raw, lse):
    groups, rows, block_rows, all_rows, blocks, stacked = attend_sizes(queries, pairs)
    steps = blocks * (all_rows // CHUNK + 1)
    limit = pltpu.VMEM((blocks, stacked, BS), jnp.int32)
    row_values = pltpu.VMEM((blocks, stacked, BS), F32)
    sorted_low = pltpu.VMEM((CHUNK + all_rows, GROUP_WIDTH), LOW)
    sorted_sum = pltpu.VMEM((CHUNK + all_rows, GROUP_WIDTH), F32)
    stacked_low = pltpu.VMEM((blocks, stacked, GROUP_WIDTH), LOW)
    square = pltpu.VMEM((stacked, CHUNK), F32)
    square_low = pltpu.VMEM((stacked, CHUNK), LOW)
    return pl.pallas_call(
        functools.partial(attend_back_kernel, len(pairs), block_rows, ends.shape[0]),
        in_specs=[smem_spec()] * 2 + [vmem_spec()] * (4 + len(pairs)),
        out_specs=[vmem_spec()] * (1 + len(pairs)),
        out_shape=[
            jax.ShapeDtypeStruct((groups, rows, GROUP_WIDTH), LOW),
            jax.ShapeDtypeStruct((groups, rows, 2 * GROUP_WIDTH), F32),
        ]
        + [jax.ShapeDtypeStruct((groups, rows, 2 * GROUP_WIDTH), LOW) for _ in pairs[1:]],
        scratch_shapes=[sorted_low] * 2
        + [sorted_sum] * 2
        + [stacked_low] * 2
        + [pltpu.VMEM((blocks, stacked, GROUP_WIDTH), F32)]
        + [limit] * 2
        + [row_values] * 2
        + [square] * 4
        + [square_low] * 4
        + [pltpu.SMEM((steps,), jnp.int32)] * 2,
        compiler_params=params(),
        cost_estimate=pl.CostEstimate(
            flops=groups * rows * HDIM,
            bytes_accessed=1_000_000,
            transcendentals=0,
        ),
        name="attend_backward",
    )(kpb, ends, queries, *pairs, out_grad, raw, lse)


def side_blocks():
    return D // BS


def bring(places, sources, held, done):
    copies = []
    for number, source in enumerate(sources):
        size = source.shape[0]
        target = held.at[pl.ds(places[number] * size, size)]
        copies.append(pltpu.make_async_copy(source, target, done.at[number]))
    for copy in copies:
        copy.start()
    for copy in copies:
        copy.wait()


def wide_tile(held, first, hidden_blocks, step):
    rows = []
    for row in range(side_blocks()):
        at = first + row * hidden_blocks + 2 * step
        rows.append(jnp.concatenate([held[at], held[at + 1]], axis=1))
    return jnp.concatenate(rows, axis=0)


def tall_tile(held, first, step):
    side = side_blocks()
    rows = []
    for half in range(2):
        at = first + (2 * step + half) * side
        rows.append(jnp.concatenate([held[at + column] for column in range(side)], axis=1))
    return jnp.concatenate(rows, axis=0)


def expert_sizes(weights):
    total = sum(array.shape[0] for array in weights[1])
    return total, total // (3 * side_blocks())


def expert_forward(rows_in, weights):
    rows = rows_in.shape[0]
    places, sources = weights
    count = len(sources)
    total_blocks, hidden_blocks = expert_sizes(weights)
    up_first = side_blocks() * hidden_blocks

    def kernel(places_ref, rows_ref, *refs):
        source_refs = refs[:count]
        result, gate_o, up_o, inner_o, total, held, done = refs[count:]
        step = pl.program_id(0)

        @pl.when(step == 0)
        def _():
            bring(places_ref, source_refs, held, done)
            total[...] = jnp.zeros_like(total)

        gate_tile = wide_tile(held, 0, hidden_blocks, step)
        up_tile = wide_tile(held, up_first, hidden_blocks, step)
        down_tile = tall_tile(held, 2 * up_first, step)

        for number in range(rows // TILE):
            first = number * TILE
            at = pl.ds(first, TILE)
            entering = rows_ref[at, :]
            gate_o[at, :] = dot(entering, gate_tile)
            up_o[at, :] = dot(entering, up_tile)
            for sub in range(TILE // SUB):
                now = pl.ds(first + sub * SUB, SUB)
                gate = gate_o[now, :]
                inner_o[now, :] = (gate * jax.nn.sigmoid(gate) * up_o[now, :]).astype(LOW)
            total[at, :] += dot(inner_o[at, :], down_tile)

        @pl.when(step == pl.num_programs(0) - 1)
        def _():
            result[...] = total[...].astype(LOW)

    fixed = pl.BlockSpec((rows, D), lambda step: (0, 0))
    hidden = pl.BlockSpec((rows, TILE), lambda step: (0, step))
    hidden_size = (rows, hidden_blocks * BS)
    return pl.pallas_call(
        kernel,
        grid=(hidden_blocks // 2,),
        in_specs=[smem_spec(), fixed] + [pl.BlockSpec(memory_space=pl.ANY)] * count,
        out_specs=[fixed] + [hidden] * 3,
        out_shape=[
            jax.ShapeDtypeStruct((rows, D), LOW),
            jax.ShapeDtypeStruct(hidden_size, F32),
            jax.ShapeDtypeStruct(hidden_size, F32),
            jax.ShapeDtypeStruct(hidden_size, LOW),
        ],
        scratch_shapes=[
            pltpu.VMEM((rows, D), F32),
            pltpu.VMEM((total_blocks, BS, BS), LOW),
            pltpu.SemaphoreType.DMA((count,)),
        ],
        compiler_params=params(),
        cost_estimate=pl.CostEstimate(
            flops=6 * rows * D * hidden_blocks * BS,
            bytes_accessed=6 * D * hidden_blocks * BS + 4 * rows * D,
            transcendentals=0,
        ),
        name="expert_forward",
    )(places, rows_in, *sources)


def expert_row_grads(grads_in, gate_in, up_in, weights):
    rows = grads_in.shape[0]
    places, sources = weights
    count = len(sources)
    total_blocks, hidden_blocks = expert_sizes(weights)
    up_first = side_blocks() * hidden_blocks

    def kernel(places_ref, grads_ref, gate_i, up_i, *refs):
        source_refs = refs[:count]
        back, gate_s, up_s, total, inner_grad_s, held, done = refs[count:]
        step = pl.program_id(0)

        @pl.when(step == 0)
        def _():
            bring(places_ref, source_refs, held, done)
            total[...] = jnp.zeros_like(total)

        gate_tile = wide_tile(held, 0, hidden_blocks, step)
        up_tile = wide_tile(held, up_first, hidden_blocks, step)
        down_tile = tall_tile(held, 2 * up_first, step)

        for number in range(rows // TILE):
            first = number * TILE
            at = pl.ds(first, TILE)
            inner_grad_s[at, :] = dot(grads_ref[at, :], down_tile, 1, 1)
            for sub in range(TILE // SUB):
                now = pl.ds(first + sub * SUB, SUB)
                gate = gate_i[now, :]
                inner_grad = inner_grad_s[now, :]
                sigmoid = jax.nn.sigmoid(gate)
                up_s[now, :] = (inner_grad * (gate * sigmoid)).astype(LOW)
                gate_s[now, :] = (
                    inner_grad * up_i[now, :] * (sigmoid * (1.0 + gate * (1.0 - sigmoid)))
                ).astype(LOW)
            total[at, :] += dot(gate_s[at, :], gate_tile, 1, 1) + dot(
                up_s[at, :], up_tile, 1, 1
            )

        @pl.when(step == pl.num_programs(0) - 1)
        def _():
            back[...] = total[...].astype(LOW)

    fixed = pl.BlockSpec((rows, D), lambda step: (0, 0))
    hidden = pl.BlockSpec((rows, TILE), lambda step: (0, step))
    hidden_shape = jax.ShapeDtypeStruct((rows, hidden_blocks * BS), LOW)
    return pl.pallas_call(
        kernel,
        grid=(hidden_blocks // 2,),
        in_specs=[smem_spec(), fixed, hidden, hidden]
        + [pl.BlockSpec(memory_space=pl.ANY)] * count,
        out_specs=[fixed] + [hidden] * 2,
        out_shape=[jax.ShapeDtypeStruct((rows, D), LOW)] + [hidden_shape] * 2,
        scratch_shapes=[
            pltpu.VMEM((rows, D), F32),
            pltpu.VMEM((rows, TILE), F32),
            pltpu.VMEM((total_blocks, BS, BS), LOW),
            pltpu.SemaphoreType.DMA((count,)),
        ],
        compiler_params=params(),
        cost_estimate=pl.CostEstimate(
            flops=6 * rows * D * hidden_blocks * BS,
            bytes_accessed=12 * D * hidden_blocks * BS + 6 * rows * D,
            transcendentals=0,
        ),
        name="expert_row_grads",
    )(places, grads_in, gate_in, up_in, *sources)


def expert_weight_grads(places, rows_in, grads_in, gate_grads, up_grads, inner, sizes):
    rows = rows_in.shape[0]
    hidden_blocks = gate_grads.shape[1] // BS
    side = side_blocks()
    total_blocks = 3 * side * hidden_blocks
    count = len(sizes)
    pieces = sum(len(group) for group in sizes)

    def kernel(places_ref, rows_ref, grads_ref, gate_s, up_s, inner_s, *refs):
        outs = refs[:count]
        turned, held, done = refs[count:]
        step = pl.program_id(0)

        @pl.when(step == 0)
        def _():
            turned[...] = rows_ref[...].T

        def wide_out(source, first):
            product = dot(turned[...], source[...]).astype(LOW)
            for row in range(side):
                for column in range(2):
                    held[first + row * hidden_blocks + 2 * step + column] = product[
                        row * BS : (row + 1) * BS, column * BS : (column + 1) * BS
                    ]

        wide_out(gate_s, 0)
        wide_out(up_s, side * hidden_blocks)
        product = dot(inner_s[...], grads_ref[...], 0, 0).astype(LOW)
        for half in range(2):
            for column in range(side):
                held[2 * side * hidden_blocks + (2 * step + half) * side + column] = product[
                    half * BS : (half + 1) * BS, column * BS : (column + 1) * BS
                ]

        @pl.when(step == pl.num_programs(0) - 1)
        def _():
            copies = []
            for target, group in zip(outs, sizes):
                first = 0
                for size in group:
                    number = len(copies)
                    source = held.at[pl.ds(places_ref[number] * size, size)]
                    into = target.at[pl.ds(first, size)]
                    copies.append(pltpu.make_async_copy(source, into, done.at[number]))
                    first += size
            for copy in copies:
                copy.start()
            for copy in copies:
                copy.wait()

    fixed = pl.BlockSpec((rows, D), lambda step: (0, 0))
    hidden = pl.BlockSpec((rows, TILE), lambda step: (0, step))
    return pl.pallas_call(
        kernel,
        grid=(hidden_blocks // 2,),
        in_specs=[smem_spec(), fixed, fixed] + [hidden] * 3,
        out_specs=[pl.BlockSpec(memory_space=pl.ANY)] * count,
        out_shape=[jax.ShapeDtypeStruct((sum(group), BS, BS), LOW) for group in sizes],
        scratch_shapes=[
            pltpu.VMEM((D, rows), LOW),
            pltpu.VMEM((total_blocks, BS, BS), LOW),
            pltpu.SemaphoreType.DMA((pieces,)),
        ],
        compiler_params=params(),
        cost_estimate=pl.CostEstimate(
            flops=6 * rows * D * hidden_blocks * BS,
            bytes_accessed=12 * D * hidden_blocks * BS + 6 * rows * D,
            transcendentals=0,
        ),
        name="expert_weight_grads",
    )(places, rows_in, grads_in, gate_grads, up_grads, inner)


def expert_half_grads(which, places, rows_in, grads_in, gate_grads, up_grads, inner, sizes):
    rows = rows_in.shape[0]
    hidden_blocks = gate_grads.shape[1] // BS
    side = side_blocks()
    middle_row = side // 2
    total_blocks = 3 * side * hidden_blocks // 2
    count = len(sizes)
    pieces = sum(len(group) for group in sizes)

    def kernel(which_ref, places_ref, rows_ref, grads_ref, gate_s, up_s, inner_s, *refs):
        outs = refs[:count]
        turned, held, done = refs[count:]
        step = pl.program_id(0)

        @pl.when(step == 0)
        def _():
            turned[...] = rows_ref[...].T

        def wide_out(source, first_row, last_row, first):
            product = dot(turned[first_row * BS : last_row * BS, :], source[...]).astype(LOW)
            for row in range(last_row - first_row):
                for column in range(2):
                    held[first + row * hidden_blocks + 2 * step + column] = product[
                        row * BS : (row + 1) * BS, column * BS : (column + 1) * BS
                    ]

        @pl.when(which_ref[0] == 0)
        def _():
            wide_out(gate_s, 0, side, 0)
            wide_out(up_s, 0, middle_row, side * hidden_blocks)

        @pl.when(which_ref[0] == 1)
        def _():
            wide_out(up_s, middle_row, side, 0)
            product = dot(inner_s[...], grads_ref[...], 0, 0).astype(LOW)
            for half in range(2):
                for column in range(side):
                    held[middle_row * hidden_blocks + (2 * step + half) * side + column] = product[
                        half * BS : (half + 1) * BS, column * BS : (column + 1) * BS
                    ]

        @pl.when(step == pl.num_programs(0) - 1)
        def _():
            copies = []
            for target, group in zip(outs, sizes):
                first = 0
                for size in group:
                    number = len(copies)
                    source = held.at[pl.ds(places_ref[number] * size, size)]
                    into = target.at[pl.ds(first, size)]
                    copies.append(pltpu.make_async_copy(source, into, done.at[number]))
                    first += size
            for copy in copies:
                copy.start()
            for copy in copies:
                copy.wait()

    fixed = pl.BlockSpec((rows, D), lambda step: (0, 0))
    hidden = pl.BlockSpec((rows, TILE), lambda step: (0, step))
    return pl.pallas_call(
        kernel,
        grid=(hidden_blocks // 2,),
        in_specs=[smem_spec(), smem_spec(), fixed, fixed] + [hidden] * 3,
        out_specs=[pl.BlockSpec(memory_space=pl.ANY)] * count,
        out_shape=[jax.ShapeDtypeStruct((sum(group), BS, BS), LOW) for group in sizes],
        scratch_shapes=[
            pltpu.VMEM((D, rows), LOW),
            pltpu.VMEM((total_blocks, BS, BS), LOW),
            pltpu.SemaphoreType.DMA((pieces,)),
        ],
        compiler_params=params(),
        cost_estimate=pl.CostEstimate(
            flops=3 * rows * D * hidden_blocks * BS,
            bytes_accessed=6 * D * hidden_blocks * BS + 6 * rows * D,
            transcendentals=0,
        ),
        name="expert_half_grads",
    )(which, places, rows_in, grads_in, gate_grads, up_grads, inner)


def split_low(values):
    high = values.astype(LOW)
    return high, (values - high.astype(F32)).astype(LOW)


def renew(gradient, weights, left, right, left_root, right_root, rate):
    short = gradient.astype(LOW)
    left_new = STAT_DECAY * left + (1.0 - STAT_DECAY) * dot(short, short, 1, 1)
    right_new = STAT_DECAY * right + (1.0 - STAT_DECAY) * dot(short, short, 0, 0)
    high, rest = split_low(right_root)
    turned = (dot(short, high) + dot(short, rest)).astype(LOW)
    high, rest = split_low(left_root)
    direction = dot(high, turned) + dot(rest, turned)
    return (gradient, left_new, right_new, weights.astype(F32) - rate * direction)


def block_width(count):
    return 4 if count % 4 == 0 else 3 if count % 3 == 0 else 1


def shampoo_half(half, gradients, stats, filled):
    parts = len(gradients)
    count = gradients[0].shape[0]
    width = block_width(count)
    steps = count // width
    spec = pl.BlockSpec((width, BS, BS), lambda step, half: (half[0] * steps + step, 0, 0))
    grad_spec = pl.BlockSpec((width, BS, BS), lambda step, half: (step, 0, 0))

    def kernel(half_ref, *refs):
        for number in range(width):
            total = refs[0][number].astype(F32)
            for ref in refs[1:parts]:
                total = total + ref[number].astype(F32)
            now = [ref[number] for ref in refs[parts : parts + 5]]
            results = renew(total, *now, RATE_EXPERT)
            for target, result in zip(refs[-4:], results):
                target[number] = result

    shape = jax.ShapeDtypeStruct(stats[0].shape, F32)
    extra = list(filled or ())
    return pl.pallas_call(
        kernel,
        grid_spec=pltpu.PrefetchScalarGridSpec(
            num_scalar_prefetch=1,
            grid=(steps,),
            in_specs=[grad_spec] * parts
            + [spec] * 5
            + [pl.BlockSpec(memory_space=pl.ANY)] * len(extra),
            out_specs=[spec] * 4,
        ),
        out_shape=[shape] * 4,
        input_output_aliases={6 + parts + number: number for number in range(len(extra))},
        compiler_params=params(),
        cost_estimate=pl.CostEstimate(
            flops=count * 24 * BS * BS * BS,
            bytes_accessed=count * BS * BS * (34 + 2 * parts),
            transcendentals=0,
        ),
        name="shampoo_half",
    )(half, *gradients, *stats, *extra)


def shampoo(rates, gradient, stats):
    count = gradient.shape[0]
    width = block_width(count)
    spec = pl.BlockSpec((width, BS, BS), lambda step: (step, 0, 0))
    shape = jax.ShapeDtypeStruct((count, BS, BS), F32)

    def kernel(rates_ref, *refs):
        step = pl.program_id(0)
        for number in range(width):
            gradient_now, *stats_now = [ref[number] for ref in refs[:6]]
            results = renew(
                gradient_now.astype(F32), *stats_now, rates_ref[step * width + number]
            )
            for target, result in zip(refs[6:], results):
                target[number] = result

    return pl.pallas_call(
        kernel,
        grid=(count // width,),
        in_specs=[smem_spec()] + [spec] * 6,
        out_specs=[spec] * 4,
        out_shape=[shape] * 4,
        compiler_params=params(),
        cost_estimate=pl.CostEstimate(
            flops=count * 24 * BS * BS * BS,
            bytes_accessed=count * BS * BS * 38,
            transcendentals=0,
        ),
        name="shampoo_blocks",
    )(rates, gradient, *stats)


def shampoo_panel(turn, places, panels, stats):
    groups = len(panels)
    panel_rows = panels[0].shape[0]
    parts = 3
    breadth = groups * GROUP_WIDTH
    count = stats[0].shape[0]
    width = block_width(count)
    spec = pl.BlockSpec((width, BS, BS), lambda step, turn, places: (step, 0, 0))
    fixed = pl.BlockSpec(panels[0].shape, lambda step, turn, places: (0, 0))
    shape = jax.ShapeDtypeStruct((count, BS, BS), F32)
    per_part = breadth // BS
    per_row = parts * per_part
    side = D // BS

    def kernel(turn_ref, places_ref, *refs):
        step = pl.program_id(0)
        panel_refs = refs[:groups]
        stat_refs = refs[groups : groups + 5]
        outs = refs[groups + 5 : groups + 9]
        ordered, matrix = refs[groups + 9 :]

        @pl.when(step == 0)
        def _():
            for number, panel in enumerate(panel_refs):
                ordered[places_ref[number]] = panel[...]
            for part in range(parts):
                matrix[:, part * breadth : (part + 1) * breadth] = jnp.concatenate(
                    [
                        ordered[group, :, part * GROUP_WIDTH : (part + 1) * GROUP_WIDTH].astype(F32)
                        for group in range(groups)
                    ],
                    axis=1,
                )

        turned = turn_ref[0] == 1
        rate = jnp.where(turned, RATE_OUTPUT, RATE_PROJECT).astype(F32)
        for number in range(width):
            block = step * width + number
            row_now = jnp.where(turned, block % side % 2, block // per_row)
            column_now = jnp.where(
                turned, block % side // 2 * per_part + block // side, block % per_row
            )
            found = matrix[
                pl.ds(pl.multiple_of(row_now * BS, BS), BS),
                pl.ds(pl.multiple_of(column_now * BS, BS), BS),
            ]
            found = jnp.where(turned, found.T, found)
            results = renew(found, *[ref[number] for ref in stat_refs], rate)
            for target, result in zip(outs, results):
                target[number] = result

    return pl.pallas_call(
        kernel,
        grid_spec=pltpu.PrefetchScalarGridSpec(
            num_scalar_prefetch=2,
            grid=(count // width,),
            in_specs=[fixed] * groups + [spec] * 5,
            out_specs=[spec] * 4,
            scratch_shapes=[
                pltpu.VMEM((groups, *panels[0].shape), LOW),
                pltpu.VMEM((panel_rows, parts * breadth), F32),
            ],
        ),
        out_shape=[shape] * 4,
        compiler_params=params(),
        cost_estimate=pl.CostEstimate(
            flops=count * 24 * BS * BS * BS,
            bytes_accessed=count * BS * BS * 38,
            transcendentals=0,
        ),
        name="shampoo_panel",
    )(turn, places, *panels, *stats)


def shampoo_small(weights, gradient, left_stat, right_stat, left_root, right_root, step_rates):
    left_new = STAT_DECAY * left_stat + (1.0 - STAT_DECAY) * jnp.einsum(
        "nij,nkj->nik", gradient, gradient, precision=PRECISE
    )
    right_new = STAT_DECAY * right_stat + (1.0 - STAT_DECAY) * jnp.einsum(
        "nji,njk->nik", gradient, gradient, precision=PRECISE
    )
    turned = jnp.einsum("nij,njk->nik", gradient, right_root, precision=PRECISE)
    direction = jnp.einsum("nij,njk->nik", left_root, turned, precision=PRECISE)
    return (left_new, right_new, weights - step_rates * direction)


def shifted(values, axis, size, distance):
    return lax.ppermute(values, axis, [(i, (i + distance) % size) for i in range(size)])


def crossed(values, axes, size, distance):
    return lax.ppermute(values, axes, [(i, i ^ distance) for i in range(size)])


def direct_sum(values, axes, size):
    terms = [values] + [crossed(values, axes, size, step) for step in range(1, size)]
    while len(terms) > 1:
        terms = [terms[at] + terms[at + 1] for at in range(0, len(terms), 2)]
    return terms[0]


def everywhere_sum(values, sizes):
    a_size, b_size, c_size, f_size = sizes
    values = direct_sum(values, "f", f_size)
    values = direct_sum(values, "c", c_size)
    return direct_sum(values, ("a", "b"), a_size * b_size)


def body(
    sizes,
    inputs,
    out_grad,
    vectors,
    block_order,
    seq_lengths,
    expert_ids,
    attn_weights,
    attn_left,
    attn_right,
    attn_left_root,
    attn_right_root,
    expert_weights,
    expert_left,
    expert_right,
    expert_left_root,
    expert_right_root,
    router_weights,
    router_left,
    router_right,
    router_left_root,
    router_right_root,
):
    a_size, b_size, c_size, f_size = sizes
    rows = inputs.shape[0]
    capacity = rows // 4
    tokens_all = rows * a_size * b_size * c_size * f_size
    per_side = D // BS
    project_blocks = 3 * per_side * per_side
    a_place = lax.axis_index("a")
    c_place = lax.axis_index("c")
    f_place = lax.axis_index("f")
    per_device = attn_weights.shape[0]
    per = expert_weights.shape[1]
    shares = b_size * c_size
    local_slices = expert_weights.shape[0]

    by_panels = f_size == 4 and c_size == 2 and a_size == 2
    ends = jnp.cumsum(seq_lengths[0]).astype(jnp.int32)
    order = block_order[0].reshape(a_size * b_size, c_size, SLOTS)
    kpb = jnp.stack(
        [
            lax.dynamic_index_in_dim(order, (c_place - step) % c_size, 1, False).reshape(-1)
            for step in range(c_size)
        ]
    )

    split_count = expert_weights.shape[0] * f_size // EXPERTS
    numbers = jnp.arange(EXPERTS, dtype=jnp.int32)
    spots = (numbers % a_size) * f_size + numbers // a_size if split_count == 1 else numbers
    route_count = EXPERTS + ZEROS
    named = expert_ids[:, :, None] == jnp.arange(route_count, dtype=jnp.int32)[None, None, :]
    route_member = named.astype(F32)
    chosen = jnp.any(named[:, :, :EXPERTS], axis=1).astype(LOW)
    row_numbers = jnp.arange(rows, dtype=jnp.int32)
    before = (row_numbers[None, :] < row_numbers[:, None]).astype(LOW)
    ranks = jnp.dot(before, chosen, preferred_element_type=F32).astype(jnp.int32)
    slots = jnp.sum(
        jnp.where(named[:, :, :EXPERTS], (spots * capacity)[None, None, :] + ranks[:, None, :], 0),
        axis=2,
    )
    slots = jnp.where(expert_ids < EXPERTS, slots, -1)
    slot_numbers = jnp.arange(EXPERTS * capacity, dtype=jnp.int32)
    picks = [
        (slot_numbers[:, None] == slots[:, which][None, :]).astype(LOW) for which in range(2)
    ]
    picks_both = picks[0] + picks[1]

    def to_owners(buffer):
        buffer = buffer.astype(LOW).reshape(EXPERTS, capacity, D)
        if split_count > 1:
            buffer = jnp.repeat(buffer, split_count, axis=0)
        arrived = lax.all_to_all(buffer, ("a", "f"), split_axis=0, concat_axis=0, tiled=True)
        return arrived.reshape(-1, D)

    def return_rows(results):
        return lax.all_to_all(
            results.reshape(EXPERTS * split_count, -1, D),
            ("a", "f"),
            split_axis=0,
            concat_axis=0,
            tiled=True,
        )

    def from_owners(back, pick_matrices):
        back = back.reshape(EXPERTS, split_count, capacity, D)
        return [
            sum(
                dot(matrix, back[:, part].reshape(-1, D), 0, 0) for part in range(split_count)
            )
            for matrix in pick_matrices
        ]

    tie = lax.optimization_barrier
    share_place = lax.axis_index(("b", "c"))

    def over_groups(values):
        return lax.all_to_all(values, ("a", "b"), split_axis=0, concat_axis=0, tiled=True)

    def over_b(values):
        return crossed(values, "b", b_size, 1)

    def over_c(values):
        return crossed(values, "c", c_size, 1)

    if by_panels:
        group_place = lax.axis_index(("a", "b"))
        share_places = jnp.stack([share_place ^ step for step in range(shares)])
        first_spots, other_spots = a_place * shares + share_places, (
            (1 - a_place) * shares + share_places
        )

        def halves(values):
            return [values[: per // 2], values[per // 2 :]]

        own = jnp.where(a_place == 0, expert_weights[0], expert_weights[1])
        own_halves = halves(own)
        sent = jnp.where(a_place == 0, expert_weights[1], expert_weights[0])
        cuts = [slice(0, per // 2), slice(per // 2, per * 3 // 4), slice(per * 3 // 4, per)]
        across = crossed(attn_weights, "f", f_size, 2)
        own_c = over_c(own)
        got = [shifted(sent[cuts[0]], "a", 2, 1), None]
        own_b = [over_b(own_halves[0]), None]

        def both(spot):
            return [2 * spot, 2 * spot + 1]

        weight_places = [first_spots[0], first_spots[1]] + both(first_spots[2])
        weight_places += both(first_spots[3]) + both(other_spots[0]) + both(other_spots[1])
        weight_places += both(other_spots[2]) + both(other_spots[3])
        weight_places = jnp.stack(weight_places).astype(jnp.int32)
        kept_places = jnp.stack([share_places[step] for step in (0, 2, 1, 3)])
        given_places = [share_places[0], 2 * share_places[1], 2 * share_places[3]]
        given_places += [2 * share_places[2] + 1, 2 * share_places[3] + 1]
        given_places += [2 * share_places[2], 2 * share_places[1] + 1]
        kept_places = kept_places.astype(jnp.int32)
        given_places = jnp.stack(given_places).astype(jnp.int32)
        group_places = jnp.stack([group_place ^ step for step in range(HEAD_GROUPS)])
        group_places = group_places.astype(jnp.int32)
        shard_places = jnp.stack([f_place ^ step for step in range(f_size)]).astype(jnp.int32)
        (across, own_c, got[0], own_b[0], kpb, ends, *tables) = tie(
            (across, own_c, got[0], own_b[0], kpb, ends)
            + (weight_places, kept_places, given_places, group_places, shard_places)
        )
        weight_places, kept_places, given_places, group_places, shard_places = tables
        shards = [
            attn_weights,
            crossed(attn_weights, "f", f_size, 1),
            across,
            crossed(across, "f", f_size, 1),
        ]
        first_low, first_factor, own_queries, own_pairs, w_project = project_kernel(
            inputs, vectors[0:1], shard_places, shards
        )
        w_project = w_project.reshape(D, 3 * D)
        own_pairs, got_next = tie((own_pairs, shifted(sent[cuts[1]], "a", 2, 1)))
        own_b[1] = over_b(own_halves[1])
        own_bc = [over_c(own_b[0]), None]
        got_c = [over_c(got[0]), None]
        mine, own_b[1], own_bc[0], got_c[0] = tie(
            (over_groups(own_pairs), own_b[1], own_bc[0], got_c[0])
        )
        other = over_c(mine)
        queries = over_groups(own_queries)
        got_last = shifted(tie((sent[cuts[2]], mine))[0], "a", 2, 1)
        queries, other, got_last = tie((queries, other, got_last))
        got[1] = jnp.concatenate([got_next, got_last], axis=0)
        pairs = [mine, other]
        first_sent, own_b1, got_0, got_1 = tie((first_low, own_b[1], *got, queries))[:4]
        first_parts = [first_low, None, crossed(first_sent, ("a", "b"), HEAD_GROUPS, 2), None]
        own_bc[1] = over_c(own_b1)
        got_c[1] = over_c(got_1)
        got_b = [over_b(got_0), None]
        w_output = shards[3]
        for step in range(f_size - 1):
            w_output = jnp.where(f_place == 3 - step, shards[step], w_output)
        w_output = to_matrix(w_output, D, D)
        raw, low, lse = attend(kpb, ends, queries, pairs)
        raw, low, lse, first_parts[2], own_bc[1], got_c[1], got_b[0] = tie(
            (raw, low, lse, first_parts[2], own_bc[1], got_c[1], got_b[0])
        )
        got_b[1] = over_b(tie((got[1], low))[0])
    else:
        attn_all = lax.all_gather(attn_weights, "f", axis=0, tiled=True)
        w_project = to_matrix(attn_all[:project_blocks], D, 3 * D)
        w_output = to_matrix(attn_all[project_blocks:], D, D)
        first_norm, first_factor = normalize_parts(inputs, vectors[0])
        first_low = first_norm.astype(LOW)
        projected = jnp.dot(first_low, w_project, preferred_element_type=F32).astype(LOW)
        by_part = projected.reshape(rows, 3, HEAD_GROUPS, GROUP_WIDTH)
        own_queries = by_part[:, 0].transpose(1, 0, 2)
        own_pairs = (
            by_part[:, 1:].transpose(2, 0, 1, 3).reshape(HEAD_GROUPS, rows, 2 * GROUP_WIDTH)
        )
        mine = over_groups(own_pairs)
        pairs = [mine] + [shifted(mine, "c", c_size, step) for step in range(1, c_size)]
        queries = over_groups(pack_rows(own_queries))
        raw, low, lse = attend(kpb, ends, queries, pairs)
        weight_places = jnp.arange(local_slices, dtype=jnp.int32)
        weight_shares = [
            lax.all_gather(expert_weights[number], ("b", "c"), axis=0, tiled=True)
            for number in range(local_slices)
        ]
        weights = (weight_places, weight_shares)
    by_heads = unpack_rows(over_groups(low))
    attended = by_heads.transpose(1, 0, 2).reshape(rows, D)
    middle = inputs + jnp.dot(attended, w_output, preferred_element_type=F32)
    second, second_factor = normalize_parts(middle, vectors[1])
    second_low = second.astype(LOW)
    if by_panels:
        second_low, got_b[1] = tie((second_low, got_b[1]))
        first_sent, *got_bc = tie((first_low, *got_b, second_low))[:3]
        first_parts[1] = crossed(first_sent, ("a", "b"), HEAD_GROUPS, 1)
        got_bc = [over_c(part) for part in got_bc]

    logits = jnp.dot(second_low, router_weights, preferred_element_type=F32)
    picked_logits = jnp.sum(jnp.where(named, logits[:, None, :], 0.0), axis=2)
    route_gates = jax.nn.softmax(picked_logits, axis=-1)
    received = to_owners(dot(picks_both, second_low))
    grad_rows = [
        (route_gates[:, which][:, None] * out_grad).astype(LOW) for which in range(2)
    ]
    if by_panels:
        grad_rows[0], first_parts[1], *got_bc = tie((grad_rows[0], first_parts[1], *got_bc))
    arrived = to_owners(dot(picks[0], grad_rows[0]) + dot(picks[1], grad_rows[1]))
    if by_panels:
        weight_shares = [own, own_c, *own_b, *own_bc, *got, *got_c, *got_b, *got_bc]
        weights = (weight_places, weight_shares)
    result, gate_kept, up_kept, inner = expert_forward(received, weights)
    result = return_rows(result)
    back_rows, gate_grads, up_grads = expert_row_grads(arrived, gate_kept, up_kept, weights)
    if by_panels:
        full, part = per, per // 2
        half = a_place.astype(jnp.int32).reshape(1)
        given, hop_c, hop_b, near_b, near_c = expert_half_grads(
            1 - half,
            given_places,
            received,
            arrived,
            gate_grads,
            up_grads,
            inner,
            [(full,), (part, part), (part, part), (part,), (part,)],
        )
        first_parts[3] = over_b(tie((first_parts[2], arrived))[0])
        back_rows, result, near_b, gate_grads, up_grads, first_parts[3] = tie(
            (back_rows, result, near_b, gate_grads, up_grads, first_parts[3])
        )
        back_rows = return_rows(back_rows)
        kept, kept_far, kept_near, kept_next = expert_half_grads(
            half,
            kept_places,
            received,
            arrived,
            gate_grads,
            up_grads,
            inner,
            [(full,)] * 4,
        )
        back_rows, kept = tie((back_rows, kept))
        hop_c, hop_b = over_c(hop_c), over_b(hop_b)
    else:
        back_rows = return_rows(back_rows)
        grad_shares = expert_weight_grads(
            jnp.arange(shares, dtype=jnp.int32),
            received,
            arrived,
            gate_grads,
            up_grads,
            inner,
            [(per,)] * shares,
        )
    expert_rows = jnp.stack(from_owners(result, picks), axis=1)
    const_member = route_member[:, :, EXPERTS + 2 :]
    copy_member = route_member[:, :, EXPERTS + 1]
    route_values = (
        expert_rows
        + copy_member[:, :, None] * second[:, None, :]
        + jnp.einsum("rkc,cd->rkd", const_member, vectors[2:], precision=PRECISE)
    )
    output = middle + jnp.sum(route_gates[:, :, None] * route_values, axis=1)

    gate_grad = jnp.sum(out_grad[:, None, :] * route_values, axis=2)
    picked_grad = route_gates * (
        gate_grad - jnp.sum(route_gates * gate_grad, axis=1, keepdims=True)
    )
    logit_grad = jnp.sum(route_member * picked_grad[:, :, None], axis=1)
    router_local = lax.dot_general(
        logit_grad, second_low.astype(F32), (((0,), (0,)), ((), ())), precision=PRECISE
    )
    second_grad = jnp.dot(logit_grad, router_weights.astype(F32).T, precision=PRECISE)
    second_grad = second_grad + jnp.sum(route_gates * copy_member, axis=1)[:, None] * out_grad
    const_grad = jnp.einsum("rkc,rk,rd->cd", const_member, route_gates, out_grad, precision=PRECISE)
    second_grad = second_grad + from_owners(back_rows, [picks_both])[0]
    middle_part, second_gain_grad = normalize_back(middle, second_factor, vectors[1], second_grad)
    middle_grad = out_grad + middle_part
    middle_low = middle_grad.astype(LOW)

    flat = (-1, BS, BS)
    expert_stats = [
        item.reshape(flat)
        for item in (
            expert_weights,
            expert_left,
            expert_right,
            expert_left_root,
            expert_right_root,
        )
    ]

    attended_grad = dot(middle_low, w_output, 1, 1).astype(LOW)
    attended_grad = attended_grad.reshape(rows, HEAD_GROUPS, GROUP_WIDTH).transpose(1, 0, 2)
    attended_grad = over_groups(pack_rows(attended_grad))
    if by_panels:
        hop_c, hop_b = tie((hop_c, hop_b, middle_low))[:2]
        given_b = over_b((near_b.astype(F32) + hop_c[part:].astype(F32)).astype(LOW))
        given_c = (near_c.astype(F32) + hop_b[part:].astype(F32)).astype(LOW)
        kept_next = over_c(tie((kept_next, given_c))[0])
        given_c = over_c(given_c)
        early = jnp.concatenate([router_local, second_gain_grad[None], const_grad], axis=0)
        early = direct_sum(early, "f", f_size)
        early = direct_sum(early, ("a", "b"), HEAD_GROUPS)
        attended_grad, given_b, given_c, kept_next, early = tie(
            (attended_grad, given_b, given_c, kept_next, early)
        )
        kept_b = over_b((kept_far.astype(F32) + kept_next.astype(F32)).astype(LOW))
        taken = jnp.concatenate(
            [
                given[:part].astype(F32) + hop_c[:part].astype(F32) + given_b.astype(F32),
                given[part:].astype(F32) + hop_b[:part].astype(F32) + given_c.astype(F32),
            ],
            axis=0,
        )
        taken = shifted(taken.astype(LOW), "a", 2, 1)
        kept_near = over_c(tie((kept_near, attended_grad))[0])
        early = direct_sum(early, "c", c_size)
    back_outs = attend_back(kpb, ends, queries, pairs, attended_grad, raw, lse)
    if by_panels:
        *back_outs, kept_near, taken, early = tie((*back_outs, kept_near, taken, early))
        middle_late = tie((middle_low, back_outs[0]))[0]
        output_panels = jnp.einsum(
            "hrj,rd->hdj", by_heads, middle_late, preferred_element_type=F32
        ).astype(LOW)
        output_panels = over_groups(output_panels)
        expert_outs = shampoo_half(1 - half, [taken], expert_stats, None)
        first_parts = tie((*first_parts, back_outs[0]))[:HEAD_GROUPS]
        first_all = jnp.zeros((HEAD_GROUPS, rows, D), LOW)
        for step, part_rows in enumerate(first_parts):
            first_all = lax.dynamic_update_index_in_dim(
                first_all, part_rows, group_place ^ step, 0
            )
        first_all = first_all.reshape(-1, D)
    query_grad, pair_grad = back_outs[:2]
    for step in range(1, c_size):
        pair_grad = pair_grad + shifted(back_outs[1 + step], "c", c_size, -step).astype(F32)
    group_grad = jnp.concatenate([query_grad, pair_grad.astype(LOW)], axis=2)
    if by_panels:
        group_grad, output_panels, first_all, early, *expert_outs = tie(
            (group_grad, output_panels, first_all, early, *expert_outs)
        )
    if by_panels:
        panels = dot(first_all, group_grad.reshape(-1, 3 * GROUP_WIDTH), 0, 0).astype(LOW)
        group_grad, panels = tie((group_grad, panels))
    project_grad = (
        over_groups(group_grad)
        .reshape(HEAD_GROUPS, rows, 3, GROUP_WIDTH)
        .transpose(1, 2, 0, 3)
        .reshape(rows, 3 * D)
    )
    first_grad = dot(project_grad, w_project, 1, 1)
    input_part, first_gain_grad = normalize_back(inputs, first_factor, vectors[0], first_grad)
    input_grad = middle_grad + input_part

    everywhere = ("a", "b", "c", "f")
    if not by_panels:
        early = jnp.concatenate([router_local, second_gain_grad[None], const_grad], axis=0)
        early = everywhere_sum(early, sizes)
    late = direct_sum(first_gain_grad[None], "f", f_size)
    late = direct_sum(late, "c", c_size)
    late = direct_sum(late, ("a", "b"), a_size * b_size)

    attn_stats = (attn_weights, attn_left, attn_right, attn_left_root, attn_right_root)
    if by_panels:
        panels = panels.reshape(3, D // 3, 3 * GROUP_WIDTH)
        output_panels = jnp.sum(output_panels.astype(F32), axis=0).astype(LOW)
        output_panels = (
            output_panels.reshape(3, D // 3, GROUP_WIDTH)
            .transpose(1, 0, 2)
            .reshape(1, D // 3, 3 * GROUP_WIDTH)
        )
        panels = jnp.concatenate([panels, output_panels], axis=0)
        own_panels = [
            lax.dynamic_index_in_dim(panels, f_place ^ step, 0, False) for step in range(f_size)
        ]
        summed = own_panels[0].astype(F32)
        for step in range(1, f_size):
            summed = summed + crossed(own_panels[step], "f", f_size, step).astype(F32)
        summed = summed.astype(LOW)
        kept = [kept, kept_near, kept_b]
        summed = (summed.astype(F32) + crossed(summed, "c", 2, 1).astype(F32)).astype(LOW)
        group_panels = [
            crossed(summed, ("a", "b"), HEAD_GROUPS, step) for step in range(1, HEAD_GROUPS)
        ]
        kept[0] = tie((kept[0], summed))[0]
        expert_outs = shampoo_half(half, kept, expert_stats, expert_outs)
        late, *joined = tie((late, *group_panels, *expert_outs))
        group_panels, expert_outs = joined[: HEAD_GROUPS - 1], joined[HEAD_GROUPS - 1 :]
        turn = (f_place == 3).astype(jnp.int32).reshape(1)
        attn_outs = shampoo_panel(
            turn, group_places, [summed, *group_panels], attn_stats
        )
    else:
        output_weight_grad = dot(attended, middle_low, 0, 0)
        project_weight_grad = dot(first_low, project_grad, 0, 0)
        attn_local = jnp.concatenate(
            [to_blocks(project_weight_grad, BS, BS), to_blocks(output_weight_grad, BS, BS)],
            axis=0,
        )
        attn_sum = lax.psum(attn_local, everywhere)
        attn_gradient = lax.dynamic_slice_in_dim(attn_sum, f_place * per_device, per_device, 0)
        block_numbers = f_place * per_device + jnp.arange(per_device, dtype=jnp.int32)
        attn_rates = jnp.where(block_numbers < project_blocks, RATE_PROJECT, RATE_OUTPUT)
        attn_outs = shampoo(attn_rates.astype(F32), attn_gradient, attn_stats)
        expert_gradient = lax.psum_scatter(
            jnp.concatenate(grad_shares, axis=0).reshape(local_slices, -1, BS, BS).astype(F32),
            ("b", "c"),
            scatter_dimension=1,
            tiled=True,
        ).reshape(flat)
        expert_outs = shampoo(
            jnp.full((expert_gradient.shape[0],), RATE_EXPERT, F32), expert_gradient, expert_stats
        )
    expert_grads, expert_left_new, expert_right_new, expert_new = [
        item.reshape(expert_weights.shape) for item in expert_outs
    ]
    attn_grads, attn_left_new, attn_right_new, attn_new = attn_outs
    router_grads = early[:route_count].T
    vector_grads = jnp.concatenate([late, early[route_count:]], axis=0)
    router_left_new, router_right_new, router_moved = shampoo_small(
        to_blocks(router_weights.astype(F32), BS, route_count),
        to_blocks(router_grads, BS, route_count),
        router_left,
        router_right,
        router_left_root,
        router_right_root,
        RATE_ROUTER,
    )
    router_new = to_matrix(router_moved, D, route_count)
    vector_new = vectors - RATE_VECTOR * float(tokens_all) ** (-0.5) * vector_grads
    return (
        output,
        input_grad,
        vector_grads,
        vector_new,
        attn_grads,
        attn_left_new,
        attn_right_new,
        attn_new,
        expert_grads,
        expert_left_new,
        expert_right_new,
        expert_new,
        router_grads,
        router_left_new,
        router_right_new,
        router_new,
    )


def solution(mesh):
    ctx_size = mesh.shape["ctx"]
    f_size = mesh.shape["fsdp"]
    context = ("a", "b", "c")
    token_rows = P(context + ("f",), None)
    group_rows = P("f", None)
    attn = P("f", None, None)
    expert = P("f", context, None, None)
    in_specs = (
        (token_rows, token_rows, P(), group_rows, group_rows, token_rows)
        + (attn,) * 5
        + (expert,) * 5
        + (P(),) * 5
    )
    out_specs = (token_rows, token_rows, P(), P()) + (attn,) * 4 + (expert,) * 4 + (P(),) * 4

    def run(*arrays):
        local_slices = arrays[11].shape[0] // f_size
        a_size = 2 if local_slices == 2 else 1
        b_size = HEAD_GROUPS // a_size
        c_size = ctx_size // HEAD_GROUPS
        sizes = (a_size, b_size, c_size, f_size)
        fine_mesh = jax.sharding.Mesh(mesh.devices.reshape(sizes), ("a", "b", "c", "f"))
        return jax.shard_map(
            functools.partial(body, sizes),
            mesh=fine_mesh,
            in_specs=in_specs,
            out_specs=out_specs,
            check_vma=False,
        )(*arrays)

    return run
```
